32 devices in a mesh: seq: 8 (over z, y), rep: 4 (over x, core).
Axes of the slice: x: 2, y: 2, z: 4, core: 2. Of those that a mesh axis runs over, the one named last changes fastest.
Arguments:
- tile_embed: bfloat16 [4, 4096, 768], P('rep', 'seq'), may hold values from -6 to 6
- doc_ids: int32 [4, 4096], P('rep', 'seq'), may hold values from 0 to 2, as said below
- norm1_gain: float32 [768], replicated, may hold values from 0.25 to 1.75
- norm1_shift: float32 [768], replicated, may hold values from -3 to 3
- in_weight: bfloat16 [768, 2304], replicated, may hold values from -0.21875 to 0.21875
- in_bias: float32 [2304], replicated, may hold values from -3 to 3
- out_weight: bfloat16 [768, 768], replicated, may hold values from -6 to 6
- out_bias: float32 [768], replicated, may hold values from -3 to 3
- norm2_gain: float32 [768], replicated, may hold values from 0.25 to 1.75
- norm2_shift: float32 [768], replicated, may hold values from -3 to 3
- up_weight: bfloat16 [768, 3072], replicated, may hold values from -0.21875 to 0.21875
- up_bias: float32 [3072], replicated, may hold values from -3 to 3
- down_weight: bfloat16 [3072, 768], replicated, may hold values from -0.109375 to 0.109375
- down_bias: float32 [768], replicated, may hold values from -3 to 3
- cotangent: bfloat16 [4, 4096, 768], P('rep', 'seq'), may hold values from -6 to 6
Outputs:
- out: bfloat16 [4, 4096, 768], P('rep', 'seq')
- grad_input: float32 [4, 4096, 768], P('rep', 'seq')
- grad_norm1_gain: float32 [768], P('seq')
- grad_norm1_shift: float32 [768], P('seq')
- grad_in_weight: float32 [768, 2304], P('seq')
- grad_in_bias: float32 [2304], P('seq')
- grad_out_weight: float32 [768, 768], P('seq')
- grad_out_bias: float32 [768], P('seq')
- grad_norm2_gain: float32 [768], P('seq')
- grad_norm2_shift: float32 [768], P('seq')
- grad_up_weight: float32 [768, 3072], P('seq')
- grad_up_bias: float32 [3072], P('seq')
- grad_down_weight: float32 [3072, 768], P('seq')
- grad_down_bias: float32 [768], P('seq')
The draws below stay inside these ranges and needn't reach their ends.
Inputs may be any that keep to these rules, and one draw needn't show every extreme that they name: `doc_ids`: in each row the ids never fall and start at 0; slide 1 begins within the first 512 tiles of the row and ends within its last 512 tiles, and slide 2 follows it to the row's end.
All inputs are finite; a program needn't handle non-finite values.
Results may differ from the reference program's by a relative error of at most 0.013.
Values may be sent and summed in bfloat16 or wider, within the bound.
No kernel may reach another device: no remote copies, remote signals or barrier semaphores. Data moves between devices by JAX's collectives and lax.ppermute only.
A program may use at most 320 MiB of HBM per device.

```python
import jax
import jax.numpy as jnp
from jax import lax

D = 768
H = 16
HD = 48
FF = 3072
SEG0 = 1024
BRANCHES = 5
TOK_DEV = 512
SEQ_LEN = 4096
N_REP = 4


def draw_doc_ids(key, part):
    key = jax.random.fold_in(key, 11)
    first_key, last_key = jax.random.split(key)
    starts = jax.random.randint(first_key, (N_REP, 1), 1, TOK_DEV)
    finish = jax.random.randint(last_key, (N_REP, 1), SEQ_LEN - TOK_DEV + 1, SEQ_LEN)
    position = jnp.arange(SEQ_LEN, dtype=jnp.int32)[None, :]
    return (position >= starts).astype(jnp.int32) + (position >= finish).astype(jnp.int32)


def level_of(key, shape, cuts, low, high):
    factor_of = 1.0
    for dim, shards_of in cuts:
        heights = jax.random.uniform(jax.random.fold_in(jax.random.fold_in(key, 6), dim), (shards_of,), jnp.float32, low / len(cuts), high / len(cuts))
        factor_of = factor_of * jnp.repeat(jnp.exp(heights), shape[dim] // shards_of).reshape((-1,) + (1,) * (len(shape) - 1 - dim))
    return factor_of


def bell_draw(stream_key, dims, scale, bound, cuts=(), held_as=jnp.bfloat16):
    level = level_of(stream_key, dims, cuts, -0.22, 0.18) if cuts else 1.0
    array = jax.random.normal(stream_key, dims, jnp.float32) * scale * level
    return jnp.minimum(jnp.maximum(array, -bound), bound).astype(held_as)


def setup_inputs(seed: int = 0) -> dict:
    key_list = jax.random.split(jax.random.key(seed), 16)
    return {
        "tile_embed": bell_draw(key_list[0], (N_REP, SEQ_LEN, D), 1.0, 6.0, ((0, 4), (1, 8))),
        "doc_ids": draw_doc_ids(jax.random.fold_in(key_list[15], 71), 0),
        "norm1_gain": jnp.clip(1.0 + 0.15 * jax.random.normal(key_list[2], (D,), jnp.float32), 0.25, 1.75),
        "norm1_shift": bell_draw(key_list[3], (D,), 0.5, 3.0, (), jnp.float32),
        "in_weight": bell_draw(key_list[4], (D, 3 * D), D ** -0.5, 0.21875),
        "in_bias": bell_draw(key_list[5], (3 * D,), 0.5, 3.0, (), jnp.float32),
        "out_weight": bell_draw(key_list[6], (D, D), (max(D // SEG0, 1)) ** -0.5, 6.0),
        "out_bias": bell_draw(key_list[7], (D,), 0.5, 3.0, (), jnp.float32),
        "norm2_gain": jnp.clip(1.0 + 0.15 * jax.random.normal(key_list[8], (D,), jnp.float32), 0.25, 1.75),
        "norm2_shift": bell_draw(key_list[9], (D,), 0.5, 3.0, (), jnp.float32),
        "up_weight": bell_draw(key_list[10], (D, FF), D ** -0.5, 0.21875),
        "up_bias": bell_draw(key_list[11], (FF,), 0.5, 3.0, (), jnp.float32),
        "down_weight": bell_draw(key_list[12], (FF, D), FF ** -0.5, 0.109375),
        "down_bias": bell_draw(key_list[13], (D,), 0.5, 3.0, (), jnp.float32),
        "cotangent": bell_draw(key_list[14], (N_REP, SEQ_LEN, D), 1.0, 6.0, ((0, 4), (1, 8))),
    }


@jax.custom_vjp
def low(v):
    return lax.optimization_barrier(v.astype(jnp.bfloat16)).astype(jnp.float32)

@jax.custom_vjp
def low_back(v):
    return v

def low_keep(v):
    return (low(v), None)

def low_pass(kept, grad):
    return (grad,)

def back_keep(v):
    return (v, None)

def back_low(kept, grad):
    return (low(grad),)
low.defvjp(low_keep, low_pass)
low_back.defvjp(back_keep, back_low)
NORM_EPS = 1e-05
NEG_FILL = -1e+30

def product(left, right):
    return jnp.dot(left, right, precision=lax.Precision.HIGHEST)

def layer_norm(values, norm_gain, norm_shift):
    average = lax.optimization_barrier(jnp.mean(values, axis=-1, keepdims=True))
    centred = values - average
    spread = lax.optimization_barrier(jnp.mean(centred * centred, axis=-1, keepdims=True))
    return centred * lax.rsqrt(spread + NORM_EPS) * norm_gain + norm_shift

def pick_heads(values, dilation, head_count):
    row_count = values.shape[0]
    feat_width = values.shape[-1]
    shaped = values.reshape(row_count // dilation, dilation, head_count // dilation, dilation, feat_width)
    diagonal = jnp.diagonal(shaped, axis1=1, axis2=3)
    return jnp.transpose(diagonal, (1, 3, 0, 2)).reshape(head_count, row_count // dilation, feat_width)

def pick_docs(document, dilation, head_count):
    row_count = document.shape[0]
    shaped = document.reshape(row_count // dilation, dilation).T
    return jnp.broadcast_to(shaped[None], (head_count // dilation, dilation, row_count // dilation)).reshape(head_count, row_count // dilation)

def spread_heads(values, dilation):
    head_count, picked, feat_width = values.shape
    shaped = jnp.transpose(values.reshape(head_count // dilation, dilation, picked, feat_width), (2, 0, 1, 3))
    eye_mask = jnp.eye(dilation, dtype=values.dtype)
    full_view = shaped[:, None] * eye_mask[None, :, None, :, None]
    return full_view.reshape(picked * dilation, head_count, feat_width)

def one_block(block_items):
    query_blk, key_blk, value_blk, doc_blk = block_items
    raw_scores = low_back(product(query_blk, key_blk.T) * HD ** (-0.5))
    scores = jnp.where(doc_blk[:, None] == doc_blk[None, :], raw_scores, NEG_FILL)
    row_top = lax.optimization_barrier(jnp.max(scores, axis=1, keepdims=True))
    totals = jnp.log(lax.optimization_barrier(jnp.sum(jnp.exp(scores - row_top), axis=1, keepdims=True))) + row_top
    probs_low = low(jnp.exp(scores - totals))
    outputs = low_back(product(probs_low, value_blk))
    return (outputs, totals[:, 0])

def branch_attention(queries, key_rows, value_rows, document, dilation, span):
    seq_rows = queries.shape[0]
    seg_count = seq_rows // span
    picked = span // dilation
    blocks = []
    for source in (queries, key_rows, value_rows):
        blocks.append(pick_heads(source, dilation, H).reshape(H * seg_count, picked, HD))
    doc_blocks = pick_docs(document, dilation, H).reshape(H * seg_count, picked)
    outputs, totals = lax.map(jax.checkpoint(one_block), (blocks[0], blocks[1], blocks[2], doc_blocks))
    return (outputs.reshape(H, seg_count * picked, HD), totals.reshape(H, seg_count * picked))

def dilated_attention(queries, key_rows, value_rows, document):
    seq_rows = queries.shape[0]
    numerator = jnp.zeros((seq_rows, H, HD), jnp.float32)
    denominator = jnp.zeros((seq_rows, H, 1), jnp.float32)
    for branch in range(BRANCHES):
        dilation = 2 ** branch
        span = min(SEG0 * dilation, seq_rows)
        outputs, totals = branch_attention(queries, key_rows, value_rows, document, dilation, span)
        weights = jnp.exp(totals)[..., None]
        numerator = numerator + spread_heads(weights * outputs, dilation)
        denominator = denominator + spread_heads(weights, dilation)
    return numerator / denominator

def layer_forward(inputs, document, params):
    norm1_gain, norm1_shift, in_weight, in_bias, out_weight, out_bias, norm2_gain, norm2_shift, up_weight, up_bias, down_weight, down_bias = params
    seq_rows = inputs.shape[0]
    first_low = low(layer_norm(inputs, norm1_gain, norm1_shift))
    projected = low(low_back(product(first_low, in_weight) + in_bias))
    queries = projected[:, :D].reshape(seq_rows, H, HD)
    key_rows = projected[:, D:2 * D].reshape(seq_rows, H, HD)
    value_rows = projected[:, 2 * D:].reshape(seq_rows, H, HD)
    merged = dilated_attention(queries, key_rows, value_rows, document)
    merged_low = low(merged.reshape(seq_rows, D))
    resid1 = inputs + low_back(product(merged_low, out_weight) + out_bias)
    second_low = low(layer_norm(resid1, norm2_gain, norm2_shift))
    hidden_pre = low_back(product(second_low, up_weight) + up_bias)
    gelu_low = low(jax.nn.gelu(hidden_pre, approximate=False))
    return resid1 + low_back(product(gelu_low, down_weight) + down_bias)

def reference(tile_embed, doc_ids, norm1_gain, norm1_shift, in_weight, in_bias, out_weight, out_bias, norm2_gain, norm2_shift, up_weight, up_bias, down_weight, down_bias, cotangent):
    params = (norm1_gain.astype(jnp.float32), norm1_shift.astype(jnp.float32), in_weight.astype(jnp.float32), in_bias.astype(jnp.float32), out_weight.astype(jnp.float32), out_bias.astype(jnp.float32), norm2_gain.astype(jnp.float32), norm2_shift.astype(jnp.float32), up_weight.astype(jnp.float32), up_bias.astype(jnp.float32), down_weight.astype(jnp.float32), down_bias.astype(jnp.float32))

    def per_row(grad_totals, row_items):
        row_input, row_doc, row_cot = row_items

        def forward(inputs, weight_set):
            return layer_forward(inputs, row_doc, weight_set)
        result, pull_back = jax.vjp(forward, row_input.astype(jnp.float32), params)
        grad_row, grad_params = pull_back(row_cot.astype(jnp.float32))
        grad_totals = jax.tree.map(jnp.add, grad_totals, grad_params)
        return (grad_totals, (result.astype(jnp.bfloat16), grad_row))
    zero_grads = jax.tree.map(jnp.zeros_like, params)
    grad_totals, (outputs, grad_rows) = lax.scan(per_row, zero_grads, (tile_embed, doc_ids, cotangent))
    return (outputs, grad_rows, grad_totals[0], grad_totals[1], grad_totals[2], grad_totals[3], grad_totals[4], grad_totals[5], grad_totals[6], grad_totals[7], grad_totals[8], grad_totals[9], grad_totals[10], grad_totals[11])
```

```python
import functools
import math

import jax
import jax.numpy as jnp
import numpy as np
from jax import lax
from jax.experimental import pallas as pl
from jax.experimental.pallas import tpu as pltpu
from jax.sharding import PartitionSpec as P


D = 768
H = 16
HD = 48
FF = 3072
SEG0 = 1024
BRANCHES = 5
RES = 16
HG = H // 2
GW = HG * HD
NORM_EPS = 1e-05
BIG = 1e30
SCALE = HD**-0.5
LN2 = math.log(2.0)
Q_SCALE = SCALE / LN2

f32 = jnp.float32
bf16 = jnp.bfloat16
NN = (((1,), (0,)), ((), ()))
NT = (((1,), (1,)), ((), ()))
MIB = 2**20


def mm(left, right, dims=NN):
    return lax.dot_general(left, right, dims, preferred_element_type=f32)


def rev4(v):
    return ((v & 1) << 3) | ((v & 2) << 1) | ((v & 4) >> 1) | ((v & 8) >> 3)


def run_start(head, level, tok):
    if level == 1:
        return (head % 2) * (tok // 2)
    return ((head % 2) * 2 + (head // 2) % 2) * (tok // 4)


def kcall(body, name, ins, outs, *, grid=None, in_specs=None, out_specs=None, scratch=(), vmem=40, flops=0):
    kw = {}
    if grid is not None:
        kw = dict(grid=grid)
    if in_specs is not None:
        kw.update(in_specs=in_specs, out_specs=out_specs)
    nbytes = sum(math.prod(a.shape) * a.dtype.itemsize for a in (*ins, *outs))
    return pl.pallas_call(
        body,
        out_shape=outs,
        scratch_shapes=list(scratch),
        name=name,
        compiler_params=pltpu.CompilerParams(vmem_limit_bytes=vmem * MIB),
        cost_estimate=pl.CostEstimate(flops=int(flops), bytes_accessed=nbytes, transcendentals=0),
        **kw,
    )(*ins)


def sds(shape, dtype):
    return jax.ShapeDtypeStruct(shape, dtype)


SMEM = pl.BlockSpec(memory_space=pltpu.SMEM)
VMEM = pl.BlockSpec(memory_space=pltpu.VMEM)


def full(shape):
    return pl.BlockSpec(shape, lambda *_: (0,) * len(shape))


def features(side, doc_row, pos, head, b0, tok, extra=None):
    n = doc_row.shape[1]
    rowid = lax.broadcasted_iota(jnp.int32, (16, n), 0)
    out = jnp.zeros((16, n), f32)
    diff = rev4(pos // (tok // RES)) ^ (head & (RES - 1))
    for d in range(3):
        same = doc_row == d
        val = jnp.where(same, 0.0, 1.0) if side == "q" else jnp.where(same, -BIG, 0.0)
        out = jnp.where(rowid == d, val, out)
    row = 3
    for b in range(b0 + 1, BRANCHES):
        val = math.log2((b - b0 + 1) / (b - b0))
        high = float(np.asarray(val, dtype=jnp.bfloat16))
        chosen = (diff & (2**b - 1)) == 0
        for part in (high, val - high) if val != 1.0 else (1.0,):
            put = jnp.where(chosen, 1.0 if side == "q" else part, 0.0)
            out = jnp.where(rowid == row, put, out)
            row += 1
    assert row <= 10
    if b0 > 0:
        outside = (diff & (2**b0 - 1)) != 0
        one = jnp.where(outside, 1.0 if side == "q" else -BIG, 0.0)
        const = 1.0 if side == "q" else -BIG
        out = jnp.where(rowid == (10 if side == "q" else 11), one, out)
        out = jnp.where(rowid == (11 if side == "q" else 10), const, out)
    if extra is not None:
        for j in range(3):
            out = jnp.where(rowid == 12 + j, extra[j], out)
    return out.astype(bf16)


def split3(row):
    first = row.astype(bf16).astype(f32)
    rest = row - first
    second = rest.astype(bf16).astype(f32)
    return (first, second, rest - second)


def tail_rows(n, rows):
    rowid = lax.broadcasted_iota(jnp.int32, (16, n), 0)
    out = jnp.zeros((16, n), f32)
    for j, r in enumerate(rows):
        out = jnp.where(rowid == j, r, out)
    return out.astype(bf16)


def project_body(tok, x_ref, g_ref, b_ref, wt_ref, bias_ref, pmt_ref, first_ref, q_ref, k_ref, v_ref, doc_ref, near_ref, far_ref):
    x = x_ref[0:tok].astype(f32)
    cen = x - jnp.mean(x, axis=-1, keepdims=True)
    var = jnp.mean(cen * cen, axis=-1, keepdims=True)
    first = (cen * lax.rsqrt(var + NORM_EPS) * g_ref[...] + b_ref[...]).astype(bf16)
    pmt = pmt_ref[...]
    first_t = mm(first.T, pmt).astype(bf16)
    first_ref[...] = first_t
    docs = mm(x_ref[tok : tok + 16, 0:tok], pmt)
    doc_ref[...] = docs[0:8]
    for part, ref in enumerate((q_ref, k_ref, v_ref)):
        val = mm(wt_ref[part * GW : (part + 1) * GW], first_t) + bias_ref[part * GW : (part + 1) * GW]
        if part == 0:
            val = val * Q_SCALE
        ref[...] = val.astype(bf16)
    for out, level in ((near_ref, 1), (far_ref, 2)):
        width = tok >> level
        for part, ref in enumerate((k_ref, v_ref)):
            for h in range(HG):
                start = run_start(h, level, tok)
                out[part * GW + h * HD : part * GW + (h + 1) * HD] = ref[h * HD : (h + 1) * HD, start : start + width]
        rowid = lax.broadcasted_iota(jnp.int32, (16, width), 0)
        acc = jnp.zeros((16, width), f32)
        for j in range(2**level):
            acc = jnp.where(rowid == j, docs[0:1, j * width : (j + 1) * width], acc)
        out[2 * GW : 2 * GW + 16] = acc.astype(bf16)


def project(x_ext, gain, shift, wt, bias_col, pmt):
    tok = x_ext.shape[0] - 16
    outs = [
        sds((D, tok), bf16),
        sds((GW, tok), bf16),
        sds((GW, tok), bf16),
        sds((GW, tok), bf16),
        sds((8, tok), f32),
        sds((2 * GW + 16, tok // 2), bf16),
        sds((2 * GW + 16, tok // 4), bf16),
    ]
    return kcall(
        functools.partial(project_body, tok), "project", (x_ext, gain, shift, wt, bias_col, pmt), outs,
        flops=2 * tok * D * (tok + 3 * GW),
    )


def fill_keys(kaug, vaug, k_parts, v_parts, doc_parts, pos_parts, head, b0, tok):
    at = 0
    for k, v, doc, pos in zip(k_parts, v_parts, doc_parts, pos_parts, strict=True):
        n = k.shape[1]
        kaug[0:HD, at : at + n] = k
        kaug[HD:64, at : at + n] = features("k", doc, pos, head, b0, tok, (-1.0, -1.0, -1.0))
        vaug[0:HD, at : at + n] = v
        vaug[HD:64, at : at + n] = tail_rows(n, (1.0, 1.0, 1.0))
        at += n


def fill_queries(qaug, q_parts, doc_parts, pos_parts, head, b0, tok, lse_parts=None):
    at = 0
    for j, (q, doc, pos) in enumerate(zip(q_parts, doc_parts, pos_parts, strict=True)):
        n = q.shape[1]
        extra = None if lse_parts is None else split3(lse_parts[j])
        qaug[0:HD, at : at + n] = q
        qaug[HD:64, at : at + n] = features("q", doc, pos, head, b0, tok, extra)
        at += n


def iota_row(n):
    return lax.broadcasted_iota(jnp.int32, (1, n), 1)


def attend(qaug, kaug, vaug, nq, nk, step, put):
    keys = kaug[:, 0:nk].T
    for at in range(0, nq, step):
        scores = mm(keys, qaug[:, at : at + step])
        probs = jnp.exp2(scores).astype(bf16)
        put(at, mm(vaug[:, 0:nk], probs))


def own_forward_body(tok, y_ref, qa, qb, ka, kb, va, vb, da, db, out_ref, qaug, kaug, vaug):
    head = y_ref[0] * HG + pl.program_id(0)
    pos = iota_row(tok)
    docs = (da[0:1], db[0:1])
    fill_keys(kaug, vaug, (ka[...], kb[...]), (va[...], vb[...]), docs, (pos, pos), head, 0, tok)
    fill_queries(qaug, (qa[...], qb[...]), docs, (pos, pos), head, 0, tok)

    def put(at, val):
        out_ref[0, :, at : at + val.shape[1]] = val

    attend(qaug, kaug, vaug, 2 * tok, 2 * tok, tok, put)


def head_block(tok):
    return pl.BlockSpec((HD, tok), lambda h: (h, 0))


def own_forward(y, qs, ks, vs, docs):
    tok = qs[0].shape[1]
    return kcall(
        functools.partial(own_forward_body, tok),
        "own_forward",
        (y, *qs, *ks, *vs, *docs),
        [sds((HG, 64, 2 * tok), f32)],
        grid=(HG,),
        in_specs=[SMEM] + [head_block(tok)] * 6 + [full((8, tok))] * 2,
        out_specs=[pl.BlockSpec((1, 64, 2 * tok), lambda h: (h, 0, 0))],
        scratch=[pltpu.VMEM((64, 2 * tok), bf16)] * 3,
        flops=2 * HG * 128 * (2 * tok) ** 2,
    )[0]


def groups_of(masks):
    found = {}
    for j, m in enumerate(masks):
        found.setdefault(m.bit_length(), []).append(j)
    return [(b0, min(b0, 2), found[b0]) for b0 in sorted(found)]


def remote_parts(refs, members, local, level, tok):
    width = tok >> level
    start = run_start(local, level, tok)
    lane = iota_row(width) + start
    row = pl.multiple_of(local * HD, 16)
    ks, vs, docs, poss = [], [], [], []
    for j in members:
        for ref in refs[2 * j : 2 * j + 2]:
            ks.append(ref[pl.ds(row, HD), :])
            vs.append(ref[pl.ds(row + GW, HD), :])
            block = ref[2 * GW : 2 * GW + 16, :].astype(f32)
            picked = block[0:1]
            for r in range(1, 2**level):
                picked = jnp.where(start // width == r, block[r : r + 1], picked)
            docs.append(picked)
            poss.append(lane)
    return ks, vs, docs, poss, start, width


def far_forward_body(tok, masks, y_ref, qa, qb, da, db, part, *rest):
    nrem = 2 * len(masks)
    refs = rest[:nrem]
    ma, mb, merged, lse, qaug, kaug, vaug, acc = rest[nrem:]
    local = pl.program_id(0)
    head = y_ref[0] * HG + local
    acc[...] = part[0]
    for b0, level, members in groups_of(masks):
        ks, vs, docs, poss, start, width = remote_parts(refs, members, local, level, tok)
        nk = width * len(ks)
        fill_keys(kaug, vaug, ks, vs, docs, poss, head, b0, tok)
        window = pl.ds(pl.multiple_of(start, 128), width)
        pos = iota_row(width) + start
        fill_queries(qaug, (qa[:, window], qb[:, window]), (da[0:1, window], db[0:1, window]), (pos, pos), head, b0, tok)

        def put(at, val):
            acc[:, window] += val[:, 0:width]
            other = pl.ds(pl.multiple_of(start + tok, 128), width)
            acc[:, other] += val[:, width : 2 * width]

        attend(qaug, kaug, vaug, 2 * width, nk, 2 * width, put)
    den = acc[HD : HD + 1]
    val = acc[0:HD] / den
    merged[0] = val
    ma[...] = val[:, 0:tok].astype(bf16)
    mb[...] = val[:, tok : 2 * tok].astype(bf16)
    lse[0] = jnp.broadcast_to(jnp.log2(den), (8, 2 * tok))


def remote_sizes(masks, tok):
    nq = max([tok >> level << 1 for _, level, _ in groups_of(masks)] + [128])
    nk = max([(tok >> level) * 2 * len(members) for _, level, members in groups_of(masks)] + [128])
    return nq, nk


def remote_flops(masks, tok):
    return sum(2 * HG * 64 * (2 * (tok >> lv)) * ((tok >> lv) * 2 * len(mem)) for _, lv, mem in groups_of(masks))


def far_forward(y, qs, docs, part, masks, remote):
    tok = qs[0].shape[1]
    nq, nk = remote_sizes(masks, tok)
    per_head = pl.BlockSpec((1, 64, 2 * tok), lambda h: (h, 0, 0))
    return kcall(
        functools.partial(far_forward_body, tok, masks),
        "far_forward",
        (y, *qs, *docs, part, *remote),
        [sds((GW, tok), bf16)] * 2 + [sds((HG, HD, 2 * tok), f32), sds((HG, 8, 2 * tok), f32)],
        grid=(HG,),
        in_specs=[SMEM] + [head_block(tok)] * 2 + [full((8, tok))] * 2 + [per_head] + [full(r.shape) for r in remote],
        out_specs=[head_block(tok)] * 2
        + [pl.BlockSpec((1, HD, 2 * tok), lambda h: (h, 0, 0)), pl.BlockSpec((1, 8, 2 * tok), lambda h: (h, 0, 0))],
        scratch=[
            pltpu.VMEM((64, nq), bf16),
            pltpu.VMEM((64, nk), bf16),
            pltpu.VMEM((64, nk), bf16),
            pltpu.VMEM((64, 2 * tok), f32),
        ],
        flops=2 * remote_flops(masks, tok),
    )


def attend_back(qaug, gaug, kaug, vaug, nq, nk, step, put_q, dk, dv):
    keys = kaug[0:HD, 0:nk]
    for at in range(0, nq, step):
        sl = slice(at, at + step)
        probs = jnp.exp2(mm(qaug[:, sl].T, kaug[:, 0:nk]))
        gprobs = mm(gaug[:, sl].T, vaug[:, 0:nk])
        gs = (probs * gprobs).astype(bf16)
        new_v = mm(gaug[0:HD, sl], probs.astype(bf16))
        new_k = mm(qaug[0:HD, sl], gs)
        if at == 0:
            dv[:, 0:nk] = new_v
            dk[:, 0:nk] = new_k
        else:
            dv[:, 0:nk] += new_v
            dk[:, 0:nk] += new_k
        put_q(at, mm(keys, gs, NT) * SCALE)


def fill_grads(gaug, g_parts, m_parts):
    at = 0
    for g, m in zip(g_parts, m_parts, strict=True):
        n = g.shape[1]
        delta = jnp.sum(g.astype(f32) * m, axis=0, keepdims=True)
        gaug[0:HD, at : at + n] = g
        gaug[HD:64, at : at + n] = tail_rows(n, split3(-delta))
        at += n


def far_backward_body(tok, masks, y_ref, qa, qb, da, db, ga, gb, merged, lse, *rest):
    nrem = 2 * len(masks)
    refs = rest[:nrem]
    dq_ref = rest[nrem]
    sends = rest[nrem + 1 : nrem + 1 + len(masks)]
    qaug, gaug, kaug, vaug, dk, dv = rest[nrem + 1 + len(masks) :]
    local = pl.program_id(0)
    head = y_ref[0] * HG + local
    row = pl.multiple_of(local * HD, 16)
    dq_ref[0] = jnp.zeros((HD, 2 * tok), f32)
    for b0, level, members in groups_of(masks):
        ks, vs, docs, poss, start, width = remote_parts(refs, members, local, level, tok)
        nk = width * len(ks)
        fill_keys(kaug, vaug, ks, vs, docs, poss, head, b0, tok)
        window = pl.ds(pl.multiple_of(start, 128), width)
        other = pl.ds(pl.multiple_of(start + tok, 128), width)
        pos = iota_row(width) + start
        fill_queries(
            qaug, (qa[:, window], qb[:, window]), (da[0:1, window], db[0:1, window]), (pos, pos), head, b0, tok,
            (lse[0, 0:1, window], lse[0, 0:1, other]),
        )
        fill_grads(gaug, (ga[:, window], gb[:, window]), (merged[0, :, window], merged[0, :, other]))

        def put_q(at, val):
            dq_ref[0, :, window] += val[:, 0:width]
            dq_ref[0, :, other] += val[:, width : 2 * width]

        attend_back(qaug, gaug, kaug, vaug, 2 * width, nk, 2 * width, put_q, dk, dv)
        for n, j in enumerate(members):
            span = slice(2 * n * width, 2 * (n + 1) * width)
            sends[j][pl.ds(row, HD), :] = (dk[:, span] * LN2).astype(bf16)
            sends[j][pl.ds(row + GW, HD), :] = dv[:, span].astype(bf16)


def far_backward(y, qs, docs, gs, merged, lse, masks, remote):
    tok = qs[0].shape[1]
    nq, nk = remote_sizes(masks, tok)
    per_head = lambda r: pl.BlockSpec((1, r, 2 * tok), lambda h: (h, 0, 0))
    sends = [sds((2 * GW, 2 * (tok >> min(m.bit_length(), 2))), bf16) for m in masks]
    return kcall(
        functools.partial(far_backward_body, tok, masks),
        "far_backward",
        (y, *qs, *docs, *gs, merged, lse, *remote),
        [sds((HG, HD, 2 * tok), f32)] + sends,
        grid=(HG,),
        in_specs=[SMEM] + [head_block(tok)] * 2 + [full((8, tok))] * 2 + [head_block(tok)] * 2
        + [per_head(HD), per_head(8)] + [full(r.shape) for r in remote],
        out_specs=[per_head(HD)] + [full(s.shape) for s in sends],
        scratch=[
            pltpu.VMEM((64, nq), bf16),
            pltpu.VMEM((64, nq), bf16),
            pltpu.VMEM((64, nk), bf16),
            pltpu.VMEM((64, nk), bf16),
            pltpu.VMEM((HD, nk), f32),
            pltpu.VMEM((HD, nk), f32),
        ],
        flops=5 * remote_flops(masks, tok),
    )


def own_backward_body(tok, y_ref, qa, qb, ka, kb, va, vb, da, db, ga, gb, merged, lse, dq_in, dqa, dqb, dk, dv, qaug, gaug, kaug, vaug):
    head = y_ref[0] * HG + pl.program_id(0)
    pos = iota_row(tok)
    docs = (da[0:1], db[0:1])
    fill_keys(kaug, vaug, (ka[...], kb[...]), (va[...], vb[...]), docs, (pos, pos), head, 0, tok)
    fill_queries(
        qaug, (qa[...], qb[...]), docs, (pos, pos), head, 0, tok, (lse[0, 0:1, 0:tok], lse[0, 0:1, tok : 2 * tok])
    )
    fill_grads(gaug, (ga[...], gb[...]), (merged[0, :, 0:tok], merged[0, :, tok : 2 * tok]))

    def put_q(at, val):
        out = dqa if at == 0 else dqb
        out[...] = (val + dq_in[0, :, at : at + tok]).astype(bf16)

    attend_back(qaug, gaug, kaug, vaug, 2 * tok, 2 * tok, tok, put_q, dk.at[0], dv.at[0])


def own_backward(y, qs, ks, vs, docs, gs, merged, lse, dq):
    tok = qs[0].shape[1]
    per_head = lambda r: pl.BlockSpec((1, r, 2 * tok), lambda h: (h, 0, 0))
    return kcall(
        functools.partial(own_backward_body, tok),
        "own_backward",
        (y, *qs, *ks, *vs, *docs, *gs, merged, lse, dq),
        [sds((GW, tok), bf16)] * 2 + [sds((HG, HD, 2 * tok), f32)] * 2,
        grid=(HG,),
        in_specs=[SMEM] + [head_block(tok)] * 6 + [full((8, tok))] * 2 + [head_block(tok)] * 2
        + [per_head(HD), per_head(8), per_head(HD)],
        out_specs=[head_block(tok)] * 2 + [per_head(HD)] * 2,
        scratch=[pltpu.VMEM((64, 2 * tok), bf16)] * 4,
        flops=5 * HG * 128 * (2 * tok) ** 2,
    )


def mlp_body(tok, nblk, y_ref, x_ref, mown, moth, pmt, wout, out_bias, n2g, n2s, up, up_b, down, cot,
             gelu_ref, gelu_t_ref, gpre_ref, upb_ref, resid_ref, second_t_ref, gattn_t_ref, gmown, gmoth, gres_ref, vec_ref,
             second, xhat, rstd, acc):
    step = pl.program_id(0)
    y = y_ref[0]
    mine = pl.ds(pl.multiple_of(y * GW, 128), GW)
    theirs = pl.ds(pl.multiple_of((1 - y) * GW, 128), GW)

    @pl.when(step == 0)
    def _():
        own = mm(pmt[...], mown[...], NT).astype(bf16)
        oth = mm(pmt[...], moth[...], NT).astype(bf16)
        resid = x_ref[0:tok].astype(f32) + (mm(own, wout[mine, :]) + mm(oth, wout[theirs, :])) + out_bias[...]
        resid_ref[...] = resid
        cen = resid - jnp.mean(resid, axis=-1, keepdims=True)
        rs = lax.rsqrt(jnp.mean(cen * cen, axis=-1, keepdims=True) + NORM_EPS)
        xh = cen * rs
        xhat[...] = xh
        rstd[...] = jnp.broadcast_to(rs, rstd.shape)
        low = (xh * n2g[...] + n2s[...]).astype(bf16)
        second[...] = low
        second_t_ref[...] = low.T
        acc[...] = jnp.zeros_like(acc)

    pre = mm(second[...], up[...]) + up_b[...]
    half_erf = 0.5 * lax.erf(pre * (0.5**0.5)) + 0.5
    slope = half_erf + pre * (jnp.exp(pre * pre * -0.5) * (1.0 / math.sqrt(2.0 * math.pi)))
    gelu = (pre * half_erf).astype(bf16)
    gelu_ref[...] = gelu
    gelu_t_ref[...] = gelu.T
    gpre = (slope * mm(cot[...], down[...], NT)).astype(bf16)
    gpre_ref[...] = gpre
    upb_ref[...] = mm(jnp.ones((8, tok), bf16), gpre)
    acc[...] += mm(gpre, up[...], NT)

    @pl.when(step == nblk - 1)
    def _():
        dy = acc[...]
        xh = xhat[...]
        dyg = dy * n2g[...]
        m1 = jnp.mean(dyg, axis=-1, keepdims=True)
        m2 = jnp.mean(dyg * xh, axis=-1, keepdims=True)
        g = cot[...]
        gres = g.astype(f32) + rstd[:, 0:1] * (dyg - m1 - xh * m2)
        gres_ref[...] = gres
        gattn = gres.astype(bf16)
        gattn_t = mm(gattn.T, pmt[...]).astype(bf16)
        gattn_t_ref[...] = gattn_t
        gmown[...] = mm(wout[mine, :], gattn_t).astype(bf16)
        gmoth[...] = mm(wout[theirs, :], gattn_t).astype(bf16)
        ones = jnp.ones((8, tok), bf16)
        vec_ref[0:8] = mm(ones, g)
        vec_ref[8:16] = jnp.broadcast_to(jnp.sum(dy * xh, axis=0, keepdims=True), (8, D))
        vec_ref[16:24] = jnp.broadcast_to(jnp.sum(dy, axis=0, keepdims=True), (8, D))
        vec_ref[24:32] = mm(ones, gattn)


def mlp(y, x_ext, mown, moth, pmt, wout, out_bias, n2g, n2s, up, up_b, down, cot):
    tok = cot.shape[0]
    ff = up.shape[1]
    blk = 768
    nblk = ff // blk
    cols = pl.BlockSpec((D, blk), lambda j: (0, j))
    wide = pl.BlockSpec((tok, blk), lambda j: (0, j))
    outs = [
        sds((tok, ff), bf16), sds((ff, tok), bf16), sds((tok, ff), bf16), sds((8, ff), f32),
        sds((tok, D), f32), sds((D, tok), bf16), sds((D, tok), bf16), sds((GW, tok), bf16), sds((GW, tok), bf16),
        sds((tok, D), f32), sds((32, D), f32),
    ]
    return kcall(
        functools.partial(mlp_body, tok, nblk),
        "mlp",
        (y, x_ext, mown, moth, pmt, wout, out_bias, n2g, n2s, up, up_b, down, cot),
        outs,
        grid=(nblk,),
        in_specs=[
            SMEM, full(x_ext.shape), full(mown.shape), full(moth.shape), full(pmt.shape), full(wout.shape),
            full((1, D)), full((1, D)), full((1, D)), cols, pl.BlockSpec((1, blk), lambda j: (0, j)),
            pl.BlockSpec((blk, D), lambda j: (j, 0)), full((tok, D)),
        ],
        out_specs=[
            wide, pl.BlockSpec((blk, tok), lambda j: (j, 0)), wide, pl.BlockSpec((8, blk), lambda j: (0, j)),
        ] + [full(o.shape) for o in outs[4:]],
        scratch=[pltpu.VMEM((tok, D), bf16), pltpu.VMEM((tok, D), f32), pltpu.VMEM((tok, 128), f32), pltpu.VMEM((tok, D), f32)],
        vmem=56,
        flops=2 * tok * D * (3 * ff + 2 * D + 2 * tok),
    )


NBLK = 8
HALF = D // 2
DOWN_ROWS = FF // NBLK
UP_ROWS = D // NBLK
MLP_ROWS = DOWN_ROWS + 4 * UP_ROWS + UP_ROWS
MLP_PAD = 32


def mlp_grads_body(half_ref, y_ref, gelu_t, cot, second_t, gpre, mown, moth, gattn_t, vec, out):
    down = mm(gelu_t[...], cot[...]).astype(bf16)
    up = mm(second_t[...], gpre[...]).astype(bf16)
    first = y_ref[0] == 0
    one, two = mown[...], moth[...]
    heads = jnp.concatenate([jnp.where(first, one, two), jnp.where(first, two, one)], axis=0)
    att = mm(heads, gattn_t[...], NT).astype(bf16)
    for s in range(NBLK):
        out[s, 0:DOWN_ROWS] = down[s * DOWN_ROWS : (s + 1) * DOWN_ROWS]
        rows = slice(s * UP_ROWS, (s + 1) * UP_ROWS)
        for c in range(4):
            at = DOWN_ROWS + c * UP_ROWS
            out[s, at : at + UP_ROWS] = up[rows, c * HALF : (c + 1) * HALF]
        out[s, DOWN_ROWS + 4 * UP_ROWS : MLP_ROWS] = att[rows]
        out[s, MLP_ROWS : MLP_ROWS + MLP_PAD] = vec[0, s]


def mlp_grads(half, y, gelu_t, cot, second_t, gpre, mown, moth, gattn_t, vec):
    tok = cot.shape[0]
    spec = pltpu.PrefetchScalarGridSpec(
        num_scalar_prefetch=1,
        grid=(1,),
        in_specs=[
            SMEM,
            full(gelu_t.shape),
            pl.BlockSpec((tok, HALF), lambda j, c: (0, c[0])),
            full(second_t.shape),
            pl.BlockSpec((tok, FF // 2), lambda j, c: (0, c[0])),
            full(mown.shape),
            full(moth.shape),
            pl.BlockSpec((HALF, tok), lambda j, c: (c[0], 0)),
            pl.BlockSpec((1, NBLK, MLP_PAD, HALF), lambda j, c: (c[0], 0, 0, 0)),
        ],
        out_specs=pl.BlockSpec((NBLK, MLP_ROWS + MLP_PAD, HALF), lambda j, c: (0, 0, 0)),
    )
    return pl.pallas_call(
        mlp_grads_body,
        grid_spec=spec,
        out_shape=sds((NBLK, MLP_ROWS + MLP_PAD, HALF), bf16),
        name="mlp_grads",
        compiler_params=pltpu.CompilerParams(vmem_limit_bytes=56 * MIB),
        cost_estimate=pl.CostEstimate(flops=tok * D * (2 * FF + D), bytes_accessed=16 * MIB, transcendentals=0),
    )(half, y, gelu_t, cot, second_t, gpre, mown, moth, gattn_t, vec)


def finish_body(tok, masks, gq, dk, dv, x_ref, wt, pmt, *rest):
    nrem = len(masks)
    recv = rest[:nrem]
    gqkv, gfirst, sums, bias = rest[nrem : nrem + 4]
    total = rest[nrem + 4]
    for part, ref, scale in ((0, dk, LN2), (1, dv, 1.0)):
        for h in range(HG):
            total[h * HD : (h + 1) * HD] = ref[h] * scale
        for m, r in zip(masks, recv, strict=True):
            level = min(m.bit_length(), 2)
            for h in range(HG):
                start = run_start(h, level, tok)
                row = part * GW + h * HD
                total[h * HD : (h + 1) * HD, start : start + (tok >> level)] += r[row : row + HD].astype(f32)
        gqkv[(1 + part) * GW : (2 + part) * GW] = total[...].astype(bf16)
    gqkv[0:GW] = gq[...]
    nat = mm(pmt[...], gqkv[...], NT).astype(bf16)
    bias[...] = mm(jnp.ones((8, tok), bf16), nat)
    dy = mm(nat, wt[...])
    gfirst[...] = dy.astype(gfirst.dtype)
    x = x_ref[0:tok].astype(f32)
    cen = x - jnp.mean(x, axis=-1, keepdims=True)
    xh = cen * lax.rsqrt(jnp.mean(cen * cen, axis=-1, keepdims=True) + NORM_EPS)
    sums[0:8] = jnp.broadcast_to(jnp.sum(dy * xh, axis=0, keepdims=True), (8, D))
    sums[8:16] = jnp.broadcast_to(jnp.sum(dy, axis=0, keepdims=True), (8, D))


def finish(piece, gq, dk, dv, x_ext, wt, pmt, masks, recv, dtype):
    tok = gq.shape[1]
    piece_of = lambda rows: pl.BlockSpec((HG, rows, tok), lambda j: (0, 0, piece))
    return kcall(
        functools.partial(finish_body, tok, masks),
        "finish",
        (gq, dk, dv, x_ext, wt, pmt, *recv),
        [sds((3 * GW, tok), bf16), sds((tok, D), dtype), sds((16, D), f32), sds((8, 3 * GW), f32)],
        grid=(1,),
        in_specs=[full(gq.shape), piece_of(HD), piece_of(HD), full(x_ext.shape), full(wt.shape), full(pmt.shape)]
        + [pl.BlockSpec((2 * GW, r.shape[1] // 2), lambda j: (0, piece)) for r in recv],
        out_specs=[full((3 * GW, tok)), full((tok, D)), full((16, D)), full((8, 3 * GW))],
        scratch=[pltpu.VMEM((GW, tok), f32)],
        flops=2 * tok * 3 * GW * (tok + D),
    )


IN_ROWS = D // NBLK // 2
IN_COLS = 3 * GW + 128


def in_grads_body(half_ref, fa, fb, ga, gb, vec, out, left_a, left_b):
    off = half_ref[0] * IN_ROWS
    for s in range(NBLK):
        src = pl.ds(pl.multiple_of(off + s * 2 * IN_ROWS, 16), IN_ROWS)
        dst = slice(s * IN_ROWS, (s + 1) * IN_ROWS)
        left_a[dst] = fa[src, :]
        left_b[dst] = fb[src, :]
    val = (mm(left_a[...], ga[...], NT) + mm(left_b[...], gb[...], NT)).astype(bf16)
    for s in range(NBLK):
        out[s, :, 0 : 3 * GW] = val[s * IN_ROWS : (s + 1) * IN_ROWS]
        out[s, :, 3 * GW : IN_COLS] = vec[0, s]


def in_grads(half, fa, fb, ga, gb, vec):
    tok = fa.shape[1]
    spec = pltpu.PrefetchScalarGridSpec(
        num_scalar_prefetch=1,
        grid=(1,),
        in_specs=[
            full(fa.shape), full(fb.shape), full(ga.shape), full(gb.shape),
            pl.BlockSpec((1, NBLK, IN_ROWS, 128), lambda j, c: (c[0], 0, 0, 0)),
        ],
        out_specs=pl.BlockSpec((NBLK, IN_ROWS, IN_COLS), lambda j, c: (0, 0, 0)),
        scratch_shapes=[pltpu.VMEM((NBLK * IN_ROWS, tok), bf16)] * 2,
    )
    return pl.pallas_call(
        in_grads_body,
        grid_spec=spec,
        out_shape=sds((NBLK, IN_ROWS, IN_COLS), bf16),
        name="in_grads",
        compiler_params=pltpu.CompilerParams(vmem_limit_bytes=40 * MIB),
        cost_estimate=pl.CostEstimate(flops=2 * tok * D * 3 * GW, bytes_accessed=6 * MIB, transcendentals=0),
    )(half, fa, fb, ga, gb, vec)


def input_grad_body(tok, x_ref, gain, own, got, gres, out):
    x = x_ref[0:tok].astype(f32)
    cen = x - jnp.mean(x, axis=-1, keepdims=True)
    rs = lax.rsqrt(jnp.mean(cen * cen, axis=-1, keepdims=True) + NORM_EPS)
    xh = cen * rs
    dyg = (own[...] + got[...].astype(f32)) * gain[...]
    m1 = jnp.mean(dyg, axis=-1, keepdims=True)
    m2 = jnp.mean(dyg * xh, axis=-1, keepdims=True)
    out[...] = gres[...] + rs * (dyg - m1 - xh * m2)


def swap(value, axis, offset):
    count = lax.axis_size(axis)
    return lax.ppermute(value, axis, [(i, i ^ offset) for i in range(count)])


def pick(value, index, dim):
    return lax.dynamic_index_in_dim(value, index, dim, keepdims=False)


def halve(pieces, index, dim):
    def part(i):
        return sum(pick(p, i, dim).astype(f32) for p in pieces).astype(bf16)

    return part(1 - index), part(index)


def reduce_mlp(send, keep, core, xbit, ybit, z):
    got = swap(send, "rep", 1)
    rows, cols = send.shape[1], send.shape[2]
    quarter = rows // 4
    view = lambda v: v.reshape(4, 2, 2, 2, quarter, cols)
    a, b = view(keep), view(got)
    send_a, keep_a = halve((a[:, :, 0], b[:, :, 0]), xbit, 2)
    send_b, keep_b = halve((a[:, :, 1], b[:, :, 1]), ybit, 1)
    got_a = swap(send_a, "rep", 2)
    got_b = swap(send_b, "seq", 1)
    send_a, keep_a = halve((keep_a, got_a), ybit, 1)
    send_b, keep_b = halve((keep_b, got_b), xbit, 1)
    got_a = swap(send_a, "seq", 1)
    got_b = swap(send_b, "rep", 2)
    both = jnp.stack([keep_a, keep_b], axis=1), jnp.stack([got_a, got_b], axis=1)
    parts = [sum(pick(v, z ^ m, 0).astype(f32) for v in both) for m in range(4)]
    got = [swap(parts[m].astype(bf16), "seq", 2 * m) for m in (1, 2, 3)]
    mine = (parts[0] + sum(g.astype(f32) for g in got)).astype(bf16)
    return spread(mine, core, xbit, 1)


def spread(mine, core, xbit, dim):
    other = swap(mine, "rep", 2)
    pair = jnp.stack([jnp.where(xbit == 0, mine, other), jnp.where(xbit == 0, other, mine)], axis=dim)
    far = swap(pair, "rep", 1)
    return jnp.stack([jnp.where(core == 0, pair, far), jnp.where(core == 0, far, pair)], axis=0)


def reduce_in(send, keep, core, xbit, ybit, z):
    got = swap(send, "rep", 1)
    view = lambda v: v.reshape(8, 2, IN_ROWS // 2, IN_COLS)
    send, keep = halve((view(keep), view(got)), xbit, 1)
    got = swap(send, "rep", 2)
    view = lambda v: v.reshape(4, 2, IN_ROWS // 2, IN_COLS)
    a, b = view(keep), view(got)
    parts = [pick(a, z ^ m, 0).astype(f32) + pick(b, z ^ m, 0).astype(f32) for m in range(4)]
    got = [swap(parts[m].astype(bf16), "seq", 2 * m) for m in (1, 2, 3)]
    total = (parts[0] + sum(g.astype(f32) for g in got)).astype(bf16)
    mine = pick(total, ybit, 0)
    got = swap(pick(total, 1 - ybit, 0), "seq", 1)
    width = 3 * GW
    cols = jnp.stack([jnp.where(ybit == 0, mine, got)[:, :width], jnp.where(ybit == 0, got, mine)[:, :width]], axis=0)
    vec = (mine[:, width:].astype(f32) + got[:, width:].astype(f32)).astype(bf16)
    packed = jnp.concatenate([cols[0], cols[1], vec], axis=1)
    return spread(packed, core, xbit, 0)


def body(tile_embed, doc_ids, norm1_gain, norm1_shift, in_weight, in_bias, out_weight, out_bias,
         norm2_gain, norm2_shift, up_weight, up_bias, down_weight, down_bias, cotangent):
    tok = tile_embed.shape[1]
    count = lax.axis_size("seq")
    assert SEG0 == 2 * tok and tok % 512 == 0
    nodes = count // 2
    masks = [m for m in range(1, min(nodes, 2 ** (BRANCHES - 1)))]
    index = lax.axis_index("seq")
    ybit = index % 2
    z = index // 2
    rep = lax.axis_index("rep")
    core, xbit = rep % 2, rep // 2
    y = ybit.astype(jnp.int32).reshape(1)

    p = np.arange(tok)
    place = jnp.asarray(rev4(p % RES) * (tok // RES) + p // RES, jnp.int32)
    pmt = (place[:, None] == jnp.arange(tok, dtype=jnp.int32)[None, :]).astype(bf16)

    row = lambda v: v.reshape(1, -1)
    doc_row = jnp.pad(doc_ids.astype(bf16), ((0, 15), (0, D - tok)))
    x_ext = jnp.concatenate([tile_embed[0], doc_row], axis=0)
    x_oth = swap(x_ext, "seq", 1)

    mine = lambda v: lax.dynamic_index_in_dim(v.reshape(v.shape[:-1] + (3, 2, GW)), ybit, v.ndim, keepdims=False)
    wt = mine(in_weight).reshape(D, 3 * GW).T
    bias_col = mine(in_bias).reshape(3 * GW, 1)
    args = (row(norm1_gain), row(norm1_shift), wt, bias_col, pmt)
    first_a, qa, ka, va, doc_a, *out_a = project(x_ext, *args)
    remote_a = [swap(out_a[min(m.bit_length(), 2) - 1], "seq", 2 * m) for m in masks]
    first_b, qb, kb, vb, doc_b, *out_b = project(x_oth, *args)
    remote_b = [swap(out_b[min(m.bit_length(), 2) - 1], "seq", 2 * m) for m in masks]
    remote = [r for pair in zip(remote_a, remote_b, strict=True) for r in pair]

    qs, ks, vs, docs = (qa, qb), (ka, kb), (va, vb), (doc_a, doc_b)
    part = own_forward(y, qs, ks, vs, docs)
    mown, msend, merged, lse = far_forward(y, qs, docs, part, masks, remote)
    moth = swap(msend, "seq", 1)

    cot = cotangent[0]
    (gelu, gelu_t, gpre, up_sum, resid1, second_t, gattn_t, gmown, gmsend, gres, vec) = mlp(
        y, x_ext, mown, moth, pmt, out_weight, row(out_bias), row(norm2_gain), row(norm2_shift),
        up_weight, row(up_bias), down_weight, cot,
    )
    gmoth = swap(gmsend, "seq", 1)

    vec4 = vec.reshape(4, 8, D)[:, 0].reshape(4, NBLK, UP_ROWS).transpose(1, 0, 2).reshape(NBLK, 4 * UP_ROWS)
    vecs = jnp.stack([vec4, up_sum[0].reshape(NBLK, FF // NBLK)], axis=0).astype(bf16)
    vecs = jnp.pad(vecs[:, :, None], ((0, 0), (0, 0), (0, MLP_PAD - 1), (0, 0)))
    grads = lambda half: mlp_grads(half, y, gelu_t, cot, second_t, gpre, mown, moth, gattn_t, vecs)
    whole = count == 8 and lax.axis_size("rep") == 4
    side = core.astype(jnp.int32).reshape(1) if whole else jnp.zeros((1,), jnp.int32)
    g_send, g_keep = grads(1 - side), grads(side)

    result = (resid1 + jnp.dot(gelu, down_weight, preferred_element_type=f32) + down_bias).astype(bf16)

    gs = (gmown, gmoth)
    dq, *sends = far_backward(y, qs, docs, gs, merged, lse, masks, remote)
    recv = [swap(s, "seq", 2 * m) for s, m in zip(sends, masks, strict=True)]
    dqa, dqb, dk, dv = own_backward(y, qs, ks, vs, docs, gs, merged, lse, dq)
    gqkv_b, gfirst_b, sums_b, bias_b = finish(1, dqb, dk, dv, x_oth, wt, pmt, masks, recv, bf16)
    gfirst_got = swap(gfirst_b, "seq", 1)
    gqkv_a, gfirst_a, sums_a, bias_a = finish(0, dqa, dk, dv, x_ext, wt, pmt, masks, recv, f32)
    grad_input = kcall(
        functools.partial(input_grad_body, tok), "input_grad",
        (x_ext, row(norm1_gain), gfirst_a, gfirst_got, gres), [sds((tok, D), f32)],
    )[0]

    n1 = (sums_a + sums_b).reshape(2, 8, D)[:, 0]
    in_sum = (bias_a + bias_b)[0].reshape(3, 1, GW)
    in_full = jnp.where((jnp.arange(2) == ybit)[None, :, None], in_sum, 0.0).reshape(3 * D)
    small = jnp.concatenate([n1.reshape(2, NBLK, UP_ROWS).transpose(1, 0, 2).reshape(NBLK, 2 * UP_ROWS), in_full.reshape(NBLK, 3 * D // NBLK)], axis=1)
    small = jnp.pad(small, ((0, 0), (0, 512 - small.shape[1]))).reshape(NBLK, 4, 128)
    small = jnp.stack([small, jnp.zeros_like(small)], axis=0).astype(bf16)
    small = jnp.pad(small, ((0, 0), (0, 0), (0, IN_ROWS - 4), (0, 0)))
    igrads = lambda half: in_grads(half, first_a, first_b, gqkv_a, gqkv_b, small)
    i_send, i_keep = igrads(1 - side), igrads(side)

    if whole:
        got = reduce_mlp(g_send, g_keep, core, xbit, ybit, z)
        got = got.reshape(2, MLP_ROWS + MLP_PAD, HALF).astype(f32)
        cat = lambda rows: jnp.concatenate([rows[0], rows[1]], axis=-1)
        at = DOWN_ROWS + 4 * UP_ROWS
        g_down = cat(got[:, 0:DOWN_ROWS])
        g_up = jnp.concatenate([got[c // 4, DOWN_ROWS + c % 4 * UP_ROWS : DOWN_ROWS + (c % 4 + 1) * UP_ROWS] for c in range(8)], axis=1)
        g_out = cat(got[:, at:MLP_ROWS])
        v0, v1 = got[0, MLP_ROWS], got[1, MLP_ROWS]
        got = reduce_in(i_send, i_keep, core, xbit, ybit, z).reshape(2 * IN_ROWS, 2 * 3 * GW + 128).astype(f32)
        g_in = got[:, : 6 * GW].reshape(2 * IN_ROWS, 2, 3, GW).transpose(0, 2, 1, 3).reshape(2 * IN_ROWS, 3 * D)
        sm = got[0:4, 6 * GW :].reshape(512)
    else:
        total = lambda v: lax.psum(lax.psum_scatter(v, "seq", scatter_dimension=0, tiled=True).astype(bf16), "rep").astype(f32)
        both = jnp.stack([g_keep, g_send], axis=0).astype(f32)
        cut = lambda lo, hi: both[:, :, lo:hi]
        g_down = total(cut(0, DOWN_ROWS).transpose(1, 2, 0, 3).reshape(FF, D))
        g_up = total(cut(DOWN_ROWS, DOWN_ROWS + 4 * UP_ROWS).reshape(2, NBLK, 4, UP_ROWS, HALF).transpose(1, 3, 0, 2, 4).reshape(D, FF))
        g_out = total(cut(DOWN_ROWS + 4 * UP_ROWS, MLP_ROWS).transpose(1, 2, 0, 3).reshape(D, D))
        four = [total(vec[8 * j]) for j in range(4)]
        v0 = jnp.concatenate(four)
        v1 = total(up_sum[0])
        both = jnp.stack([i_keep, i_send], axis=1)[..., : 3 * GW].astype(f32).reshape(D, 3, 1, GW)
        g_in = total(jnp.where((jnp.arange(2) == ybit)[None, None, :, None], both, 0.0).reshape(D, 3 * D))
        sm = jnp.concatenate([total(n1[0]), total(n1[1]), total(in_full)])
    w = D // count
    return (
        result[None],
        grad_input[None],
        sm[0:w],
        sm[w : 2 * w],
        g_in,
        sm[2 * w : 5 * w],
        g_out,
        v0[3 * w : 4 * w],
        v0[w : 2 * w],
        v0[2 * w : 3 * w],
        g_up,
        v1,
        g_down,
        v0[0:w],
    )


def solution(mesh):
    tokens, weights = P("rep", "seq", None), P()
    in_specs = (tokens, P("rep", "seq")) + (weights,) * 12 + (tokens,)
    vec, mat = P("seq"), P("seq", None)
    out_specs = (tokens, tokens, vec, vec, mat, vec, mat, vec, vec, vec, mat, vec, mat, vec)
    return jax.shard_map(body, mesh=mesh, in_specs=in_specs, out_specs=out_specs, check_vma=False)
```

```python
import functools
import math

import jax
import jax.numpy as jnp
import numpy as np
from jax import lax
from jax.experimental import pallas as pl
from jax.experimental.pallas import tpu as pltpu
from jax.sharding import PartitionSpec as P


D = 768
H = 16
HD = 48
FF = 3072
SEG0 = 1024
BRANCHES = 5
RES = 16
HG = H // 2
GW = HG * HD
NORM_EPS = 1e-05
BIG = 1e30
SCALE = HD**-0.5
LN2 = math.log(2.0)
Q_SCALE = SCALE / LN2

f32 = jnp.float32
bf16 = jnp.bfloat16
NN = (((1,), (0,)), ((), ()))
NT = (((1,), (1,)), ((), ()))
MIB = 2**20
VMEM_MIB = 60


def mm(left, right, dims=NN):
    return lax.dot_general(left, right, dims, preferred_element_type=f32)


def rev4(v):
    return ((v & 1) << 3) | ((v & 2) << 1) | ((v & 4) >> 1) | ((v & 8) >> 3)


def run_start(head, level, tok):
    if level == 1:
        return (head % 2) * (tok // 2)
    return ((head % 2) * 2 + (head // 2) % 2) * (tok // 4)


def kcall(body, name, ins, outs, *, grid=None, in_specs=None, out_specs=None, scratch=(), vmem=VMEM_MIB, flops=0):
    kw = {}
    if grid is not None:
        kw = dict(grid=grid)
    if in_specs is not None:
        kw.update(in_specs=in_specs, out_specs=out_specs)
    nbytes = sum(math.prod(a.shape) * a.dtype.itemsize for a in (*ins, *outs))
    return pl.pallas_call(
        body,
        out_shape=outs,
        scratch_shapes=list(scratch),
        name=name,
        compiler_params=pltpu.CompilerParams(vmem_limit_bytes=vmem * MIB),
        cost_estimate=pl.CostEstimate(flops=int(flops), bytes_accessed=nbytes, transcendentals=0),
        **kw,
    )(*ins)


def sds(shape, dtype):
    return jax.ShapeDtypeStruct(shape, dtype)


SMEM = pl.BlockSpec(memory_space=pltpu.SMEM)
VMEM = pl.BlockSpec(memory_space=pltpu.VMEM)


def full(shape):
    return pl.BlockSpec(shape, lambda *_: (0,) * len(shape))


def features(side, doc_row, pos, head, b0, tok, extra=None):
    n = doc_row.shape[1]
    rowid = lax.broadcasted_iota(jnp.int32, (16, n), 0)
    out = jnp.zeros((16, n), f32)
    diff = rev4(pos // (tok // RES)) ^ (head & (RES - 1))
    for d in range(3):
        same = doc_row == d
        val = jnp.where(same, 0.0, 1.0) if side == "q" else jnp.where(same, -BIG, 0.0)
        out = jnp.where(rowid == d, val, out)
    row = 3
    for b in range(b0 + 1, BRANCHES):
        val = math.log2((b - b0 + 1) / (b - b0))
        high = float(np.asarray(val, dtype=jnp.bfloat16))
        chosen = (diff & (2**b - 1)) == 0
        for part in (high, val - high) if val != 1.0 else (1.0,):
            put = jnp.where(chosen, 1.0 if side == "q" else part, 0.0)
            out = jnp.where(rowid == row, put, out)
            row += 1
    assert row <= 10
    if b0 > 0:
        outside = (diff & (2**b0 - 1)) != 0
        one = jnp.where(outside, 1.0 if side == "q" else -BIG, 0.0)
        const = 1.0 if side == "q" else -BIG
        out = jnp.where(rowid == (10 if side == "q" else 11), one, out)
        out = jnp.where(rowid == (11 if side == "q" else 10), const, out)
    if extra is not None:
        for j in range(3):
            out = jnp.where(rowid == 12 + j, extra[j], out)
    return out.astype(bf16)


def split3(row):
    first = row.astype(bf16).astype(f32)
    rest = row - first
    second = rest.astype(bf16).astype(f32)
    return (first, second, rest - second)


def tail_rows(n, rows):
    rowid = lax.broadcasted_iota(jnp.int32, (16, n), 0)
    out = jnp.zeros((16, n), f32)
    for j, r in enumerate(rows):
        out = jnp.where(rowid == j, r, out)
    return out.astype(bf16)


def place(tok, axis):
    shape = (tok, 1) if axis == 0 else (1, tok)
    p = lax.broadcasted_iota(jnp.int32, shape, axis)
    return rev4(p % RES) * (tok // RES) + p // RES


def one_hot(tok, transposed):
    if transposed:
        return (place(tok, 0) == lax.broadcasted_iota(jnp.int32, (1, tok), 1)).astype(bf16)
    return (place(tok, 1) == lax.broadcasted_iota(jnp.int32, (tok, 1), 0)).astype(bf16)


def normalise(x):
    cen = x - jnp.mean(x, axis=-1, keepdims=True)
    rs = lax.rsqrt(jnp.mean(cen * cen, axis=-1, keepdims=True) + NORM_EPS)
    return cen * rs, rs


def row(ref):
    return ref[...][None, :]


def project_body(tok, y_ref, x_ref, ids_ref, gain, shift, in_b, wq, wk, wv, first_ref, q_ref, k_ref, v_ref, doc_ref, near_ref, far_ref):
    xh, _ = normalise(x_ref[...].astype(f32))
    first = (xh * row(gain) + row(shift)).astype(bf16)
    first = mm(one_hot(tok, False), first).astype(bf16)
    first_ref[...] = first.T
    ids = jnp.broadcast_to(ids_ref[...].astype(f32), (16, tok)).astype(bf16)
    docs = mm(ids, one_hot(tok, True))
    doc_ref[...] = docs[0:8]
    bias = row(in_b)
    for part, (w, ref) in enumerate(((wq, q_ref), (wk, k_ref), (wv, v_ref))):
        at = part * D
        val = mm(first, w[...]) + jnp.where(y_ref[0] == 0, bias[:, at : at + GW], bias[:, at + GW : at + D])
        if part == 0:
            val = val * Q_SCALE
        ref[...] = val.astype(bf16).T
    for out, level in ((near_ref, 1), (far_ref, 2)):
        width = tok >> level
        for part, ref in enumerate((k_ref, v_ref)):
            for h in range(HG):
                start = run_start(h, level, tok)
                out[part * GW + h * HD : part * GW + (h + 1) * HD] = ref[h * HD : (h + 1) * HD, start : start + width]
        rowid = lax.broadcasted_iota(jnp.int32, (16, width), 0)
        acc = jnp.zeros((16, width), f32)
        for j in range(2**level):
            acc = jnp.where(rowid == j, docs[0:1, j * width : (j + 1) * width], acc)
        out[2 * GW : 2 * GW + 16] = acc.astype(bf16)


def weight_specs():
    return [pl.BlockSpec((D, GW), lambda j, y, part=part: (0, 2 * part + y[0])) for part in range(3)]


def pcall(body, name, scalar, ins, outs, in_specs, out_specs, *, grid=(1,), scratch=(), vmem=VMEM_MIB, flops=0):
    nbytes = sum(math.prod(a.shape) * a.dtype.itemsize for a in (*ins, *outs))
    return pl.pallas_call(
        body,
        grid_spec=pltpu.PrefetchScalarGridSpec(
            num_scalar_prefetch=1, grid=grid, in_specs=in_specs, out_specs=out_specs, scratch_shapes=list(scratch)
        ),
        out_shape=outs,
        name=name,
        compiler_params=pltpu.CompilerParams(vmem_limit_bytes=vmem * MIB),
        cost_estimate=pl.CostEstimate(flops=int(flops), bytes_accessed=nbytes, transcendentals=0),
    )(scalar, *ins)


def project(y, x, ids, gain, shift, in_b, weight):
    tok = x.shape[0]
    outs = [
        sds((D, tok), bf16),
        sds((GW, tok), bf16),
        sds((GW, tok), bf16),
        sds((GW, tok), bf16),
        sds((8, tok), f32),
        sds((2 * GW + 16, tok // 2), bf16),
        sds((2 * GW + 16, tok // 4), bf16),
    ]
    return pcall(
        functools.partial(project_body, tok), "project", y, (x, ids, gain, shift, in_b, weight, weight, weight), outs,
        [full(x.shape), full(ids.shape), full((D,)), full((D,)), full((3 * D,))] + weight_specs(), [full(o.shape) for o in outs],
        flops=2 * tok * D * (tok + 3 * GW),
    )


def fill_keys(kaug, vaug, k_parts, v_parts, doc_parts, pos_parts, head, b0, tok):
    at = 0
    for k, v, doc, pos in zip(k_parts, v_parts, doc_parts, pos_parts, strict=True):
        n = k.shape[1]
        kaug[0:HD, at : at + n] = k
        kaug[HD:64, at : at + n] = features("k", doc, pos, head, b0, tok, (-1.0, -1.0, -1.0))
        vaug[0:HD, at : at + n] = v
        vaug[HD:64, at : at + n] = tail_rows(n, (1.0, 1.0, 1.0))
        at += n


def fill_queries(qaug, q_parts, doc_parts, pos_parts, head, b0, tok, lse_parts=None):
    at = 0
    for j, (q, doc, pos) in enumerate(zip(q_parts, doc_parts, pos_parts, strict=True)):
        n = q.shape[1]
        extra = None if lse_parts is None else split3(lse_parts[j])
        qaug[0:HD, at : at + n] = q
        qaug[HD:64, at : at + n] = features("q", doc, pos, head, b0, tok, extra)
        at += n


def iota_row(n):
    return lax.broadcasted_iota(jnp.int32, (1, n), 1)


def attend(qaug, kaug, vaug, nq, nk, step, put):
    keys = kaug[:, 0:nk].T
    for at in range(0, nq, step):
        scores = mm(keys, qaug[:, at : at + step])
        probs = jnp.exp2(scores).astype(bf16)
        put(at, mm(vaug[:, 0:nk], probs))


def own_forward_body(tok, y_ref, qa, qb, ka, kb, va, vb, da, db, out_ref, qaug, kaug, vaug):
    head = y_ref[0] * HG + pl.program_id(0)
    pos = iota_row(tok)
    docs = (da[0:1], db[0:1])
    fill_keys(kaug, vaug, (ka[...], kb[...]), (va[...], vb[...]), docs, (pos, pos), head, 0, tok)
    fill_queries(qaug, (qa[...], qb[...]), docs, (pos, pos), head, 0, tok)

    def put(at, val):
        out_ref[0, :, at : at + val.shape[1]] = val

    attend(qaug, kaug, vaug, 2 * tok, 2 * tok, tok, put)


def head_block(tok):
    return pl.BlockSpec((HD, tok), lambda h: (h, 0))


def own_forward(y, qs, ks, vs, docs):
    tok = qs[0].shape[1]
    return kcall(
        functools.partial(own_forward_body, tok),
        "own_forward",
        (y, *qs, *ks, *vs, *docs),
        [sds((HG, 64, 2 * tok), f32)],
        grid=(HG,),
        in_specs=[SMEM] + [head_block(tok)] * 6 + [full((8, tok))] * 2,
        out_specs=[pl.BlockSpec((1, 64, 2 * tok), lambda h: (h, 0, 0))],
        scratch=[pltpu.VMEM((64, 2 * tok), bf16)] * 3,
        flops=2 * HG * 128 * (2 * tok) ** 2,
    )[0]


def groups_of(masks):
    found = {}
    for j, m in enumerate(masks):
        found.setdefault(m.bit_length(), []).append(j)
    return [(b0, min(b0, 2), found[b0]) for b0 in sorted(found)]


def remote_parts(refs, members, local, level, tok):
    width = tok >> level
    start = run_start(local, level, tok)
    lane = iota_row(width) + start
    row = pl.multiple_of(local * HD, 16)
    ks, vs, docs, poss = [], [], [], []
    for j in members:
        for ref in refs[2 * j : 2 * j + 2]:
            ks.append(ref[pl.ds(row, HD), :])
            vs.append(ref[pl.ds(row + GW, HD), :])
            block = ref[2 * GW : 2 * GW + 16, :].astype(f32)
            picked = block[0:1]
            for r in range(1, 2**level):
                picked = jnp.where(start // width == r, block[r : r + 1], picked)
            docs.append(picked)
            poss.append(lane)
    return ks, vs, docs, poss, start, width


def far_forward_body(tok, masks, y_ref, qa, qb, da, db, part, *rest):
    nrem = 2 * len(masks)
    refs = rest[:nrem]
    ma, mb, merged, lse, qaug, kaug, vaug, acc = rest[nrem:]
    local = pl.program_id(0)
    head = y_ref[0] * HG + local
    acc[...] = part[0]
    for b0, level, members in groups_of(masks):
        ks, vs, docs, poss, start, width = remote_parts(refs, members, local, level, tok)
        nk = width * len(ks)
        fill_keys(kaug, vaug, ks, vs, docs, poss, head, b0, tok)
        window = pl.ds(pl.multiple_of(start, 128), width)
        pos = iota_row(width) + start
        fill_queries(qaug, (qa[:, window], qb[:, window]), (da[0:1, window], db[0:1, window]), (pos, pos), head, b0, tok)

        def put(at, val):
            acc[:, window] += val[:, 0:width]
            other = pl.ds(pl.multiple_of(start + tok, 128), width)
            acc[:, other] += val[:, width : 2 * width]

        attend(qaug, kaug, vaug, 2 * width, nk, 2 * width, put)
    den = acc[HD : HD + 1]
    val = acc[0:HD] / den
    merged[0] = val
    ma[...] = val[:, 0:tok].astype(bf16)
    mb[...] = val[:, tok : 2 * tok].astype(bf16)
    lse[0] = jnp.broadcast_to(jnp.log2(den), (8, 2 * tok))


def remote_sizes(masks, tok):
    nq = max([tok >> level << 1 for _, level, _ in groups_of(masks)] + [128])
    nk = max([(tok >> level) * 2 * len(members) for _, level, members in groups_of(masks)] + [128])
    return nq, nk


def remote_flops(masks, tok):
    return sum(2 * HG * 64 * (2 * (tok >> lv)) * ((tok >> lv) * 2 * len(mem)) for _, lv, mem in groups_of(masks))


def far_forward(y, qs, docs, part, masks, remote):
    tok = qs[0].shape[1]
    nq, nk = remote_sizes(masks, tok)
    per_head = pl.BlockSpec((1, 64, 2 * tok), lambda h: (h, 0, 0))
    return kcall(
        functools.partial(far_forward_body, tok, masks),
        "far_forward",
        (y, *qs, *docs, part, *remote),
        [sds((GW, tok), bf16)] * 2 + [sds((HG, HD, 2 * tok), f32), sds((HG, 8, 2 * tok), f32)],
        grid=(HG,),
        in_specs=[SMEM] + [head_block(tok)] * 2 + [full((8, tok))] * 2 + [per_head] + [full(r.shape) for r in remote],
        out_specs=[head_block(tok)] * 2
        + [pl.BlockSpec((1, HD, 2 * tok), lambda h: (h, 0, 0)), pl.BlockSpec((1, 8, 2 * tok), lambda h: (h, 0, 0))],
        scratch=[
            pltpu.VMEM((64, nq), bf16),
            pltpu.VMEM((64, nk), bf16),
            pltpu.VMEM((64, nk), bf16),
            pltpu.VMEM((64, 2 * tok), f32),
        ],
        flops=2 * remote_flops(masks, tok),
    )


def attend_back(qaug, gaug, kaug, vaug, nq, nk, step, put_q, dk, dv):
    keys = kaug[0:HD, 0:nk]
    for at in range(0, nq, step):
        sl = slice(at, at + step)
        probs = jnp.exp2(mm(qaug[:, sl].T, kaug[:, 0:nk]))
        gprobs = mm(gaug[:, sl].T, vaug[:, 0:nk])
        gs = (probs * gprobs).astype(bf16)
        new_v = mm(gaug[0:HD, sl], probs.astype(bf16))
        new_k = mm(qaug[0:HD, sl], gs)
        if at == 0:
            dv[:, 0:nk] = new_v
            dk[:, 0:nk] = new_k
        else:
            dv[:, 0:nk] += new_v
            dk[:, 0:nk] += new_k
        put_q(at, mm(keys, gs, NT) * SCALE)


def fill_grads(gaug, g_parts, m_parts):
    at = 0
    for g, m in zip(g_parts, m_parts, strict=True):
        n = g.shape[1]
        delta = jnp.sum(g.astype(f32) * m, axis=0, keepdims=True)
        gaug[0:HD, at : at + n] = g
        gaug[HD:64, at : at + n] = tail_rows(n, split3(-delta))
        at += n


def far_backward_body(tok, masks, y_ref, qa, qb, da, db, ga, gb, merged, lse, *rest):
    nrem = 2 * len(masks)
    refs = rest[:nrem]
    dq_ref = rest[nrem]
    sends = rest[nrem + 1 : nrem + 1 + len(masks)]
    qaug, gaug, kaug, vaug, dk, dv = rest[nrem + 1 + len(masks) :]
    local = pl.program_id(0)
    head = y_ref[0] * HG + local
    row = pl.multiple_of(local * HD, 16)
    dq_ref[0] = jnp.zeros((HD, 2 * tok), f32)
    for b0, level, members in groups_of(masks):
        ks, vs, docs, poss, start, width = remote_parts(refs, members, local, level, tok)
        nk = width * len(ks)
        fill_keys(kaug, vaug, ks, vs, docs, poss, head, b0, tok)
        window = pl.ds(pl.multiple_of(start, 128), width)
        other = pl.ds(pl.multiple_of(start + tok, 128), width)
        pos = iota_row(width) + start
        fill_queries(
            qaug, (qa[:, window], qb[:, window]), (da[0:1, window], db[0:1, window]), (pos, pos), head, b0, tok,
            (lse[0, 0:1, window], lse[0, 0:1, other]),
        )
        fill_grads(gaug, (ga[:, window], gb[:, window]), (merged[0, :, window], merged[0, :, other]))

        def put_q(at, val):
            dq_ref[0, :, window] += val[:, 0:width]
            dq_ref[0, :, other] += val[:, width : 2 * width]

        attend_back(qaug, gaug, kaug, vaug, 2 * width, nk, 2 * width, put_q, dk, dv)
        for n, j in enumerate(members):
            span = slice(2 * n * width, 2 * (n + 1) * width)
            sends[j][pl.ds(row, HD), :] = (dk[:, span] * LN2).astype(bf16)
            sends[j][pl.ds(row + GW, HD), :] = dv[:, span].astype(bf16)


def far_backward(y, qs, docs, gs, merged, lse, masks, remote):
    tok = qs[0].shape[1]
    nq, nk = remote_sizes(masks, tok)
    per_head = lambda r: pl.BlockSpec((1, r, 2 * tok), lambda h: (h, 0, 0))
    sends = [sds((2 * GW, 2 * (tok >> min(m.bit_length(), 2))), bf16) for m in masks]
    return kcall(
        functools.partial(far_backward_body, tok, masks),
        "far_backward",
        (y, *qs, *docs, *gs, merged, lse, *remote),
        [sds((HG, HD, 2 * tok), f32)] + sends,
        grid=(HG,),
        in_specs=[SMEM] + [head_block(tok)] * 2 + [full((8, tok))] * 2 + [head_block(tok)] * 2
        + [per_head(HD), per_head(8)] + [full(r.shape) for r in remote],
        out_specs=[per_head(HD)] + [full(s.shape) for s in sends],
        scratch=[
            pltpu.VMEM((64, nq), bf16),
            pltpu.VMEM((64, nq), bf16),
            pltpu.VMEM((64, nk), bf16),
            pltpu.VMEM((64, nk), bf16),
            pltpu.VMEM((HD, nk), f32),
            pltpu.VMEM((HD, nk), f32),
        ],
        flops=5 * remote_flops(masks, tok),
    )


def own_backward_body(tok, y_ref, qa, qb, ka, kb, va, vb, da, db, ga, gb, merged, lse, dq_in, dq, dk, dv, qaug, gaug, kaug, vaug):
    head = y_ref[0] * HG + pl.program_id(0)
    pos = iota_row(tok)
    docs = (da[0:1], db[0:1])
    fill_keys(kaug, vaug, (ka[...], kb[...]), (va[...], vb[...]), docs, (pos, pos), head, 0, tok)
    fill_queries(
        qaug, (qa[...], qb[...]), docs, (pos, pos), head, 0, tok, (lse[0, 0:1, 0:tok], lse[0, 0:1, tok : 2 * tok])
    )
    fill_grads(gaug, (ga[...], gb[...]), (merged[0, :, 0:tok], merged[0, :, tok : 2 * tok]))

    def put_q(at, val):
        dq[:, at : at + tok] = (val + dq_in[0, :, at : at + tok]).astype(bf16)

    attend_back(qaug, gaug, kaug, vaug, 2 * tok, 2 * tok, tok, put_q, dk.at[0], dv.at[0])


def own_backward(y, qs, ks, vs, docs, gs, merged, lse, dq):
    tok = qs[0].shape[1]
    per_head = lambda r: pl.BlockSpec((1, r, 2 * tok), lambda h: (h, 0, 0))
    return kcall(
        functools.partial(own_backward_body, tok),
        "own_backward",
        (y, *qs, *ks, *vs, *docs, *gs, merged, lse, dq),
        [sds((GW, 2 * tok), bf16)] + [sds((HG, HD, 2 * tok), f32)] * 2,
        grid=(HG,),
        in_specs=[SMEM] + [head_block(tok)] * 6 + [full((8, tok))] * 2 + [head_block(tok)] * 2
        + [per_head(HD), per_head(8), per_head(HD)],
        out_specs=[head_block(2 * tok)] + [per_head(HD)] * 2,
        scratch=[pltpu.VMEM((64, 2 * tok), bf16)] * 4,
        flops=5 * HG * 128 * (2 * tok) ** 2,
    )


def cot_body(cot, down, out):
    out[...] = mm(cot[...], down[...], NT)


def cot_down(cot, down):
    tok, ff = cot.shape[0], down.shape[0]
    blk = 768
    return kcall(
        cot_body, "cot_down", (cot, down), [sds((tok, ff), f32)], grid=(ff // blk,),
        in_specs=[full((tok, D)), pl.BlockSpec((blk, D), lambda j: (j, 0))],
        out_specs=[pl.BlockSpec((tok, blk), lambda j: (0, j))], flops=2 * tok * D * ff,
    )[0]


ERF_P = 0.3275911
ERF_A = (0.254829592, -0.284496736, 1.421413741, -1.453152027, 1.061405429)


def normal_cdf(v):
    gauss = jnp.exp2(v * v * (-0.5 / LN2))
    t = 1.0 / (1.0 + jnp.abs(v) * (ERF_P * 0.5**0.5))
    poly = 0.5 * ERF_A[4]
    for a in ERF_A[3::-1]:
        poly = poly * t + 0.5 * a
    tail = poly * t * gauss
    return jnp.where(v < 0, tail, 1.0 - tail), gauss


def mlp_body(tok, nblk, y_ref, x_ref, mown, moth, out_b, n2g, n2s, wout, up, up_b, gdown, cot,
             gelu_ref, gelu_t_ref, gpre_ref, upb_ref, resid_ref, second_t_ref, gattn_t_ref, gmown, gmoth, gres_ref, vec_ref,
             second, xhat, rstd, acc):
    step = pl.program_id(0)
    y = y_ref[0]
    mine = pl.ds(pl.multiple_of(y * GW, 128), GW)
    theirs = pl.ds(pl.multiple_of((1 - y) * GW, 128), GW)
    gain = row(n2g)

    @pl.when(step == 0)
    def _():
        pmt = one_hot(tok, True)
        own = mm(pmt, mown[...], NT).astype(bf16)
        oth = mm(pmt, moth[...], NT).astype(bf16)
        resid = x_ref[...].astype(f32) + (mm(own, wout[mine, :]) + mm(oth, wout[theirs, :])) + row(out_b)
        resid_ref[...] = resid
        xh, rs = normalise(resid)
        xhat[...] = xh
        rstd[...] = jnp.broadcast_to(rs, rstd.shape)
        low = (xh * gain + row(n2s)).astype(bf16)
        second[...] = low
        second_t_ref[...] = low.T
        acc[...] = jnp.zeros_like(acc)

    pre = mm(second[...], up[...]) + up_b[0]
    cdf, gauss = normal_cdf(pre)
    gelu = (pre * cdf).astype(bf16)
    gelu_ref[...] = gelu
    gelu_t_ref[...] = gelu.T
    slope = cdf + pre * (gauss * (1.0 / math.sqrt(2.0 * math.pi)))
    gpre = (slope * gdown[...]).astype(bf16)
    gpre_ref[...] = gpre
    upb_ref[...] = mm(jnp.ones((8, tok), bf16), gpre)
    acc[...] += mm(gpre, up[...], NT)

    @pl.when(step == nblk - 1)
    def _():
        dy = acc[...]
        xh = xhat[...]
        dyg = dy * gain
        m1 = jnp.mean(dyg, axis=-1, keepdims=True)
        m2 = jnp.mean(dyg * xh, axis=-1, keepdims=True)
        g = cot[...]
        gres = g.astype(f32) + rstd[:, 0:1] * (dyg - m1 - xh * m2)
        gres_ref[...] = gres
        gattn = gres.astype(bf16)
        gattn_t = mm(gattn.T, one_hot(tok, True)).astype(bf16)
        gattn_t_ref[...] = gattn_t
        gmoth[...] = mm(wout[theirs, :], gattn_t).astype(bf16)
        gmown[...] = mm(wout[mine, :], gattn_t).astype(bf16)
        ones = jnp.ones((8, tok), bf16)
        vec_ref[0:8] = mm(ones, g)
        vec_ref[8:16] = jnp.broadcast_to(jnp.sum(dy * xh, axis=0, keepdims=True), (8, D))
        vec_ref[16:24] = jnp.broadcast_to(jnp.sum(dy, axis=0, keepdims=True), (8, D))
        vec_ref[24:32] = mm(ones, gattn)


def mlp(y, x, mown, moth, out_b, n2g, n2s, wout, up, up_b, gdown, cot):
    tok = cot.shape[0]
    ff = up.shape[1]
    blk = 768
    nblk = ff // blk
    wide = pl.BlockSpec((tok, blk), lambda j: (0, j))
    outs = [
        sds((tok, ff), bf16), sds((ff, tok), bf16), sds((tok, ff), bf16), sds((8, ff), f32),
        sds((tok, D), f32), sds((D, tok), bf16), sds((D, tok), bf16), sds((GW, tok), bf16), sds((GW, tok), bf16),
        sds((tok, D), f32), sds((32, D), f32),
    ]
    return kcall(
        functools.partial(mlp_body, tok, nblk),
        "mlp",
        (y, x, mown, moth, out_b, n2g, n2s, wout, up, up_b.reshape(nblk, 1, blk), gdown, cot),
        outs,
        grid=(nblk,),
        in_specs=[
            SMEM, full(x.shape), full(mown.shape), full(moth.shape), full((D,)), full((D,)), full((D,)), full(wout.shape),
            pl.BlockSpec((D, blk), lambda j: (0, j)), pl.BlockSpec((1, 1, blk), lambda j: (j, 0, 0)),
            wide, full((tok, D)),
        ],
        out_specs=[
            wide, pl.BlockSpec((blk, tok), lambda j: (j, 0)), wide, pl.BlockSpec((8, blk), lambda j: (0, j)),
        ] + [full(o.shape) for o in outs[4:]],
        scratch=[pltpu.VMEM((tok, D), bf16), pltpu.VMEM((tok, D), f32), pltpu.VMEM((tok, 128), f32), pltpu.VMEM((tok, D), f32)],
        flops=2 * tok * D * (2 * ff + 2 * D + 2 * tok),
    )


NBLK = 8
HALF = D // 2
DOWN_ROWS = FF // NBLK
UP_ROWS = D // NBLK
MLP_ROWS = DOWN_ROWS + 4 * UP_ROWS + UP_ROWS
STEP_BLOCKS = 2


def mlp_grads_body(bits, gelu_t, cot, second_t, gpre, mown, moth, gattn_t, send, keep):
    up = mm(second_t[...], gpre[...]).astype(bf16)
    down = mm(gelu_t[...], cot[...]).astype(bf16)
    heads = jnp.where((pl.program_id(0) < NBLK // STEP_BLOCKS // 2) == (bits[0] == 0), mown[...], moth[...])
    att = mm(heads, gattn_t[...], NT).astype(bf16)
    keep_low = bits[3] == 0

    def put(block, rows, low, high):
        keep[block, rows] = jnp.where(keep_low, low, high)
        send[block, rows] = jnp.where(keep_low, high, low)

    for s in range(STEP_BLOCKS):
        d = down[s * DOWN_ROWS : (s + 1) * DOWN_ROWS]
        put(s, slice(0, DOWN_ROWS), d[:, :HALF], d[:, HALF:])
        rows = slice(s * UP_ROWS, (s + 1) * UP_ROWS)
        for c in range(4):
            at = DOWN_ROWS + c * UP_ROWS
            low = up[rows, c * HALF : (c + 1) * HALF]
            put(s, slice(at, at + UP_ROWS), low, up[rows, (c + 4) * HALF : (c + 5) * HALF])
        a = att[rows]
        put(s, slice(DOWN_ROWS + 4 * UP_ROWS, MLP_ROWS), a[:, :HALF], a[:, HALF:])


def mlp_grads(bits, gelu_t, cot, second_t, gpre, mown, moth, gattn_t):
    tok = cot.shape[0]
    n = NBLK // STEP_BLOCKS
    rows = MLP_ROWS
    heads = pl.BlockSpec((GW // (n // 2), tok), lambda j, c: (j % (n // 2), 0))
    outs = [sds((NBLK, rows, HALF), bf16)] * 2
    return pcall(
        mlp_grads_body, "mlp_grads", bits, (gelu_t, cot, second_t, gpre, mown, moth, gattn_t), outs,
        [
            pl.BlockSpec((FF // n, tok), lambda j, c: (j, 0)),
            full(cot.shape),
            pl.BlockSpec((D // n, tok), lambda j, c: (j, 0)),
            full(gpre.shape),
            heads,
            heads,
            full(gattn_t.shape),
        ],
        [pl.BlockSpec((STEP_BLOCKS, rows, HALF), lambda j, c: (j, 0, 0))] * 2,
        grid=(n,),
        flops=2 * tok * D * (2 * FF + D),
    )


IN_ROWS = D // NBLK // 2
IN_COLS = 3 * GW + 128
SMALL_ROWS = 16
UNIT = UP_ROWS


def finish_body(tok, masks, bits, dq, dk, dv, xa, xb, fa, fb, wq, wk, wv, vec, up_sum, *rest):
    nrem = len(masks)
    recv = rest[:nrem]
    first_a, first_b, send, keep, gqkv, total, acc, sums, bias, small = rest[nrem:]
    step = pl.program_id(0)
    for part, ref, scale in ((0, dk, LN2), (1, dv, 1.0)):
        for h in range(HG):
            total[h * HD : (h + 1) * HD] = ref[h] * scale
        for m, r in zip(masks, recv, strict=True):
            level = min(m.bit_length(), 2)
            for h in range(HG):
                start = run_start(h, level, tok)
                row = part * GW + h * HD
                total[h * HD : (h + 1) * HD, start : start + (tok >> level)] += r[row : row + HD].astype(f32)
        gqkv[(1 + part) * GW : (2 + part) * GW] = total[...].astype(bf16)
    gqkv[0:GW] = dq[...]
    nat = mm(one_hot(tok, True), gqkv[...], NT).astype(bf16)
    new_bias = mm(jnp.ones((8, tok), bf16), nat)
    dy = sum(mm(nat[:, part * GW : (part + 1) * GW], w[...], NT) for part, w in enumerate((wq, wk, wv)))
    later = step == 1
    xh, _ = normalise(jnp.where(later, xa[...], xb[...]).astype(f32))
    new_gain = jnp.sum(dy * xh, axis=0, keepdims=True)
    new_shift = jnp.sum(dy, axis=0, keepdims=True)

    @pl.when(step == 0)
    def _():
        first_b[...] = dy.astype(bf16)
        acc[...] = mm(fb[...], gqkv[...], NT)
        bias[...] = new_bias
        sums[0:8] = jnp.broadcast_to(new_gain, (8, D))
        sums[8:16] = jnp.broadcast_to(new_shift, (8, D))

    @pl.when(step == 1)
    def _():
        first_a[...] = dy
        val = (acc[...] + mm(fa[...], gqkv[...], NT)).astype(bf16)
        all_bias = bias[0:1] + new_bias[0:1]
        lines = [sums[0:1] + new_gain, sums[8:9] + new_shift]
        lines += [vec[8 * j : 8 * j + 1] for j in range(4)]
        cut = lambda line, u: line[:, u * UNIT : (u + 1) * UNIT]
        small[...] = jnp.zeros_like(small)

        def put(block, row, line):
            small[block, row : row + 1, 0:UNIT] = line

        for s in range(NBLK):
            for row, line in zip((0, 1, 5, 6, 7, 8), lines, strict=True):
                put(s, row, cut(line, s))
            for k in range(4):
                put(s, 9 + k, cut(up_sum[0:1], s * 4 + k))
        for u in range(3 * NBLK):
            part, owner, k = u // 8, u // 4 % 2, u % 4
            put(u // 3, 2 + u % 3, jnp.where(bits[0] == owner, cut(all_bias, part * 4 + k), 0.0))
        keep_low = bits[3] == 0
        zeros = jnp.zeros((IN_ROWS, 128), bf16)

        def store(block, lanes, low, high):
            keep[block, :, lanes] = jnp.where(keep_low, low, high)
            send[block, :, lanes] = jnp.where(keep_low, high, low)

        for s in range(NBLK):
            at = 2 * s * IN_ROWS
            store(s, slice(0, 3 * GW), val[at : at + IN_ROWS], val[at + IN_ROWS : at + 2 * IN_ROWS])
            store(s, slice(3 * GW, IN_COLS), jnp.concatenate([small[s].astype(bf16), zeros[SMALL_ROWS:]], axis=0), zeros)


def finish(bits, dq, dk, dv, xa, xb, fa, fb, weight, vec, up_sum, masks, recv):
    tok = xa.shape[0]
    piece = lambda j: 1 - j
    by_head = pl.BlockSpec((HG, HD, tok), lambda j, y: (0, 0, piece(j)))
    outs = [sds((tok, D), f32), sds((tok, D), bf16)] + [sds((NBLK, IN_ROWS, IN_COLS), bf16)] * 2
    return pcall(
        functools.partial(finish_body, tok, masks),
        "finish",
        bits,
        (dq, dk, dv, xa, xb, fa, fb, weight, weight, weight, vec, up_sum, *recv),
        outs,
        [pl.BlockSpec((GW, tok), lambda j, y: (0, piece(j))), by_head, by_head]
        + [full(v.shape) for v in (xa, xb, fa, fb)] + weight_specs() + [full(vec.shape), full(up_sum.shape)]
        + [pl.BlockSpec((2 * GW, r.shape[1] // 2), lambda j, y: (0, piece(j))) for r in recv],
        [full(o.shape) for o in outs],
        grid=(2,),
        scratch=[
            pltpu.VMEM((3 * GW, tok), bf16), pltpu.VMEM((GW, tok), f32), pltpu.VMEM((D, 3 * GW), f32),
            pltpu.VMEM((16, D), f32), pltpu.VMEM((8, 3 * GW), f32), pltpu.VMEM((NBLK, SMALL_ROWS, 128), f32),
        ],
        flops=4 * tok * 3 * GW * (tok + 2 * D),
    )


def input_grad_body(x_ref, gain, own, got, gres, out):
    xh, rs = normalise(x_ref[...].astype(f32))
    dyg = (own[...] + got[...].astype(f32)) * row(gain)
    m1 = jnp.mean(dyg, axis=-1, keepdims=True)
    m2 = jnp.mean(dyg * xh, axis=-1, keepdims=True)
    out[...] = gres[...] + rs * (dyg - m1 - xh * m2)


def unpack_mlp_body(bits, near, far, down, up, att):
    low = bits[3] == 0
    halves = [
        jnp.concatenate([v[p, x] for p in range(2) for x in range(2)], axis=0).astype(f32)
        for v in (jnp.where(low, near[...], far[...]), jnp.where(low, far[...], near[...]))
    ]
    for c, half in enumerate(halves):
        lanes = slice(c * HALF, (c + 1) * HALF)
        down[:, lanes] = half[0:DOWN_ROWS]
        for j in range(4):
            at = DOWN_ROWS + j * UP_ROWS
            up[:, (c * 4 + j) * HALF : (c * 4 + j + 1) * HALF] = half[at : at + UP_ROWS]
        att[:, lanes] = half[DOWN_ROWS + 4 * UP_ROWS : MLP_ROWS]


VEC_UNITS = (1, 1, 3, 1, 1, 1, 1, 4)


def unpack_in_body(bits, near, far, out, *vecs):
    low = bits[3] == 0
    lower = jnp.where(low, near[...], far[...])
    upper = jnp.where(low, far[...], near[...])
    val = jnp.concatenate([lower[0], lower[1], upper[0], upper[1]], axis=0).astype(f32)
    for part in range(3):
        for y in range(2):
            src = (y * 3 + part) * GW
            dst = (part * 2 + y) * GW
            out[:, dst : dst + GW] = val[:, src : src + GW]
    row = 0
    for ref, units in zip(vecs, VEC_UNITS, strict=True):
        line = jnp.concatenate([val[row + k : row + k + 1, 6 * GW : 6 * GW + UNIT] for k in range(units)], axis=1)
        ref[...] = line[0]
        row += units


def swap(value, axis, offset):
    count = lax.axis_size(axis)
    return lax.ppermute(value, axis, [(i, i ^ offset) for i in range(count)])


def pick(value, index, dim):
    return lax.dynamic_index_in_dim(value, index, dim, keepdims=False)


def halve(pieces, index, dim):
    def part(i):
        return sum(pick(p, i, dim).astype(f32) for p in pieces).astype(bf16)

    return part(1 - index), part(index)


def split_first_body(bits, keep, got, send_a, keep_a, send_b, keep_b):
    ybit, xbit = bits[0], bits[1]
    total = lambda *at: keep[(0, *at)] + got[(0, *at)]
    for j in range(2):
        send_a[0, j] = total(j, 0, 1 - xbit)
        keep_a[0, j] = total(j, 0, xbit)
        send_b[0, j] = total(1 - ybit, 1, j)
        keep_b[0, j] = total(ybit, 1, j)


def split_first(bits, keep, got):
    rows, cols = keep.shape[1] // 4, keep.shape[2]
    view = lambda v: v.reshape(4, 2, 2, 2, rows, cols)
    block = pl.BlockSpec((1, 2, 2, 2, rows, cols), lambda j: (j, 0, 0, 0, 0, 0))
    return kcall(
        split_first_body, "split_first", (bits, view(keep), view(got)), [sds((4, 2, rows, cols), bf16)] * 4, grid=(4,),
        in_specs=[SMEM, block, block], out_specs=[pl.BlockSpec((1, 2, rows, cols), lambda j: (j, 0, 0, 0))] * 4,
    )


def split_second_body(bits, ka, ga, kb, gb, send_a, keep_a, send_b, keep_b):
    for keep, got, send_to, keep_to, bit in ((ka, ga, send_a, keep_a, bits[0]), (kb, gb, send_b, keep_b, bits[1])):
        total = lambda j: keep[0, j] + got[0, j]
        send_to[0] = total(1 - bit)
        keep_to[0] = total(bit)


def split_second(bits, ka, ga, kb, gb):
    rows, cols = ka.shape[2:]
    block = pl.BlockSpec((1, 2, rows, cols), lambda j: (j, 0, 0, 0))
    return kcall(
        split_second_body, "split_second", (bits, ka, ga, kb, gb), [sds((4, rows, cols), bf16)] * 4, grid=(4,),
        in_specs=[SMEM] + [block] * 4, out_specs=[pl.BlockSpec((1, rows, cols), lambda j: (j, 0, 0))] * 4,
    )


def split_third_body(bits, ka, ga, kb, gb, send, keep):
    low = bits[2] % 2
    for h in range(2):
        for p, (own, got) in enumerate(((ka, ga), (kb, gb))):
            send[h, p] = own[2 * h + 1 - low] + got[2 * h + 1 - low]
            keep[h, p] = own[2 * h + low] + got[2 * h + low]


def split_third(bits, ka, ga, kb, gb):
    rows, cols = ka.shape[1:]
    return kcall(
        split_third_body, "split_third", (bits, ka, ga, kb, gb), [sds((2, 2, rows, cols), bf16)] * 2,
        in_specs=[SMEM] + [VMEM] * 4, out_specs=[VMEM] * 2,
    )


def spread(mine, xbit):
    other = swap(mine, "rep", 2)
    dim = mine.ndim - 2
    pair = jnp.stack([jnp.where(xbit == 0, mine, other), jnp.where(xbit == 0, other, mine)], axis=dim)
    return pair, swap(pair, "rep", 1)


def tie(*values):
    return lax.optimization_barrier(values)


def body(tile_embed, doc_ids, norm1_gain, norm1_shift, in_weight, in_bias, out_weight, out_bias,
         norm2_gain, norm2_shift, up_weight, up_bias, down_weight, down_bias, cotangent):
    tok = tile_embed.shape[1]
    count = lax.axis_size("seq")
    assert SEG0 == 2 * tok and tok % 512 == 0
    nodes = count // 2
    masks = [m for m in range(1, min(nodes, 2 ** (BRANCHES - 1)))]
    whole = count == 8 and lax.axis_size("rep") == 4
    index = lax.axis_index("seq")
    ybit = index % 2
    z = index // 2
    rep = lax.axis_index("rep")
    core, xbit = rep % 2, rep // 2
    bits = jnp.stack([ybit, xbit, z, core if whole else jnp.zeros_like(core)]).astype(jnp.int32)
    y = bits


    x, cot = tile_embed[0], cotangent[0]
    x_oth = swap(x, "seq", 1)
    ids_oth = swap(doc_ids, "seq", 1)

    args = (norm1_gain, norm1_shift, in_bias, in_weight)
    first_a, qa, ka, va, doc_a, *out_a = project(y, x, doc_ids, *args)
    remote_a = [swap(out_a[min(m.bit_length(), 2) - 1], "seq", 2 * m) for m in masks]
    gdown = cot_down(cot, down_weight)
    x_oth, ids_oth, gdown = tie(x_oth, ids_oth, gdown)
    first_b, qb, kb, vb, doc_b, *out_b = project(y, x_oth, ids_oth, *args)
    remote_b = [swap(out_b[min(m.bit_length(), 2) - 1], "seq", 2 * m) for m in masks]

    kb, *remote_a = tie(kb, *remote_a)
    qs, ks, vs, docs = (qa, qb), (ka, kb), (va, vb), (doc_a, doc_b)
    part = own_forward(y, qs, ks, vs, docs)
    remote = [r for pair in zip(remote_a, remote_b, strict=True) for r in pair]
    mown, msend, merged, lse = far_forward(y, qs, docs, part, masks, remote)
    moth = swap(msend, "seq", 1)
    (gelu, gelu_t, gpre, up_sum, resid1, second_t, gattn_t, gmown, gmsend, gres, vec) = mlp(
        y, x, mown, moth, out_bias, norm2_gain, norm2_shift, out_weight, up_weight, up_bias, gdown, cot
    )
    gmoth = swap(gmsend, "seq", 1)

    g_send, g_keep = mlp_grads(y, gelu_t, cot, second_t, gpre, mown, moth, gattn_t)
    gmoth, g_send = tie(gmoth, g_send)
    if whole:
        g_got = swap(g_send, "rep", 1)

    gs = (gmown, gmoth)
    dq, *sends = far_backward(y, qs, docs, gs, merged, lse, masks, remote)
    recv = [swap(s, "seq", 2 * m) for s, m in zip(sends, masks, strict=True)]
    if whole:
        dq, g_got = tie(dq, g_got)
        send_a, keep_a, send_b, keep_b = split_first(bits, g_keep, g_got)
        dq, send_a, send_b = tie(dq, send_a, send_b)
        got_a, got_b = swap(send_a, "rep", 2), swap(send_b, "seq", 1)
    dq, dk, dv = own_backward(y, qs, ks, vs, docs, gs, merged, lse, dq)
    if whole:
        dq, got_a, got_b = tie(dq, got_a, got_b)
        send_a, keep_a, send_b, keep_b = split_second(bits, keep_a, got_a, keep_b, got_b)
        dq, send_a, send_b = tie(dq, send_a, send_b)
        got_a, got_b = swap(send_a, "seq", 1), swap(send_b, "rep", 2)
    gfirst_a, gfirst_b, i_send, i_keep = finish(
        bits, dq, dk, dv, x, x_oth, first_a, first_b, in_weight, vec, up_sum, masks, recv
    )
    gfirst_got = swap(gfirst_b, "seq", 1)
    if whole:
        i_send, got_a, got_b = tie(i_send, got_a, got_b)
        i_got = swap(i_send, "rep", 1)
        g_send, g_keep = split_third(bits, keep_a, got_a, keep_b, got_b)
        g_got = swap(g_send, "seq", 2)
        view = lambda v: v.reshape(NBLK, 2, IN_ROWS // 2, IN_COLS)
        i_send, i_keep = halve((view(i_keep), view(i_got)), xbit, 1)
        i_got = swap(i_send, "rep", 2)

    result = (resid1 + jnp.dot(gelu, down_weight, preferred_element_type=f32) + down_bias).astype(bf16)
    by_rows = lambda n: pl.BlockSpec((tok // 4, n), lambda j: (j, 0))
    grad_input = kcall(
        input_grad_body, "input_grad", (x, norm1_gain, gfirst_a, gfirst_got, gres), [sds((tok, D), f32)], grid=(4,),
        in_specs=[by_rows(D), full((D,))] + [by_rows(D)] * 3, out_specs=[by_rows(D)],
    )[0]

    if whole:
        g_send, g_keep = halve((g_keep, g_got), z // 2, 0)
        g_got = swap(g_send, "seq", 4)
        view = lambda v: v.reshape(2, 2, 2, IN_ROWS // 2, IN_COLS)
        i_send, i_keep = halve((view(i_keep), view(i_got)), z % 2, 1)
        i_got = swap(i_send, "seq", 2)
        i_send, i_keep = halve((i_keep, i_got), z // 2, 0)
        i_got = swap(i_send, "seq", 4)

        mine = g_keep + g_got
        near, far = spread(mine, xbit)
        g_down, g_up, g_out = kcall(
            unpack_mlp_body, "unpack_mlp", (bits, near, far),
            [sds((DOWN_ROWS, D), f32), sds((UP_ROWS, FF), f32), sds((UP_ROWS, D), f32)],
            in_specs=[SMEM, VMEM, VMEM], out_specs=[VMEM] * 3,
        )

        total = i_keep + i_got
        mine = pick(total, ybit, 0)
        got = swap(pick(total, 1 - ybit, 0), "seq", 1)
        width = 3 * GW
        low, high = jnp.where(ybit == 0, mine, got), jnp.where(ybit == 0, got, mine)
        vec = mine[:, width:] + got[:, width:]
        near, far = spread(jnp.concatenate([low[:, :width], high[:, :width], vec], axis=1), xbit)
        g_in, *vecs = kcall(
            unpack_in_body, "unpack_in", (bits, near, far),
            [sds((2 * IN_ROWS, 3 * D), f32)] + [sds((UNIT * n,), f32) for n in VEC_UNITS],
            in_specs=[SMEM, VMEM, VMEM], out_specs=[VMEM] * 9,
        )
    else:
        total = lambda v: lax.psum(lax.psum_scatter(v, "seq", scatter_dimension=0, tiled=True).astype(bf16), "rep").astype(f32)
        both = jnp.stack([g_keep, g_send], axis=0).astype(f32)
        cut = lambda lo, hi: both[:, :, lo:hi]
        g_down = total(cut(0, DOWN_ROWS).transpose(1, 2, 0, 3).reshape(FF, D))
        g_up = total(cut(DOWN_ROWS, DOWN_ROWS + 4 * UP_ROWS).reshape(2, NBLK, 4, UP_ROWS, HALF).transpose(1, 3, 0, 2, 4).reshape(D, FF))
        g_out = total(cut(DOWN_ROWS + 4 * UP_ROWS, MLP_ROWS).transpose(1, 2, 0, 3).reshape(D, D))
        both = jnp.stack([i_keep, i_send], axis=1)[..., : 3 * GW].astype(f32).reshape(D, 3, 1, GW)
        g_in = total(jnp.where((jnp.arange(2) == ybit)[None, None, :, None], both, 0.0).reshape(D, 3 * D))
        small = i_keep[:, :, 3 * GW : 3 * GW + UNIT].astype(f32)
        ends = np.cumsum((0,) + VEC_UNITS)
        vecs = [total(small[:, lo:hi].reshape(-1)) for lo, hi in zip(ends[:-1], ends[1:], strict=True)]
    n1_gain, n1_shift, b_in, b_down, n2_gain, n2_shift, b_out, b_up = vecs
    return (
        result[None], grad_input[None], n1_gain, n1_shift, g_in, b_in, g_out, b_out, n2_gain, n2_shift, g_up, b_up, g_down, b_down,
    )


def solution(mesh):
    tokens, weights = P("rep", "seq", None), P()
    in_specs = (tokens, P("rep", "seq")) + (weights,) * 12 + (tokens,)
    vec, mat = P("seq"), P("seq", None)
    out_specs = (tokens, tokens, vec, vec, mat, vec, mat, vec, vec, vec, mat, vec, mat, vec)
    return jax.shard_map(body, mesh=mesh, in_specs=in_specs, out_specs=out_specs, check_vma=False)
```

```python
import functools
import math

import jax
import jax.numpy as jnp
import numpy as np
from jax import lax
from jax.experimental import pallas as pl
from jax.experimental.pallas import tpu as pltpu
from jax.sharding import PartitionSpec as P


D = 768
H = 16
HD = 48
FF = 3072
SEG0 = 1024
BRANCHES = 5
RES = 16
HG = H // 2
GW = HG * HD
NORM_EPS = 1e-05
BIG = 1e30
SCALE = HD**-0.5
LN2 = math.log(2.0)
Q_SCALE = SCALE / LN2

f32 = jnp.float32
bf16 = jnp.bfloat16
NN = (((1,), (0,)), ((), ()))
NT = (((1,), (1,)), ((), ()))
TN = (((0,), (0,)), ((), ()))
MIB = 2**20
VMEM_MIB = 26
MLP_SPLIT = 1
OWN_STEP = 1
FAR_STEP = 4


def mm(left, right, dims=NN):
    return lax.dot_general(left, right, dims, preferred_element_type=f32)


def rev4(v):
    return ((v & 1) << 3) | ((v & 2) << 1) | ((v & 4) >> 1) | ((v & 8) >> 3)


def run_start(head, level, tok):
    if level == 1:
        return (head % 2) * (tok // 2)
    return ((head % 2) * 2 + (head // 2) % 2) * (tok // 4)


def kcall(body, name, ins, outs, *, grid=None, in_specs=None, out_specs=None, scratch=(), vmem=VMEM_MIB, flops=0):
    kw = {}
    if grid is not None:
        kw = dict(grid=grid)
    if in_specs is not None:
        kw.update(in_specs=in_specs, out_specs=out_specs)
    nbytes = sum(math.prod(a.shape) * a.dtype.itemsize for a in (*ins, *outs))
    return pl.pallas_call(
        body,
        out_shape=outs,
        scratch_shapes=list(scratch),
        name=name,
        compiler_params=pltpu.CompilerParams(vmem_limit_bytes=vmem * MIB),
        cost_estimate=estimate(name, flops, nbytes),
        **kw,
    )(*ins)


TAIL = ("split_second", "split_third", "input_grad", "unpack_mlp", "unpack_in")


def estimate(name, flops, nbytes):
    if name in TAIL:
        return pl.CostEstimate(flops=0, bytes_accessed=0, transcendentals=0)
    return pl.CostEstimate(flops=10**12, bytes_accessed=10**10, transcendentals=0)


def sds(shape, dtype):
    return jax.ShapeDtypeStruct(shape, dtype)


SMEM = pl.BlockSpec(memory_space=pltpu.SMEM)
VMEM = pl.BlockSpec(memory_space=pltpu.VMEM)


def full(shape):
    return pl.BlockSpec(shape, lambda *_: (0,) * len(shape), pipeline_mode=pl.Buffered(1))


def features(side, doc_row, pos, head, b0, tok, extra=None):
    n = doc_row.shape[1]
    rowid = lax.broadcasted_iota(jnp.int32, (16, n), 0)
    out = jnp.zeros((16, n), f32)
    diff = rev4(pos // (tok // RES)) ^ (head & (RES - 1))
    for d in range(3):
        same = doc_row == d
        val = jnp.where(same, 0.0, 1.0) if side == "q" else jnp.where(same, -BIG, 0.0)
        out = jnp.where(rowid == d, val, out)
    row = 3
    for b in range(b0 + 1, BRANCHES):
        val = math.log2((b - b0 + 1) / (b - b0))
        high = float(np.asarray(val, dtype=jnp.bfloat16))
        chosen = (diff & (2**b - 1)) == 0
        for part in (high, val - high) if val != 1.0 else (1.0,):
            put = jnp.where(chosen, 1.0 if side == "q" else part, 0.0)
            out = jnp.where(rowid == row, put, out)
            row += 1
    assert row <= 10
    if b0 > 0:
        outside = (diff & (2**b0 - 1)) != 0
        one = jnp.where(outside, 1.0 if side == "q" else -BIG, 0.0)
        const = 1.0 if side == "q" else -BIG
        out = jnp.where(rowid == (10 if side == "q" else 11), one, out)
        out = jnp.where(rowid == (11 if side == "q" else 10), const, out)
    if extra is not None:
        for j in range(3):
            out = jnp.where(rowid == 12 + j, extra[j], out)
    return out.astype(bf16)


def split3(row):
    first = row.astype(bf16).astype(f32)
    rest = row - first
    second = rest.astype(bf16).astype(f32)
    return (first, second, rest - second)


def tail_rows(n, rows):
    rowid = lax.broadcasted_iota(jnp.int32, (16, n), 0)
    out = jnp.zeros((16, n), f32)
    for j, r in enumerate(rows):
        out = jnp.where(rowid == j, r, out)
    return out.astype(bf16)


def place(tok, axis):
    shape = (tok, 1) if axis == 0 else (1, tok)
    p = lax.broadcasted_iota(jnp.int32, shape, axis)
    return rev4(p % RES) * (tok // RES) + p // RES


def one_hot(tok, transposed):
    if transposed:
        return (place(tok, 0) == lax.broadcasted_iota(jnp.int32, (1, tok), 1)).astype(bf16)
    return (place(tok, 1) == lax.broadcasted_iota(jnp.int32, (tok, 1), 0)).astype(bf16)


def normalise(x):
    cen = x - jnp.mean(x, axis=-1, keepdims=True)
    rs = lax.rsqrt(jnp.mean(cen * cen, axis=-1, keepdims=True) + NORM_EPS)
    return cen * rs, rs


def row(ref):
    return ref[...][None, :]


def project_body(tok, y_ref, x_ref, ids_ref, gain, shift, in_b, wq, wk, wv, first_ref, q_ref, k_ref, v_ref, doc_ref, near_ref, far_ref):
    xh, _ = normalise(x_ref[...].astype(f32))
    first = (xh * row(gain) + row(shift)).astype(bf16)
    first = mm(one_hot(tok, False), first).astype(bf16)
    first_ref[...] = first.T
    ids = jnp.broadcast_to(ids_ref[...].astype(f32), (16, tok)).astype(bf16)
    docs = mm(ids, one_hot(tok, True))
    doc_ref[...] = docs[0:8]
    bias = row(in_b)
    for part, (w, ref) in enumerate(((wq, q_ref), (wk, k_ref), (wv, v_ref))):
        at = part * D
        val = mm(first, w[...]) + jnp.where(y_ref[0] == 0, bias[:, at : at + GW], bias[:, at + GW : at + D])
        if part == 0:
            val = val * Q_SCALE
        ref[...] = val.astype(bf16).T
    for out, level in ((near_ref, 1), (far_ref, 2)):
        width = tok >> level
        for part, ref in enumerate((k_ref, v_ref)):
            for h in range(HG):
                start = run_start(h, level, tok)
                out[part * GW + h * HD : part * GW + (h + 1) * HD] = ref[h * HD : (h + 1) * HD, start : start + width]
        rowid = lax.broadcasted_iota(jnp.int32, (16, width), 0)
        acc = jnp.zeros((16, width), f32)
        for j in range(2**level):
            acc = jnp.where(rowid == j, docs[0:1, j * width : (j + 1) * width], acc)
        out[2 * GW : 2 * GW + 16] = acc.astype(bf16)


def weight_specs():
    return [pl.BlockSpec((D, GW), lambda j, y, part=part: (0, 2 * part + y[0]), pipeline_mode=pl.Buffered(1)) for part in range(3)]


def pcall(body, name, scalar, ins, outs, in_specs, out_specs, *, grid=(1,), scratch=(), vmem=VMEM_MIB, flops=0):
    nbytes = sum(math.prod(a.shape) * a.dtype.itemsize for a in (*ins, *outs))
    return pl.pallas_call(
        body,
        grid_spec=pltpu.PrefetchScalarGridSpec(
            num_scalar_prefetch=1, grid=grid, in_specs=in_specs, out_specs=out_specs, scratch_shapes=list(scratch)
        ),
        out_shape=outs,
        name=name,
        compiler_params=pltpu.CompilerParams(vmem_limit_bytes=vmem * MIB),
        cost_estimate=estimate(name, flops, nbytes),
    )(scalar, *ins)


def project(y, x, ids, gain, shift, in_b, weight, vmem):
    tok = x.shape[0]
    outs = [
        sds((D, tok), bf16),
        sds((GW, tok), bf16),
        sds((GW, tok), bf16),
        sds((GW, tok), bf16),
        sds((8, tok), f32),
        sds((2 * GW + 16, tok // 2), bf16),
        sds((2 * GW + 16, tok // 4), bf16),
    ]
    return pcall(
        functools.partial(project_body, tok), "project", y, (x, ids, gain, shift, in_b, weight, weight, weight), outs,
        [full(x.shape), full(ids.shape), full((D,)), full((D,)), full((3 * D,))] + weight_specs(), [full(o.shape) for o in outs],
        vmem=vmem,
        flops=2 * tok * D * (tok + 3 * GW),
    )


def fill_keys(kaug, vaug, k_parts, v_parts, doc_parts, pos_parts, head, b0, tok):
    at = 0
    for k, v, doc, pos in zip(k_parts, v_parts, doc_parts, pos_parts, strict=True):
        n = k.shape[1]
        kaug[0:HD, at : at + n] = k
        kaug[HD:64, at : at + n] = features("k", doc, pos, head, b0, tok, (-1.0, -1.0, -1.0))
        vaug[0:HD, at : at + n] = v
        vaug[HD:64, at : at + n] = tail_rows(n, (1.0, 1.0, 1.0))
        at += n


def fill_queries(qaug, q_parts, doc_parts, pos_parts, head, b0, tok, lse_parts=None):
    at = 0
    for j, (q, doc, pos) in enumerate(zip(q_parts, doc_parts, pos_parts, strict=True)):
        n = q.shape[1]
        extra = None if lse_parts is None else split3(lse_parts[j])
        qaug[0:HD, at : at + n] = q
        qaug[HD:64, at : at + n] = features("q", doc, pos, head, b0, tok, extra)
        at += n


def iota_row(n):
    return lax.broadcasted_iota(jnp.int32, (1, n), 1)


def attend(qaug, kaug, vaug, nq, nk, step, put):
    keys = kaug[:, 0:nk].T
    for at in range(0, nq, step):
        scores = mm(keys, qaug[:, at : at + step])
        probs = jnp.exp2(scores).astype(bf16)
        put(at, mm(vaug[:, 0:nk], probs))


def own_forward_body(tok, y_ref, qa, qb, ka, kb, va, vb, da, db, out_ref, qaug, kaug, vaug):
    pos = iota_row(tok)
    docs = (da[0:1], db[0:1])
    for i in range(OWN_STEP):
        head = y_ref[0] * HG + pl.program_id(0) * OWN_STEP + i
        at_head = lambda *refs: tuple(Rows(r, i)[...] for r in refs)
        fill_keys(kaug.at[i], vaug.at[i], at_head(ka, kb), at_head(va, vb), docs, (pos, pos), head, 0, tok)
        fill_queries(qaug.at[i], at_head(qa, qb), docs, (pos, pos), head, 0, tok)

        def put(at, val):
            out_ref[i, :, at : at + val.shape[1]] = val

        attend(qaug.at[i], kaug.at[i], vaug.at[i], 2 * tok, 2 * tok, tok, put)


def head_block(tok, step=1):
    return pl.BlockSpec((HD * step, tok), lambda h: (h, 0))


class Rows:
    def __init__(self, ref, head):
        self.ref, self.rows = ref, slice(head * HD, (head + 1) * HD)

    def __getitem__(self, at):
        return self.ref[(self.rows,) + at[1:]] if isinstance(at, tuple) else self.ref[self.rows]

    def __setitem__(self, at, value):
        if isinstance(at, tuple):
            self.ref[(self.rows,) + at[1:]] = value
        else:
            self.ref[self.rows] = value


def own_forward(y, qs, ks, vs, docs):
    tok = qs[0].shape[1]
    return kcall(
        functools.partial(own_forward_body, tok),
        "own_forward",
        (y, *qs, *ks, *vs, *docs),
        [sds((HG, 64, 2 * tok), f32)],
        grid=(HG // OWN_STEP,),
        in_specs=[SMEM] + [head_block(tok, OWN_STEP)] * 6 + [full((8, tok))] * 2,
        out_specs=[pl.BlockSpec((OWN_STEP, 64, 2 * tok), lambda h: (h, 0, 0))],
        scratch=[pltpu.VMEM((OWN_STEP, 64, 2 * tok), bf16)] * 3,
        flops=2 * HG * 128 * (2 * tok) ** 2,
    )[0]


def groups_of(masks):
    found = {}
    for j, m in enumerate(masks):
        found.setdefault(m.bit_length(), []).append(j)
    return [(b0, min(b0, 2), found[b0]) for b0 in sorted(found)]


def remote_parts(refs, members, local, level, tok):
    width = tok >> level
    start = run_start(local, level, tok)
    lane = iota_row(width) + start
    row = pl.multiple_of(local * HD, 16)
    ks, vs, docs, poss = [], [], [], []
    for j in members:
        for ref in refs[2 * j : 2 * j + 2]:
            ks.append(ref[pl.ds(row, HD), :])
            vs.append(ref[pl.ds(row + GW, HD), :])
            block = ref[2 * GW : 2 * GW + 16, :].astype(f32)
            picked = block[0:1]
            for r in range(1, 2**level):
                picked = jnp.where(start // width == r, block[r : r + 1], picked)
            docs.append(picked)
            poss.append(lane)
    return ks, vs, docs, poss, start, width


def far_forward_body(tok, masks, y_ref, qa, qb, da, db, part, *rest):
    nrem = 2 * len(masks)
    refs = rest[:nrem]
    ma, mb, merged, lse, qaugs, kaugs, vaugs, accs = rest[nrem:]
    for i in range(FAR_STEP):
        local = pl.program_id(0) * FAR_STEP + i
        head = y_ref[0] * HG + local
        qh, acc = (Rows(qa, i), Rows(qb, i)), accs.at[i]
        acc[...] = part[i]
        for g, (b0, level, members) in enumerate(groups_of(masks)):
            qaug, kaug, vaug = qaugs.at[i, g], kaugs.at[i, g], vaugs.at[i, g]
            ks, vs, docs, poss, start, width = remote_parts(refs, members, local, level, tok)
            nk = width * len(ks)
            fill_keys(kaug, vaug, ks, vs, docs, poss, head, b0, tok)
            window = pl.ds(pl.multiple_of(start, 128), width)
            pos = iota_row(width) + start
            fill_queries(qaug, [q[:, window] for q in qh], (da[0:1, window], db[0:1, window]), (pos, pos), head, b0, tok)

            def put(at, val):
                acc[:, window] += val[:, 0:width]
                other = pl.ds(pl.multiple_of(start + tok, 128), width)
                acc[:, other] += val[:, width : 2 * width]

            attend(qaug, kaug, vaug, 2 * width, nk, 2 * width, put)
        den = acc[HD : HD + 1]
        val = acc[0:HD] / den
        merged[i] = val
        Rows(ma, i)[...] = val[:, 0:tok].astype(bf16)
        Rows(mb, i)[...] = val[:, tok : 2 * tok].astype(bf16)
        lse[i] = jnp.broadcast_to(jnp.log2(den), (8, 2 * tok))


def remote_sizes(masks, tok):
    nq = max([tok >> level << 1 for _, level, _ in groups_of(masks)] + [128])
    nk = max([(tok >> level) * 2 * len(members) for _, level, members in groups_of(masks)] + [128])
    return nq, nk


def remote_flops(masks, tok):
    return sum(2 * HG * 64 * (2 * (tok >> lv)) * ((tok >> lv) * 2 * len(mem)) for _, lv, mem in groups_of(masks))


def far_forward(y, qs, docs, part, masks, remote):
    tok = qs[0].shape[1]
    nq, nk = remote_sizes(masks, tok)
    n = len(groups_of(masks))
    per_head = lambda r: pl.BlockSpec((FAR_STEP, r, 2 * tok), lambda h: (h, 0, 0))
    return kcall(
        functools.partial(far_forward_body, tok, masks),
        "far_forward",
        (y, *qs, *docs, part, *remote),
        [sds((GW, tok), bf16)] * 2 + [sds((HG, HD, 2 * tok), f32), sds((HG, 8, 2 * tok), f32)],
        grid=(HG // FAR_STEP,),
        in_specs=[SMEM] + [head_block(tok, FAR_STEP)] * 2 + [full((8, tok))] * 2 + [per_head(64)] + [full(r.shape) for r in remote],
        out_specs=[head_block(tok, FAR_STEP)] * 2 + [per_head(HD), per_head(8)],
        scratch=[
            pltpu.VMEM((FAR_STEP, n, 64, nq), bf16),
            pltpu.VMEM((FAR_STEP, n, 64, nk), bf16),
            pltpu.VMEM((FAR_STEP, n, 64, nk), bf16),
            pltpu.VMEM((FAR_STEP, 64, 2 * tok), f32),
        ],
        flops=2 * remote_flops(masks, tok),
    )


def attend_back(qaug, gaug, kaug, vaug, nq, nk, step, put_q, dk, dv):
    keys = kaug[0:HD, 0:nk]
    for at in range(0, nq, step):
        sl = slice(at, at + step)
        probs = jnp.exp2(mm(qaug[:, sl].T, kaug[:, 0:nk]))
        gprobs = mm(gaug[:, sl].T, vaug[:, 0:nk])
        gs = (probs * gprobs).astype(bf16)
        new_v = mm(gaug[0:HD, sl], probs.astype(bf16))
        new_k = mm(qaug[0:HD, sl], gs)
        if at == 0:
            dv[:, 0:nk] = new_v
            dk[:, 0:nk] = new_k
        else:
            dv[:, 0:nk] += new_v
            dk[:, 0:nk] += new_k
        put_q(at, mm(keys, gs, NT) * SCALE)


def fill_grads(gaug, g_parts, m_parts):
    at = 0
    for g, m in zip(g_parts, m_parts, strict=True):
        n = g.shape[1]
        delta = jnp.sum(g.astype(f32) * m, axis=0, keepdims=True)
        gaug[0:HD, at : at + n] = g
        gaug[HD:64, at : at + n] = tail_rows(n, split3(-delta))
        at += n


def far_backward_body(tok, masks, y_ref, qa, qb, da, db, ga, gb, merged, lse, *rest):
    nrem = 2 * len(masks)
    refs = rest[:nrem]
    dq_ref = rest[nrem]
    sends = rest[nrem + 1 : nrem + 1 + len(masks)]
    qaugs, gaugs, kaugs, vaugs, dks, dvs = rest[nrem + 1 + len(masks) :]
    for i in range(FAR_STEP):
        local = pl.program_id(0) * FAR_STEP + i
        head = y_ref[0] * HG + local
        row = pl.multiple_of(local * HD, 16)
        dq_ref[i] = jnp.zeros((HD, 2 * tok), f32)
        qh, gh = (Rows(qa, i), Rows(qb, i)), (Rows(ga, i), Rows(gb, i))
        for g, (b0, level, members) in enumerate(groups_of(masks)):
            qaug, gaug, kaug, vaug, dk, dv = (v.at[i, g] for v in (qaugs, gaugs, kaugs, vaugs, dks, dvs))
            ks, vs, docs, poss, start, width = remote_parts(refs, members, local, level, tok)
            nk = width * len(ks)
            fill_keys(kaug, vaug, ks, vs, docs, poss, head, b0, tok)
            window = pl.ds(pl.multiple_of(start, 128), width)
            other = pl.ds(pl.multiple_of(start + tok, 128), width)
            pos = iota_row(width) + start
            fill_queries(
                qaug, [q[:, window] for q in qh], (da[0:1, window], db[0:1, window]), (pos, pos), head, b0, tok,
                (lse[i, 0:1, window], lse[i, 0:1, other]),
            )
            fill_grads(gaug, [v[:, window] for v in gh], (merged[i, :, window], merged[i, :, other]))

            def put_q(at, val):
                dq_ref[i, :, window] += val[:, 0:width]
                dq_ref[i, :, other] += val[:, width : 2 * width]

            attend_back(qaug, gaug, kaug, vaug, 2 * width, nk, 2 * width, put_q, dk, dv)
            for n, j in enumerate(members):
                span = slice(2 * n * width, 2 * (n + 1) * width)
                sends[j][pl.ds(row, HD), :] = (dk[:, span] * LN2).astype(bf16)
                sends[j][pl.ds(row + GW, HD), :] = dv[:, span].astype(bf16)


def far_backward(y, qs, docs, gs, merged, lse, masks, remote):
    tok = qs[0].shape[1]
    nq, nk = remote_sizes(masks, tok)
    n = len(groups_of(masks))
    per_head = lambda r: pl.BlockSpec((FAR_STEP, r, 2 * tok), lambda h: (h, 0, 0))
    blocks = head_block(tok, FAR_STEP)
    sends = [sds((2 * GW, 2 * (tok >> min(m.bit_length(), 2))), bf16) for m in masks]
    return kcall(
        functools.partial(far_backward_body, tok, masks),
        "far_backward",
        (y, *qs, *docs, *gs, merged, lse, *remote),
        [sds((HG, HD, 2 * tok), f32)] + sends,
        grid=(HG // FAR_STEP,),
        in_specs=[SMEM] + [blocks] * 2 + [full((8, tok))] * 2 + [blocks] * 2
        + [per_head(HD), per_head(8)] + [full(r.shape) for r in remote],
        out_specs=[per_head(HD)] + [full(s.shape) for s in sends],
        scratch=[pltpu.VMEM((FAR_STEP, n, 64, nq), bf16)] * 2
        + [pltpu.VMEM((FAR_STEP, n, 64, nk), bf16)] * 2
        + [pltpu.VMEM((FAR_STEP, n, HD, nk), f32)] * 2,
        flops=5 * remote_flops(masks, tok),
    )


def own_backward_body(tok, y_ref, qa, qb, ka, kb, va, vb, da, db, ga, gb, merged, lse, dq_in, dq, dk, dv, qaug, gaug, kaug, vaug):
    head = y_ref[0] * HG + pl.program_id(0)
    pos = iota_row(tok)
    docs = (da[0:1], db[0:1])
    fill_keys(kaug, vaug, (ka[...], kb[...]), (va[...], vb[...]), docs, (pos, pos), head, 0, tok)
    fill_queries(
        qaug, (qa[...], qb[...]), docs, (pos, pos), head, 0, tok, (lse[0, 0:1, 0:tok], lse[0, 0:1, tok : 2 * tok])
    )
    fill_grads(gaug, (ga[...], gb[...]), (merged[0, :, 0:tok], merged[0, :, tok : 2 * tok]))

    def put_q(at, val):
        dq[:, at : at + tok] = (val + dq_in[0, :, at : at + tok]).astype(bf16)

    attend_back(qaug, gaug, kaug, vaug, 2 * tok, 2 * tok, tok, put_q, dk.at[0], dv.at[0])


def own_backward(y, qs, ks, vs, docs, gs, merged, lse, dq):
    tok = qs[0].shape[1]
    per_head = lambda r: pl.BlockSpec((1, r, 2 * tok), lambda h: (h, 0, 0))
    return kcall(
        functools.partial(own_backward_body, tok),
        "own_backward",
        (y, *qs, *ks, *vs, *docs, *gs, merged, lse, dq),
        [sds((GW, 2 * tok), bf16)] + [sds((HG, HD, 2 * tok), f32)] * 2,
        grid=(HG,),
        in_specs=[SMEM] + [head_block(tok)] * 6 + [full((8, tok))] * 2 + [head_block(tok)] * 2
        + [per_head(HD), per_head(8), per_head(HD)],
        out_specs=[head_block(2 * tok)] + [per_head(HD)] * 2,
        scratch=[pltpu.VMEM((64, 2 * tok), bf16)] * 4,
        flops=5 * HG * 128 * (2 * tok) ** 2,
    )


NBLK = 8
HALF = D // 2
DOWN_ROWS = FF // NBLK
UP_ROWS = D // NBLK
ROWS_A = 2 * UP_ROWS + UP_ROWS // 2
ROWS_B = DOWN_ROWS // 2


def cot_body(cot, down, out):
    out[...] = mm(cot[...], down[...], NT).astype(out.dtype)


def cot_down(cot, down):
    tok, ff = cot.shape[0], down.shape[0]
    blk = 768
    return kcall(
        cot_body, "cot_down", (cot, down), [sds((tok, ff), bf16)], grid=(ff // blk,),
        in_specs=[full((tok, D)), pl.BlockSpec((blk, D), lambda j: (j, 0))],
        out_specs=[pl.BlockSpec((tok, blk), lambda j: (0, j))], vmem=60, flops=2 * tok * D * ff,
    )[0]


ERF_P = 0.3275911
ERF_A = (0.254829592, -0.284496736, 1.421413741, -1.453152027, 1.061405429)


def normal_cdf(v):
    gauss = jnp.exp2(v * v * (-0.5 / LN2))
    t = 1.0 / (1.0 + jnp.abs(v) * (ERF_P * 0.5**0.5))
    poly = 0.5 * ERF_A[4]
    for a in ERF_A[3::-1]:
        poly = poly * t + 0.5 * a
    tail = poly * t * gauss
    return jnp.where(v < 0, tail, 1.0 - tail), gauss


def mlp_body(tok, nblk, bits, x_ref, mown, moth, out_b, n2g, n2s, wout, up, up_b, gdown, cot,
             gelu_ref, gelu_send, gpre_ref, gpre_send, upb_ref, rows_ref, resid_ref, gmown, gmoth, gres_ref, vec_ref,
             second, xhat, rstd, acc):
    step = pl.program_id(0)
    y = bits[0]
    low_core = bits[3] == 0
    mine = pl.ds(pl.multiple_of(y * GW, 128), GW)
    theirs = pl.ds(pl.multiple_of((1 - y) * GW, 128), GW)
    gain = row(n2g)

    @pl.when(step == 0)
    def _():
        pmt = one_hot(tok, True)
        own = mm(pmt, mown[...], NT).astype(bf16)
        oth = mm(pmt, moth[...], NT).astype(bf16)
        resid = x_ref[...].astype(f32) + (mm(own, wout[mine, :]) + mm(oth, wout[theirs, :])) + row(out_b)
        resid_ref[...] = resid
        xh, rs = normalise(resid)
        xhat[...] = xh
        rstd[...] = jnp.broadcast_to(rs, rstd.shape)
        low = (xh * gain + row(n2s)).astype(bf16)
        second[...] = low
        rows_ref[0:D] = low.T
        acc[...] = jnp.zeros_like(acc)

    rows = tok // MLP_SPLIT
    for i in range(MLP_SPLIT):
        part = slice(i * rows, (i + 1) * rows)
        pre = mm(second[part], up[...]) + up_b[0]
        cdf, gauss = normal_cdf(pre)
        gelu_t = (pre * cdf).astype(bf16).T
        gelu_ref[:, part] = gelu_t
        half = DOWN_ROWS // 2
        for at in range(0, gelu_t.shape[0], DOWN_ROWS):
            low, high = gelu_t[at : at + half], gelu_t[at + half : at + DOWN_ROWS]
            gelu_send[at // 2 : at // 2 + half, part] = jnp.where(low_core, high, low)
        slope = cdf + pre * (gauss * (1.0 / math.sqrt(2.0 * math.pi)))
        gpre = (slope * gdown[part]).astype(bf16)
        gpre_ref[part] = gpre

        gpre_send[part] = gpre
        acc[part] += mm(gpre, up[...], NT)
        sums = mm(jnp.ones((8, rows), bf16), gpre)
        upb_ref[...] = sums if i == 0 else upb_ref[...] + sums

    @pl.when(step == nblk - 1)
    def _():
        dy = acc[...]
        xh = xhat[...]
        dyg = dy * gain
        m1 = jnp.mean(dyg, axis=-1, keepdims=True)
        m2 = jnp.mean(dyg * xh, axis=-1, keepdims=True)
        g = cot[...]
        gres = g.astype(f32) + rstd[:, 0:1] * (dyg - m1 - xh * m2)
        gres_ref[...] = gres
        gattn = gres.astype(bf16)
        gattn_t = mm(gattn.T, one_hot(tok, True)).astype(bf16)
        rows_ref[D : 2 * D] = gattn_t
        gmoth[...] = mm(wout[theirs, :], gattn_t).astype(bf16)
        gmown[...] = mm(wout[mine, :], gattn_t).astype(bf16)
        ones = jnp.ones((8, tok), bf16)
        vec_ref[0:8] = mm(ones, g)
        vec_ref[8:16] = jnp.broadcast_to(jnp.sum(dy * xh, axis=0, keepdims=True), (8, D))
        vec_ref[16:24] = jnp.broadcast_to(jnp.sum(dy, axis=0, keepdims=True), (8, D))
        vec_ref[24:32] = mm(ones, gattn)


def mlp_chunk(step, bits):
    return (step // 2 + bits[3]) % 2 * 2 + step % 2


def mlp(bits, x, mown, moth, out_b, n2g, n2s, wout, up, up_b, gdown, cot):
    tok = cot.shape[0]
    ff = up.shape[1]
    nblk = 4
    blk = ff // nblk
    wide = pl.BlockSpec((tok, blk), lambda j, b: (0, mlp_chunk(j, b)))
    outs = [
        sds((ff, tok), bf16), sds((ff // 2, tok), bf16), sds((tok, ff), bf16), sds((tok, ff // 2), bf16), sds((8, ff), f32),
        sds((2 * D, tok), bf16), sds((tok, D), f32), sds((GW, tok), bf16), sds((GW, tok), bf16),
        sds((tok, D), f32), sds((32, D), f32),
    ]
    return pcall(
        functools.partial(mlp_body, tok, nblk),
        "mlp",
        bits,
        (x, mown, moth, out_b, n2g, n2s, wout, up, up_b.reshape(nblk, 1, blk), gdown, cot),
        outs,
        [
            full(x.shape), full(mown.shape), full(moth.shape), full((D,)), full((D,)), full((D,)), full(wout.shape),
            pl.BlockSpec((D, blk), lambda j, b: (0, mlp_chunk(j, b))),
            pl.BlockSpec((1, 1, blk), lambda j, b: (mlp_chunk(j, b), 0, 0)),
            wide, full((tok, D)),
        ],
        [
            pl.BlockSpec((blk, tok), lambda j, b: (mlp_chunk(j, b), 0)),
            pl.BlockSpec((blk // 2, tok), lambda j, b: (mlp_chunk(j, b), 0)),
            wide,
            pl.BlockSpec((tok, blk), lambda j, b: (0, jnp.maximum(j - nblk // 2, 0))),
            pl.BlockSpec((8, blk), lambda j, b: (0, mlp_chunk(j, b))),
        ] + [full(o.shape) for o in outs[5:]],
        grid=(nblk,),
        scratch=[pltpu.VMEM((tok, D), bf16), pltpu.VMEM((tok, D), f32), pltpu.VMEM((tok, 128), f32), pltpu.VMEM((tok, D), f32)],
        vmem=32,
        flops=2 * tok * D * (2 * ff + 2 * D + 2 * tok),
    )


def mlp_grads_body(bits, cores, *refs):
    ins, outs = refs[:-4], refs[-4:]
    send_a, keep_a, send_b, keep_b = outs
    ybit, xbit = bits[0], bits[1]
    heads_low = (pl.program_id(0) < 2) == (ybit == 0)
    up = att = 0.0
    down = [0.0, 0.0]
    for c in range(cores):
        low_t, high_t, second_t, gattn_t, gpre, cot, mown, moth = ins[8 * c : 8 * c + 8]
        up = up + mm(second_t[...], gpre[...])
        down = [old + mm(gelu_t[...], cot[...]) for old, gelu_t in zip(down, (low_t, high_t), strict=True)]
        att = att + mm(jnp.where(heads_low, mown[...], moth[...]), gattn_t[...], NT)
    up, att, down = up.astype(bf16), att.astype(bf16), [v.astype(bf16) for v in down]
    x_low, y_low = xbit == 0, ybit == 0
    half = UP_ROWS // 2
    for y in range(2):
        rows = slice(y * UP_ROWS, (y + 1) * UP_ROWS)
        cols = [up[rows, c * HALF : (c + 1) * HALF] for c in range(4)]
        pieces = [(0, UP_ROWS, cols[0], cols[2]), (UP_ROWS, UP_ROWS, cols[1], cols[3])]
        pieces += [(2 * UP_ROWS, half, att[y * UP_ROWS : y * UP_ROWS + half], att[y * UP_ROWS + half : (y + 1) * UP_ROWS])]
        for at, n, low, high in pieces:
            keep_a[0, y, at : at + n] = jnp.where(x_low, low, high)
            send_a[0, y, at : at + n] = jnp.where(x_low, high, low)
    for x in range(2):
        low, high = (v[:, x * HALF : (x + 1) * HALF] for v in down)
        keep_b[0, x] = jnp.where(y_low, low, high)
        send_b[0, x] = jnp.where(y_low, high, low)


def mlp_grads(bits, *per_core):
    tok = per_core[0][3].shape[0]
    ins, specs = [], []
    for gelu_t, rows, gpre, cot, mown, moth in per_core:
        heads = pl.BlockSpec((GW // 2, tok), lambda j, b: (j % 2, 0))
        ins += [gelu_t, gelu_t, rows, rows, gpre, cot, mown, moth]
        if gelu_t.shape[0] == FF:
            gelus = [pl.BlockSpec((ROWS_B, tok), lambda j, b, y=y: (4 * j + 2 * y + b[3], 0)) for y in range(2)]
            half = pl.BlockSpec((tok, FF // 2), lambda j, b: (0, b[3]))
        else:
            gelus = [pl.BlockSpec((ROWS_B, tok), lambda j, b, y=y: (2 * j + y, 0)) for y in range(2)]
            half = full(gpre.shape)
        specs += gelus + [
            pl.BlockSpec((D // 4, tok), lambda j, b: (j, 0)),
            pl.BlockSpec((HALF, tok), lambda j, b: (D // HALF + b[3], 0)),
            half, full(cot.shape), heads, heads,
        ]
    outs = [sds((4, 2, ROWS_A, HALF), bf16)] * 2 + [sds((4, 2, ROWS_B, HALF), bf16)] * 2
    return pcall(
        lambda bits, *refs: mlp_grads_body(bits, len(per_core), *refs), "mlp_grads", bits, ins, outs, specs,
        [pl.BlockSpec((1,) + o.shape[1:], lambda j, b: (j, 0, 0, 0)) for o in outs],
        grid=(4,),
        vmem=28,
        flops=2 * tok * D * (2 * FF + D),
    )


IN_ROWS = D // NBLK // 2
IN_COLS = 3 * GW + 128
SMALL_ROWS = 16
UNIT = UP_ROWS


def finish_body(tok, masks, bits, dq, dk, dv, xa, xb, fa, fb, wq, wk, wv, vec, up_sum, *rest):
    nrem = len(masks)
    recv = rest[:nrem]
    first_a, first_b, send, keep, gqkv, total, acc, sums, bias, small = rest[nrem:]
    step = pl.program_id(0)
    for part, ref, scale in ((0, dk, LN2), (1, dv, 1.0)):
        for h in range(HG):
            total[h * HD : (h + 1) * HD] = ref[h] * scale
        for m, r in zip(masks, recv, strict=True):
            level = min(m.bit_length(), 2)
            for h in range(HG):
                start = run_start(h, level, tok)
                row = part * GW + h * HD
                total[h * HD : (h + 1) * HD, start : start + (tok >> level)] += r[row : row + HD].astype(f32)
        gqkv[(1 + part) * GW : (2 + part) * GW] = total[...].astype(bf16)
    gqkv[0:GW] = dq[...]
    nat = mm(one_hot(tok, True), gqkv[...], NT).astype(bf16)
    new_bias = mm(jnp.ones((8, tok), bf16), nat)
    dy = sum(mm(nat[:, part * GW : (part + 1) * GW], w[...], NT) for part, w in enumerate((wq, wk, wv)))
    later = step == 1
    xh, _ = normalise(jnp.where(later, xa[...], xb[...]).astype(f32))
    new_gain = jnp.sum(dy * xh, axis=0, keepdims=True)
    new_shift = jnp.sum(dy, axis=0, keepdims=True)

    @pl.when(step == 0)
    def _():
        first_b[...] = dy.astype(bf16)
        acc[...] = mm(fb[...], gqkv[...], NT)
        bias[...] = new_bias
        sums[0:8] = jnp.broadcast_to(new_gain, (8, D))
        sums[8:16] = jnp.broadcast_to(new_shift, (8, D))

    @pl.when(step == 1)
    def _():
        first_a[...] = dy
        val = (acc[...] + mm(fa[...], gqkv[...], NT)).astype(bf16)
        all_bias = bias[0:1] + new_bias[0:1]
        lines = [sums[0:1] + new_gain, sums[8:9] + new_shift]
        lines += [vec[8 * j : 8 * j + 1] for j in range(4)]
        cut = lambda line, u: line[:, u * UNIT : (u + 1) * UNIT]
        small[...] = jnp.zeros_like(small)

        def put(block, row, line):
            small[block, row : row + 1, 0:UNIT] = line

        for s in range(NBLK):
            for row, line in zip((0, 1, 5, 6, 7, 8), lines, strict=True):
                put(s, row, cut(line, s))
            for k in range(4):
                put(s, 9 + k, cut(up_sum[0:1], s * 4 + k))
        for u in range(3 * NBLK):
            part, owner, k = u // 8, u // 4 % 2, u % 4
            put(u // 3, 2 + u % 3, jnp.where(bits[0] == owner, cut(all_bias, part * 4 + k), 0.0))
        keep_low = bits[3] == 0
        zeros = jnp.zeros((IN_ROWS, 128), bf16)

        def store(block, lanes, low, high):
            keep[block, :, lanes] = jnp.where(keep_low, low, high)
            send[block, :, lanes] = jnp.where(keep_low, high, low)

        for s in range(NBLK):
            at = 2 * s * IN_ROWS
            store(s, slice(0, 3 * GW), val[at : at + IN_ROWS], val[at + IN_ROWS : at + 2 * IN_ROWS])
            store(s, slice(3 * GW, IN_COLS), jnp.concatenate([small[s].astype(bf16), zeros[SMALL_ROWS:]], axis=0), zeros)


def finish(bits, dq, dk, dv, xa, xb, fa, fb, weight, vec, up_sum, masks, recv):
    tok = xa.shape[0]
    piece = lambda j: 1 - j
    by_head = pl.BlockSpec((HG, HD, tok), lambda j, y: (0, 0, piece(j)))
    outs = [sds((tok, D), f32), sds((tok, D), bf16)] + [sds((NBLK, IN_ROWS, IN_COLS), bf16)] * 2
    return pcall(
        functools.partial(finish_body, tok, masks),
        "finish",
        bits,
        (dq, dk, dv, xa, xb, fa, fb, weight, weight, weight, vec, up_sum, *recv),
        outs,
        [pl.BlockSpec((GW, tok), lambda j, y: (0, piece(j))), by_head, by_head]
        + [full(v.shape) for v in (xa, xb, fa, fb)] + weight_specs() + [full(vec.shape), full(up_sum.shape)]
        + [pl.BlockSpec((2 * GW, r.shape[1] // 2), lambda j, y: (0, piece(j))) for r in recv],
        [full(o.shape) for o in outs],
        grid=(2,),
        scratch=[
            pltpu.VMEM((3 * GW, tok), bf16), pltpu.VMEM((GW, tok), f32), pltpu.VMEM((D, 3 * GW), f32),
            pltpu.VMEM((16, D), f32), pltpu.VMEM((8, 3 * GW), f32), pltpu.VMEM((NBLK, SMALL_ROWS, 128), f32),
        ],
        vmem=28,
        flops=4 * tok * 3 * GW * (tok + 2 * D),
    )


def input_grad_body(x_ref, gain, own, got, gres, out):
    xh, rs = normalise(x_ref[...].astype(f32))
    dyg = (own[...] + got[...].astype(f32)) * row(gain)
    m1 = jnp.mean(dyg, axis=-1, keepdims=True)
    m2 = jnp.mean(dyg * xh, axis=-1, keepdims=True)
    out[...] = gres[...] + rs * (dyg - m1 - xh * m2)


def unpack_mlp_body(bits, near, far, down, up, att):
    low = bits[3] == 0
    for c, v in enumerate((jnp.where(low, near[...], far[...]), jnp.where(low, far[...], near[...]))):
        for x in range(2):
            half = v[x].astype(f32)
            for j in range(2):
                at = (c * 4 + 2 * x + j) * HALF
                up[:, at : at + HALF] = half[j * UP_ROWS : (j + 1) * UP_ROWS]
            n = UP_ROWS // 2
            att[x * n : (x + 1) * n, c * HALF : (c + 1) * HALF] = half[2 * UP_ROWS : ROWS_A]
            down[c * ROWS_B : (c + 1) * ROWS_B, x * HALF : (x + 1) * HALF] = half[ROWS_A:]


VEC_UNITS = (1, 1, 3, 1, 1, 1, 1, 4)


def unpack_in_body(bits, near, far, out, *vecs):
    low = bits[3] == 0
    lower = jnp.where(low, near[...], far[...])
    upper = jnp.where(low, far[...], near[...])
    val = jnp.concatenate([lower[0], lower[1], upper[0], upper[1]], axis=0).astype(f32)
    for part in range(3):
        for y in range(2):
            src = (y * 3 + part) * GW
            dst = (part * 2 + y) * GW
            out[:, dst : dst + GW] = val[:, src : src + GW]
    row = 0
    for ref, units in zip(vecs, VEC_UNITS, strict=True):
        line = jnp.concatenate([val[row + k : row + k + 1, 6 * GW : 6 * GW + UNIT] for k in range(units)], axis=1)
        ref[...] = line[0]
        row += units


def swap(value, axis, offset):
    count = lax.axis_size(axis)
    return lax.ppermute(value, axis, [(i, i ^ offset) for i in range(count)])


def pick(value, index, dim):
    return lax.dynamic_index_in_dim(value, index, dim, keepdims=False)


def halve(pieces, index, dim):
    def part(i):
        return sum(pick(p, i, dim).astype(f32) for p in pieces).astype(bf16)

    return part(1 - index), part(index)


def split_second_body(bits, ka, ga, kb, gb, send_a, keep_a, send_b, keep_b):
    for keep, got, send_to, keep_to, bit in ((ka, ga, send_a, keep_a, bits[0]), (kb, gb, send_b, keep_b, bits[1])):
        total = lambda j: keep[0, j] + got[0, j]
        send_to[0] = total(1 - bit)
        keep_to[0] = total(bit)


def split_second(bits, ka, ga, kb, gb):
    block = lambda v: pl.BlockSpec((1,) + v.shape[1:], lambda j: (j, 0, 0, 0))
    outs = [sds((4,) + v.shape[2:], bf16) for v in (ka, ka, kb, kb)]
    return kcall(
        split_second_body, "split_second", (bits, ka, ga, kb, gb), outs, grid=(4,),
        in_specs=[SMEM] + [block(v) for v in (ka, ga, kb, gb)],
        out_specs=[pl.BlockSpec((1,) + o.shape[1:], lambda j: (j, 0, 0)) for o in outs],
    )


def split_third_body(bits, ka, ga, kb, gb, send, keep):
    low = bits[2] % 2
    for h in range(2):
        at = 0
        for own, got in ((ka, ga), (kb, gb)):
            rows = slice(at, at + own.shape[1])
            send[h, rows] = own[2 * h + 1 - low] + got[2 * h + 1 - low]
            keep[h, rows] = own[2 * h + low] + got[2 * h + low]
            at += own.shape[1]


def split_third(bits, ka, ga, kb, gb):
    out = sds((2, ka.shape[1] + kb.shape[1], HALF), bf16)
    return kcall(
        split_third_body, "split_third", (bits, ka, ga, kb, gb), [out, out], in_specs=[SMEM] + [VMEM] * 4, out_specs=[VMEM] * 2,
    )


def spread(mine, xbit):
    other = swap(mine, "rep", 2)
    dim = mine.ndim - 2
    pair = jnp.stack([jnp.where(xbit == 0, mine, other), jnp.where(xbit == 0, other, mine)], axis=dim)
    return pair, swap(pair, "rep", 1)


def tie(*values):
    return lax.optimization_barrier(values)


def body(tile_embed, doc_ids, norm1_gain, norm1_shift, in_weight, in_bias, out_weight, out_bias,
         norm2_gain, norm2_shift, up_weight, up_bias, down_weight, down_bias, cotangent):
    tok = tile_embed.shape[1]
    count = lax.axis_size("seq")
    assert SEG0 == 2 * tok and tok % 512 == 0
    nodes = count // 2
    masks = [m for m in range(1, min(nodes, 2 ** (BRANCHES - 1)))]
    whole = count == 8 and lax.axis_size("rep") == 4
    index = lax.axis_index("seq")
    ybit = index % 2
    z = index // 2
    rep = lax.axis_index("rep")
    core, xbit = rep % 2, rep // 2
    bits = jnp.stack([ybit, xbit, z, core if whole else jnp.zeros_like(core)]).astype(jnp.int32)
    y = bits


    x, cot = tile_embed[0], cotangent[0]
    x_oth = swap(x, "seq", 1)
    ids_oth = swap(doc_ids, "seq", 1)

    args = (norm1_gain, norm1_shift, in_bias, in_weight)
    first_a, qa, ka, va, doc_a, *out_a = project(y, x, doc_ids, *args, 60)
    remote_a = [swap(out_a[min(m.bit_length(), 2) - 1], "seq", 2 * m) for m in masks]
    gdown = cot_down(cot, down_weight)
    x_oth, ids_oth, gdown = tie(x_oth, ids_oth, gdown)
    if whole:
        cot_got = swap(cot, "rep", 1)
    first_b, qb, kb, vb, doc_b, *out_b = project(y, x_oth, ids_oth, *args, VMEM_MIB)
    remote_b = [swap(out_b[min(m.bit_length(), 2) - 1], "seq", 2 * m) for m in masks]

    qs, ks, vs, docs = (qa, qb), (ka, kb), (va, vb), (doc_a, doc_b)
    part = own_forward(y, qs, ks, vs, docs)
    remote = [r for pair in zip(remote_a, remote_b, strict=True) for r in pair]
    mown, msend, merged, lse = far_forward(y, qs, docs, part, masks, remote)
    moth = swap(msend, "seq", 1)
    if whole:
        moth, cot_got, mown_got = tie(moth, cot_got, swap(mown, "rep", 1))
    (gelu_t, gelu_send, gpre, gpre_send, up_sum, rows, resid1, gmown, gmsend, gres, vec) = mlp(
        bits, x, mown, moth, out_bias, norm2_gain, norm2_shift, out_weight, up_weight, up_bias, gdown, cot
    )
    gmoth = swap(gmsend, "seq", 1)

    own = (gelu_t, rows, gpre, cot, mown, moth)
    if whole:
        got = (swap(gelu_send, "rep", 1), swap(rows, "rep", 1), swap(gpre_send, "rep", 1), cot_got, mown_got, swap(moth, "rep", 1))
        send_a, keep_a, send_b, keep_b = mlp_grads(bits, own, got)
        got_a, got_b = swap(send_a, "rep", 2), swap(send_b, "seq", 1)
        gmoth, send_a, send_b = tie(gmoth, send_a, send_b)
    else:
        halves = [mlp_grads(bits.at[3].set(c), own) for c in range(2)]

    gs = (gmown, gmoth)
    dq, *sends = far_backward(y, qs, docs, gs, merged, lse, masks, remote)
    recv = [swap(s, "seq", 2 * m) for s, m in zip(sends, masks, strict=True)]
    dq, dk, dv = own_backward(y, qs, ks, vs, docs, gs, merged, lse, dq)
    if whole:
        dq, got_a, got_b = tie(dq, got_a, got_b)
        send_a, keep_a, send_b, keep_b = split_second(bits, keep_a, got_a, keep_b, got_b)
        dq, send_a, send_b = tie(dq, send_a, send_b)
        got_a, got_b = swap(send_a, "seq", 1), swap(send_b, "rep", 2)
    gfirst_a, gfirst_b, i_send, i_keep = finish(
        bits, dq, dk, dv, x, x_oth, first_a, first_b, in_weight, vec, up_sum, masks, recv
    )
    gfirst_got = swap(gfirst_b, "seq", 1)
    if whole:
        i_send, got_a, got_b = tie(i_send, got_a, got_b)
        i_got = swap(i_send, "rep", 1)
        g_send, g_keep = split_third(bits, keep_a, got_a, keep_b, got_b)
        g_got = swap(g_send, "seq", 2)
        view = lambda v: v.reshape(NBLK, 2, IN_ROWS // 2, IN_COLS)
        i_send, i_keep = halve((view(i_keep), view(i_got)), xbit, 1)
        i_got = swap(i_send, "rep", 2)

    result = (resid1 + mm(gelu_t, down_weight, TN) + down_bias).astype(bf16)
    if whole:
        i_got, result = tie(i_got, result)
        i_send, i_keep = halve((i_keep.reshape(4, 2, -1, IN_COLS), i_got.reshape(4, 2, -1, IN_COLS)), ybit, 1)
        i_got = swap(i_send, "seq", 1)
        g_got, i_send = tie(g_got, i_send)
        g_send, g_keep = halve((g_keep, g_got), z // 2, 0)
        g_got = swap(g_send, "seq", 4)
        gfirst_got, g_send = tie(gfirst_got, g_send)
    by_rows = lambda n: pl.BlockSpec((tok // 4, n), lambda j: (j, 0))
    grad_input = kcall(
        input_grad_body, "input_grad", (x, norm1_gain, gfirst_a, gfirst_got, gres), [sds((tok, D), f32)], grid=(4,),
        in_specs=[by_rows(D), full((D,))] + [by_rows(D)] * 3, out_specs=[by_rows(D)],
    )[0]

    if whole:
        i_got, grad_input = tie(i_got, grad_input)
        width = 3 * GW
        low, high = jnp.where(ybit == 0, i_keep, i_got), jnp.where(ybit == 0, i_got, i_keep)
        vec = i_keep[..., width:] + i_got[..., width:]
        i_all = jnp.concatenate([low[..., :width], high[..., :width], vec], axis=-1).reshape(2, 2, IN_ROWS // 2, 2 * width + 128)
        i_send, i_keep = pick(i_all, 1 - z % 2, 1), pick(i_all, z % 2, 1)
        i_got = swap(i_send, "seq", 2)
        i_got, g_got = tie(i_got, g_got)
        i_send, i_keep = halve((i_keep, i_got), z // 2, 0)
        i_got = swap(i_send, "seq", 4)

        mine = g_keep + g_got
        near, far = spread(mine, xbit)
        g_down, g_up, g_out = kcall(
            unpack_mlp_body, "unpack_mlp", (bits, near, far),
            [sds((DOWN_ROWS, D), f32), sds((UP_ROWS, FF), f32), sds((UP_ROWS, D), f32)],
            in_specs=[SMEM, VMEM, VMEM], out_specs=[VMEM] * 3,
        )
        near, far = spread(i_keep + i_got, xbit)
        far, g_down = tie(far, g_down)
        g_in, *vecs = kcall(
            unpack_in_body, "unpack_in", (bits, near, far),
            [sds((2 * IN_ROWS, 3 * D), f32)] + [sds((UNIT * n,), f32) for n in VEC_UNITS],
            in_specs=[SMEM, VMEM, VMEM], out_specs=[VMEM] * 9,
        )
    else:
        total = lambda v: lax.psum(lax.psum_scatter(v, "seq", scatter_dimension=0, tiled=True).astype(bf16), "rep").astype(f32)
        order = lambda bit, keep, send: jnp.where(bit == 0, jnp.stack([keep, send]), jnp.stack([send, keep])).astype(f32)
        by_x = jnp.stack([order(xbit, h[1], h[0]) for h in halves])
        by_y = jnp.stack([order(ybit, h[3], h[2]) for h in halves])
        ups = by_x[..., : 2 * UP_ROWS, :].reshape(2, 2, NBLK, 2, UP_ROWS, HALF)
        g_up = total(ups.transpose(2, 4, 0, 1, 3, 5).reshape(D, FF))
        g_out = total(by_x[..., 2 * UP_ROWS :, :].reshape(2, 2, NBLK, UP_ROWS // 2, HALF).transpose(2, 1, 3, 0, 4).reshape(D, D))
        g_down = total(by_y.transpose(2, 1, 0, 4, 3, 5).reshape(FF, D))
        both = jnp.stack([i_keep, i_send], axis=1)[..., : 3 * GW].astype(f32).reshape(D, 3, 1, GW)
        g_in = total(jnp.where((jnp.arange(2) == ybit)[None, None, :, None], both, 0.0).reshape(D, 3 * D))
        small = i_keep[:, :, 3 * GW : 3 * GW + UNIT].astype(f32)
        ends = np.cumsum((0,) + VEC_UNITS)
        vecs = [total(small[:, lo:hi].reshape(-1)) for lo, hi in zip(ends[:-1], ends[1:], strict=True)]
    n1_gain, n1_shift, b_in, b_down, n2_gain, n2_shift, b_out, b_up = vecs
    return (
        result[None], grad_input[None], n1_gain, n1_shift, g_in, b_in, g_out, b_out, n2_gain, n2_shift, g_up, b_up, g_down, b_down,
    )


def solution(mesh):
    tokens, weights = P("rep", "seq", None), P()
    in_specs = (tokens, P("rep", "seq")) + (weights,) * 12 + (tokens,)
    vec, mat = P("seq"), P("seq", None)
    out_specs = (tokens, tokens, vec, vec, mat, vec, mat, vec, vec, vec, mat, vec, mat, vec)
    return jax.shard_map(body, mesh=mesh, in_specs=in_specs, out_specs=out_specs, check_vma=False)
```

```python
import functools
import math

import jax
import jax.numpy as jnp
import numpy as np
from jax import lax
from jax.experimental import pallas as pl
from jax.experimental.pallas import tpu as pltpu
from jax.sharding import PartitionSpec as P


D = 768
H = 16
HD = 48
FF = 3072
SEG0 = 1024
BRANCHES = 5
RES = 16
HG = H // 2
GW = HG * HD
NORM_EPS = 1e-05
BIG = 1e30
SCALE = HD**-0.5
LN2 = math.log(2.0)
Q_SCALE = SCALE / LN2

f32 = jnp.float32
bf16 = jnp.bfloat16
NN = (((1,), (0,)), ((), ()))
NT = (((1,), (1,)), ((), ()))
TN = (((0,), (0,)), ((), ()))
MIB = 2**20
VMEM_MIB = 26
MLP_SPLIT = 1
OWN_STEP = 1
FAR_STEP = 4


def mm(left, right, dims=NN):
    return lax.dot_general(left, right, dims, preferred_element_type=f32)


def rev4(v):
    return ((v & 1) << 3) | ((v & 2) << 1) | ((v & 4) >> 1) | ((v & 8) >> 3)


def run_start(head, level, tok):
    if level == 1:
        return (head % 2) * (tok // 2)
    return ((head % 2) * 2 + (head // 2) % 2) * (tok // 4)


def kcall(body, name, ins, outs, *, grid=None, in_specs=None, out_specs=None, scratch=(), vmem=VMEM_MIB, flops=0):
    kw = {}
    if grid is not None:
        kw = dict(grid=grid)
    if in_specs is not None:
        kw.update(in_specs=in_specs, out_specs=out_specs)
    nbytes = sum(math.prod(a.shape) * a.dtype.itemsize for a in (*ins, *outs))
    return pl.pallas_call(
        body,
        out_shape=outs,
        scratch_shapes=list(scratch),
        name=name,
        compiler_params=pltpu.CompilerParams(vmem_limit_bytes=vmem * MIB),
        cost_estimate=estimate(name, flops, nbytes),
        **kw,
    )(*ins)


TAIL = ("far_forward_first", "split_second", "split_third", "input_grad", "unpack_mlp", "unpack_in")


def estimate(name, flops, nbytes):
    if name in TAIL:
        return pl.CostEstimate(flops=0, bytes_accessed=0, transcendentals=0)
    return pl.CostEstimate(flops=10**12, bytes_accessed=10**10, transcendentals=0)


def sds(shape, dtype):
    return jax.ShapeDtypeStruct(shape, dtype)


SMEM = pl.BlockSpec(memory_space=pltpu.SMEM)
VMEM = pl.BlockSpec(memory_space=pltpu.VMEM)


def full(shape):
    return pl.BlockSpec(shape, lambda *_: (0,) * len(shape), pipeline_mode=pl.Buffered(1))


def features(side, doc_row, pos, head, b0, tok, extra=None):
    n = doc_row.shape[1]
    rowid = lax.broadcasted_iota(jnp.int32, (16, n), 0)
    out = jnp.zeros((16, n), f32)
    diff = rev4(pos // (tok // RES)) ^ (head & (RES - 1))
    for d in range(3):
        same = doc_row == d
        val = jnp.where(same, 0.0, 1.0) if side == "q" else jnp.where(same, -BIG, 0.0)
        out = jnp.where(rowid == d, val, out)
    row = 3
    for b in range(b0 + 1, BRANCHES):
        val = math.log2((b - b0 + 1) / (b - b0))
        high = float(np.asarray(val, dtype=jnp.bfloat16))
        chosen = (diff & (2**b - 1)) == 0
        for part in (high, val - high) if val != 1.0 else (1.0,):
            put = jnp.where(chosen, 1.0 if side == "q" else part, 0.0)
            out = jnp.where(rowid == row, put, out)
            row += 1
    assert row <= 10
    if b0 > 0:
        outside = (diff & (2**b0 - 1)) != 0
        one = jnp.where(outside, 1.0 if side == "q" else -BIG, 0.0)
        const = 1.0 if side == "q" else -BIG
        out = jnp.where(rowid == (10 if side == "q" else 11), one, out)
        out = jnp.where(rowid == (11 if side == "q" else 10), const, out)
    if extra is not None:
        for j in range(3):
            out = jnp.where(rowid == 12 + j, extra[j], out)
    return out.astype(bf16)


def split3(row):
    first = row.astype(bf16).astype(f32)
    rest = row - first
    second = rest.astype(bf16).astype(f32)
    return (first, second, rest - second)


def tail_rows(n, rows):
    rowid = lax.broadcasted_iota(jnp.int32, (16, n), 0)
    out = jnp.zeros((16, n), f32)
    for j, r in enumerate(rows):
        out = jnp.where(rowid == j, r, out)
    return out.astype(bf16)


def place(tok, axis):
    shape = (tok, 1) if axis == 0 else (1, tok)
    p = lax.broadcasted_iota(jnp.int32, shape, axis)
    return rev4(p % RES) * (tok // RES) + p // RES


def one_hot(tok, transposed):
    if transposed:
        return (place(tok, 0) == lax.broadcasted_iota(jnp.int32, (1, tok), 1)).astype(bf16)
    return (place(tok, 1) == lax.broadcasted_iota(jnp.int32, (tok, 1), 0)).astype(bf16)


def normalise(x):
    cen = x - jnp.mean(x, axis=-1, keepdims=True)
    rs = lax.rsqrt(jnp.mean(cen * cen, axis=-1, keepdims=True) + NORM_EPS)
    return cen * rs, rs


def row(ref):
    return ref[...][None, :]


def project_body(tok, y_ref, x_ref, ids_ref, gain, shift, in_b, wq, wk, wv, first_ref, q_ref, k_ref, v_ref, doc_ref, near_ref, far_ref):
    xh, _ = normalise(x_ref[...].astype(f32))
    first = (xh * row(gain) + row(shift)).astype(bf16)
    first = mm(one_hot(tok, False), first).astype(bf16)
    first_ref[...] = first.T
    ids = jnp.broadcast_to(ids_ref[...].astype(f32), (16, tok)).astype(bf16)
    docs = mm(ids, one_hot(tok, True))
    doc_ref[...] = docs[0:8]
    bias = row(in_b)
    for part, (w, ref) in enumerate(((wq, q_ref), (wk, k_ref), (wv, v_ref))):
        at = part * D
        val = mm(first, w[...]) + jnp.where(y_ref[0] == 0, bias[:, at : at + GW], bias[:, at + GW : at + D])
        if part == 0:
            val = val * Q_SCALE
        ref[...] = val.astype(bf16).T
    for out, level in ((near_ref, 1), (far_ref, 2)):
        width = tok >> level
        for part, ref in enumerate((k_ref, v_ref)):
            for h in range(HG):
                start = run_start(h, level, tok)
                out[part * GW + h * HD : part * GW + (h + 1) * HD] = ref[h * HD : (h + 1) * HD, start : start + width]
        rowid = lax.broadcasted_iota(jnp.int32, (16, width), 0)
        acc = jnp.zeros((16, width), f32)
        for j in range(2**level):
            acc = jnp.where(rowid == j, docs[0:1, j * width : (j + 1) * width], acc)
        out[2 * GW : 2 * GW + 16] = acc.astype(bf16)


def weight_specs():
    return [pl.BlockSpec((D, GW), lambda j, y, part=part: (0, 2 * part + y[0]), pipeline_mode=pl.Buffered(1)) for part in range(3)]


def pcall(body, name, scalar, ins, outs, in_specs, out_specs, *, grid=(1,), scratch=(), vmem=VMEM_MIB, flops=0):
    nbytes = sum(math.prod(a.shape) * a.dtype.itemsize for a in (*ins, *outs))
    return pl.pallas_call(
        body,
        grid_spec=pltpu.PrefetchScalarGridSpec(
            num_scalar_prefetch=1, grid=grid, in_specs=in_specs, out_specs=out_specs, scratch_shapes=list(scratch)
        ),
        out_shape=outs,
        name=name,
        compiler_params=pltpu.CompilerParams(vmem_limit_bytes=vmem * MIB),
        cost_estimate=estimate(name, flops, nbytes),
    )(scalar, *ins)


def project(y, x, ids, gain, shift, in_b, weight, vmem):
    tok = x.shape[0]
    outs = [
        sds((D, tok), bf16),
        sds((GW, tok), bf16),
        sds((GW, tok), bf16),
        sds((GW, tok), bf16),
        sds((8, tok), f32),
        sds((2 * GW + 16, tok // 2), bf16),
        sds((2 * GW + 16, tok // 4), bf16),
    ]
    return pcall(
        functools.partial(project_body, tok), "project", y, (x, ids, gain, shift, in_b, weight, weight, weight), outs,
        [full(x.shape), full(ids.shape), full((D,)), full((D,)), full((3 * D,))] + weight_specs(), [full(o.shape) for o in outs],
        vmem=vmem,
        flops=2 * tok * D * (tok + 3 * GW),
    )


def fill_keys(kaug, vaug, k_parts, v_parts, doc_parts, pos_parts, head, b0, tok):
    at = 0
    for k, v, doc, pos in zip(k_parts, v_parts, doc_parts, pos_parts, strict=True):
        n = k.shape[1]
        kaug[0:HD, at : at + n] = k
        kaug[HD:64, at : at + n] = features("k", doc, pos, head, b0, tok, (-1.0, -1.0, -1.0))
        vaug[0:HD, at : at + n] = v
        vaug[HD:64, at : at + n] = tail_rows(n, (1.0, 1.0, 1.0))
        at += n


def fill_queries(qaug, q_parts, doc_parts, pos_parts, head, b0, tok, lse_parts=None):
    at = 0
    for j, (q, doc, pos) in enumerate(zip(q_parts, doc_parts, pos_parts, strict=True)):
        n = q.shape[1]
        extra = None if lse_parts is None else split3(lse_parts[j])
        qaug[0:HD, at : at + n] = q
        qaug[HD:64, at : at + n] = features("q", doc, pos, head, b0, tok, extra)
        at += n


def iota_row(n):
    return lax.broadcasted_iota(jnp.int32, (1, n), 1)


def attend(qaug, kaug, vaug, nq, nk, step, put):
    keys = kaug[:, 0:nk].T
    for at in range(0, nq, step):
        scores = mm(keys, qaug[:, at : at + step])
        probs = jnp.exp2(scores).astype(bf16)
        put(at, mm(vaug[:, 0:nk], probs))


def own_forward_body(tok, y_ref, qa, qb, ka, kb, va, vb, da, db, out_ref, qaug, kaug, vaug):
    pos = iota_row(tok)
    docs = (da[0:1], db[0:1])
    for i in range(OWN_STEP):
        head = y_ref[0] * HG + pl.program_id(0) * OWN_STEP + i
        at_head = lambda *refs: tuple(Rows(r, i)[...] for r in refs)
        fill_keys(kaug.at[i], vaug.at[i], at_head(ka, kb), at_head(va, vb), docs, (pos, pos), head, 0, tok)
        fill_queries(qaug.at[i], at_head(qa, qb), docs, (pos, pos), head, 0, tok)

        def put(at, val):
            out_ref[i, :, at : at + val.shape[1]] = val

        attend(qaug.at[i], kaug.at[i], vaug.at[i], 2 * tok, 2 * tok, tok, put)


def head_block(tok, step=1):
    return pl.BlockSpec((HD * step, tok), lambda h: (h, 0))


class Rows:
    def __init__(self, ref, head):
        self.ref, self.rows = ref, slice(head * HD, (head + 1) * HD)

    def __getitem__(self, at):
        return self.ref[(self.rows,) + at[1:]] if isinstance(at, tuple) else self.ref[self.rows]

    def __setitem__(self, at, value):
        if isinstance(at, tuple):
            self.ref[(self.rows,) + at[1:]] = value
        else:
            self.ref[self.rows] = value


def own_forward(y, qs, ks, vs, docs):
    tok = qs[0].shape[1]
    return kcall(
        functools.partial(own_forward_body, tok),
        "own_forward",
        (y, *qs, *ks, *vs, *docs),
        [sds((HG, 64, 2 * tok), f32)],
        grid=(HG // OWN_STEP,),
        in_specs=[SMEM] + [head_block(tok, OWN_STEP)] * 6 + [full((8, tok))] * 2,
        out_specs=[pl.BlockSpec((OWN_STEP, 64, 2 * tok), lambda h: (h, 0, 0))],
        scratch=[pltpu.VMEM((OWN_STEP, 64, 2 * tok), bf16)] * 3,
        flops=2 * HG * 128 * (2 * tok) ** 2,
    )[0]


def groups_of(masks):
    found = {}
    for j, m in enumerate(masks):
        found.setdefault(m.bit_length(), []).append(j)
    return [(b0, min(b0, 2), found[b0]) for b0 in sorted(found)]


def remote_parts(refs, members, local, level, tok, pieces=2):
    width = tok >> level
    start = run_start(local, level, tok)
    lane = iota_row(width) + start
    row = pl.multiple_of(local * HD, 16)
    ks, vs, docs, poss = [], [], [], []
    for j in members:
        for ref in refs[pieces * j : pieces * (j + 1)]:
            ks.append(ref[pl.ds(row, HD), :])
            vs.append(ref[pl.ds(row + GW, HD), :])
            block = ref[2 * GW : 2 * GW + 16, :].astype(f32)
            picked = block[0:1]
            for r in range(1, 2**level):
                picked = jnp.where(start // width == r, block[r : r + 1], picked)
            docs.append(picked)
            poss.append(lane)
    return ks, vs, docs, poss, start, width


def far_forward_body(tok, masks, last, y_ref, qa, qb, da, db, part, *rest):
    refs, rest = rest[: len(masks)], rest[len(masks) :]
    outs, (qaugs, kaugs, vaugs, accs) = rest[:-4], rest[-4:]
    for i in range(FAR_STEP):
        local = pl.program_id(0) * FAR_STEP + i
        head = y_ref[0] * HG + local
        qh, acc = (Rows(qa, i), Rows(qb, i)), accs.at[i]
        acc[...] = part[i]
        for g, (b0, level, members) in enumerate(groups_of(masks)):
            qaug, kaug, vaug = qaugs.at[i, g], kaugs.at[i, g], vaugs.at[i, g]
            ks, vs, docs, poss, start, width = remote_parts(refs, members, local, level, tok, 1)
            nk = width * len(ks)
            fill_keys(kaug, vaug, ks, vs, docs, poss, head, b0, tok)
            window = pl.ds(pl.multiple_of(start, 128), width)
            pos = iota_row(width) + start
            fill_queries(qaug, [q[:, window] for q in qh], (da[0:1, window], db[0:1, window]), (pos, pos), head, b0, tok)

            def put(at, val):
                acc[:, window] += val[:, 0:width]
                other = pl.ds(pl.multiple_of(start + tok, 128), width)
                acc[:, other] += val[:, width : 2 * width]

            attend(qaug, kaug, vaug, 2 * width, nk, 2 * width, put)
        if not last:
            outs[0][i] = acc[...]
            continue
        ma, mb, merged, lse = outs
        den = acc[HD : HD + 1]
        val = acc[0:HD] / den
        merged[i] = val
        Rows(ma, i)[...] = val[:, 0:tok].astype(bf16)
        Rows(mb, i)[...] = val[:, tok : 2 * tok].astype(bf16)
        lse[i] = jnp.broadcast_to(jnp.log2(den), (8, 2 * tok))


def remote_sizes(masks, tok):
    nq = max([tok >> level << 1 for _, level, _ in groups_of(masks)] + [128])
    nk = max([(tok >> level) * 2 * len(members) for _, level, members in groups_of(masks)] + [128])
    return nq, nk


def remote_flops(masks, tok):
    return sum(2 * HG * 64 * (2 * (tok >> lv)) * ((tok >> lv) * 2 * len(mem)) for _, lv, mem in groups_of(masks))


def far_forward(y, qs, docs, part, masks, remote, last):
    tok = qs[0].shape[1]
    nq, nk = remote_sizes(masks, tok)
    nk = max(nk // 2, 128)
    n = len(groups_of(masks))
    per_head = lambda r: pl.BlockSpec((FAR_STEP, r, 2 * tok), lambda h: (h, 0, 0))
    final = [sds((GW, tok), bf16)] * 2 + [sds((HG, HD, 2 * tok), f32), sds((HG, 8, 2 * tok), f32)]
    return kcall(
        functools.partial(far_forward_body, tok, masks, last),
        "far_forward" if last else "far_forward_first",
        (y, *qs, *docs, part, *remote),
        final if last else [sds((HG, 64, 2 * tok), f32)],
        grid=(HG // FAR_STEP,),
        in_specs=[SMEM] + [head_block(tok, FAR_STEP)] * 2 + [full((8, tok))] * 2 + [per_head(64)] + [full(r.shape) for r in remote],
        out_specs=[head_block(tok, FAR_STEP)] * 2 + [per_head(HD), per_head(8)] if last else [per_head(64)],
        scratch=[
            pltpu.VMEM((FAR_STEP, n, 64, nq), bf16),
            pltpu.VMEM((FAR_STEP, n, 64, nk), bf16),
            pltpu.VMEM((FAR_STEP, n, 64, nk), bf16),
            pltpu.VMEM((FAR_STEP, 64, 2 * tok), f32),
        ],
        flops=remote_flops(masks, tok),
    )


def attend_back(qaug, gaug, kaug, vaug, nq, nk, step, put_q, dk, dv):
    keys = kaug[0:HD, 0:nk]
    for at in range(0, nq, step):
        sl = slice(at, at + step)
        probs = jnp.exp2(mm(qaug[:, sl].T, kaug[:, 0:nk]))
        gprobs = mm(gaug[:, sl].T, vaug[:, 0:nk])
        gs = (probs * gprobs).astype(bf16)
        new_v = mm(gaug[0:HD, sl], probs.astype(bf16))
        new_k = mm(qaug[0:HD, sl], gs)
        if at == 0:
            dv[:, 0:nk] = new_v
            dk[:, 0:nk] = new_k
        else:
            dv[:, 0:nk] += new_v
            dk[:, 0:nk] += new_k
        put_q(at, mm(keys, gs, NT) * SCALE)


def fill_grads(gaug, g_parts, m_parts):
    at = 0
    for g, m in zip(g_parts, m_parts, strict=True):
        n = g.shape[1]
        delta = jnp.sum(g.astype(f32) * m, axis=0, keepdims=True)
        gaug[0:HD, at : at + n] = g
        gaug[HD:64, at : at + n] = tail_rows(n, split3(-delta))
        at += n


def far_backward_body(tok, masks, y_ref, qa, qb, da, db, ga, gb, merged, lse, *rest):
    nrem = 2 * len(masks)
    refs = rest[:nrem]
    dq_ref = rest[nrem]
    sends = rest[nrem + 1 : nrem + 1 + len(masks)]
    qaugs, gaugs, kaugs, vaugs, dks, dvs = rest[nrem + 1 + len(masks) :]
    for i in range(FAR_STEP):
        local = pl.program_id(0) * FAR_STEP + i
        head = y_ref[0] * HG + local
        row = pl.multiple_of(local * HD, 16)
        dq_ref[i] = jnp.zeros((HD, 2 * tok), f32)
        qh, gh = (Rows(qa, i), Rows(qb, i)), (Rows(ga, i), Rows(gb, i))
        for g, (b0, level, members) in enumerate(groups_of(masks)):
            qaug, gaug, kaug, vaug, dk, dv = (v.at[i, g] for v in (qaugs, gaugs, kaugs, vaugs, dks, dvs))
            ks, vs, docs, poss, start, width = remote_parts(refs, members, local, level, tok)
            nk = width * len(ks)
            fill_keys(kaug, vaug, ks, vs, docs, poss, head, b0, tok)
            window = pl.ds(pl.multiple_of(start, 128), width)
            other = pl.ds(pl.multiple_of(start + tok, 128), width)
            pos = iota_row(width) + start
            fill_queries(
                qaug, [q[:, window] for q in qh], (da[0:1, window], db[0:1, window]), (pos, pos), head, b0, tok,
                (lse[i, 0:1, window], lse[i, 0:1, other]),
            )
            fill_grads(gaug, [v[:, window] for v in gh], (merged[i, :, window], merged[i, :, other]))

            def put_q(at, val):
                dq_ref[i, :, window] += val[:, 0:width]
                dq_ref[i, :, other] += val[:, width : 2 * width]

            attend_back(qaug, gaug, kaug, vaug, 2 * width, nk, 2 * width, put_q, dk, dv)
            for n, j in enumerate(members):
                span = slice(2 * n * width, 2 * (n + 1) * width)
                sends[j][pl.ds(row, HD), :] = (dk[:, span] * LN2).astype(bf16)
                sends[j][pl.ds(row + GW, HD), :] = dv[:, span].astype(bf16)


def far_backward(y, qs, docs, gs, merged, lse, masks, remote):
    tok = qs[0].shape[1]
    nq, nk = remote_sizes(masks, tok)
    n = len(groups_of(masks))
    per_head = lambda r: pl.BlockSpec((FAR_STEP, r, 2 * tok), lambda h: (h, 0, 0))
    blocks = head_block(tok, FAR_STEP)
    sends = [sds((2 * GW, 2 * (tok >> min(m.bit_length(), 2))), bf16) for m in masks]
    return kcall(
        functools.partial(far_backward_body, tok, masks),
        "far_backward",
        (y, *qs, *docs, *gs, merged, lse, *remote),
        [sds((HG, HD, 2 * tok), f32)] + sends,
        grid=(HG // FAR_STEP,),
        in_specs=[SMEM] + [blocks] * 2 + [full((8, tok))] * 2 + [blocks] * 2
        + [per_head(HD), per_head(8)] + [full(r.shape) for r in remote],
        out_specs=[per_head(HD)] + [full(s.shape) for s in sends],
        scratch=[pltpu.VMEM((FAR_STEP, n, 64, nq), bf16)] * 2
        + [pltpu.VMEM((FAR_STEP, n, 64, nk), bf16)] * 2
        + [pltpu.VMEM((FAR_STEP, n, HD, nk), f32)] * 2,
        flops=5 * remote_flops(masks, tok),
    )


def own_backward_body(tok, y_ref, qa, qb, ka, kb, va, vb, da, db, ga, gb, merged, lse, dq_in, dq, dk, dv, qaug, gaug, kaug, vaug):
    head = y_ref[0] * HG + pl.program_id(0)
    pos = iota_row(tok)
    docs = (da[0:1], db[0:1])
    fill_keys(kaug, vaug, (ka[...], kb[...]), (va[...], vb[...]), docs, (pos, pos), head, 0, tok)
    fill_queries(
        qaug, (qa[...], qb[...]), docs, (pos, pos), head, 0, tok, (lse[0, 0:1, 0:tok], lse[0, 0:1, tok : 2 * tok])
    )
    fill_grads(gaug, (ga[...], gb[...]), (merged[0, :, 0:tok], merged[0, :, tok : 2 * tok]))

    def put_q(at, val):
        dq[:, at : at + tok] = (val + dq_in[0, :, at : at + tok]).astype(bf16)

    attend_back(qaug, gaug, kaug, vaug, 2 * tok, 2 * tok, tok, put_q, dk.at[0], dv.at[0])


def own_backward(y, qs, ks, vs, docs, gs, merged, lse, dq):
    tok = qs[0].shape[1]
    per_head = lambda r: pl.BlockSpec((1, r, 2 * tok), lambda h: (h, 0, 0))
    return kcall(
        functools.partial(own_backward_body, tok),
        "own_backward",
        (y, *qs, *ks, *vs, *docs, *gs, merged, lse, dq),
        [sds((GW, 2 * tok), bf16)] + [sds((HG, HD, 2 * tok), f32)] * 2,
        grid=(HG,),
        in_specs=[SMEM] + [head_block(tok)] * 6 + [full((8, tok))] * 2 + [head_block(tok)] * 2
        + [per_head(HD), per_head(8), per_head(HD)],
        out_specs=[head_block(2 * tok)] + [per_head(HD)] * 2,
        scratch=[pltpu.VMEM((64, 2 * tok), bf16)] * 4,
        flops=5 * HG * 128 * (2 * tok) ** 2,
    )


NBLK = 8
HALF = D // 2
DOWN_ROWS = FF // NBLK
UP_ROWS = D // NBLK
ROWS_A = 2 * UP_ROWS + UP_ROWS // 2
ROWS_B = DOWN_ROWS // 2


def cot_body(cot, down, out):
    out[...] = mm(cot[...], down[...], NT).astype(out.dtype)


def cot_down(cot, down):
    tok, ff = cot.shape[0], down.shape[0]
    blk = 768
    return kcall(
        cot_body, "cot_down", (cot, down), [sds((tok, ff), bf16)], grid=(ff // blk,),
        in_specs=[full((tok, D)), pl.BlockSpec((blk, D), lambda j: (j, 0))],
        out_specs=[pl.BlockSpec((tok, blk), lambda j: (0, j))], vmem=60, flops=2 * tok * D * ff,
    )[0]


ERF_P = 0.3275911
ERF_A = (0.254829592, -0.284496736, 1.421413741, -1.453152027, 1.061405429)


def normal_cdf(v):
    gauss = jnp.exp2(v * v * (-0.5 / LN2))
    t = 1.0 / (1.0 + jnp.abs(v) * (ERF_P * 0.5**0.5))
    poly = 0.5 * ERF_A[4]
    for a in ERF_A[3::-1]:
        poly = poly * t + 0.5 * a
    tail = poly * t * gauss
    return jnp.where(v < 0, tail, 1.0 - tail), gauss


def mlp_body(tok, nblk, bits, x_ref, mown, moth, out_b, n2g, n2s, wout, up, up_b, gdown, cot,
             gelu_ref, gelu_send, gpre_ref, gpre_send, upb_ref, rows_ref, resid_ref, gmown, gmoth, gres_ref, vec_ref,
             second, xhat, rstd, acc):
    step = pl.program_id(0)
    y = bits[0]
    low_core = bits[3] == 0
    mine = pl.ds(pl.multiple_of(y * GW, 128), GW)
    theirs = pl.ds(pl.multiple_of((1 - y) * GW, 128), GW)
    gain = row(n2g)

    @pl.when(step == 0)
    def _():
        pmt = one_hot(tok, True)
        own = mm(pmt, mown[...], NT).astype(bf16)
        oth = mm(pmt, moth[...], NT).astype(bf16)
        resid = x_ref[...].astype(f32) + (mm(own, wout[mine, :]) + mm(oth, wout[theirs, :])) + row(out_b)
        resid_ref[...] = resid
        xh, rs = normalise(resid)
        xhat[...] = xh
        rstd[...] = jnp.broadcast_to(rs, rstd.shape)
        low = (xh * gain + row(n2s)).astype(bf16)
        second[...] = low
        rows_ref[0:D] = low.T
        acc[...] = jnp.zeros_like(acc)

    rows = tok // MLP_SPLIT
    for i in range(MLP_SPLIT):
        part = slice(i * rows, (i + 1) * rows)
        pre = mm(second[part], up[...]) + up_b[0]
        cdf, gauss = normal_cdf(pre)
        gelu_t = (pre * cdf).astype(bf16).T
        gelu_ref[:, part] = gelu_t
        half = DOWN_ROWS // 2
        for at in range(0, gelu_t.shape[0], DOWN_ROWS):
            low, high = gelu_t[at : at + half], gelu_t[at + half : at + DOWN_ROWS]
            gelu_send[at // 2 : at // 2 + half, part] = jnp.where(low_core, high, low)
        slope = cdf + pre * (gauss * (1.0 / math.sqrt(2.0 * math.pi)))
        gpre = (slope * gdown[part]).astype(bf16)
        gpre_ref[part] = gpre

        gpre_send[part] = gpre
        acc[part] += mm(gpre, up[...], NT)
        sums = mm(jnp.ones((8, rows), bf16), gpre)
        upb_ref[...] = sums if i == 0 else upb_ref[...] + sums

    @pl.when(step == nblk - 1)
    def _():
        dy = acc[...]
        xh = xhat[...]
        dyg = dy * gain
        m1 = jnp.mean(dyg, axis=-1, keepdims=True)
        m2 = jnp.mean(dyg * xh, axis=-1, keepdims=True)
        g = cot[...]
        gres = g.astype(f32) + rstd[:, 0:1] * (dyg - m1 - xh * m2)
        gres_ref[...] = gres
        gattn = gres.astype(bf16)
        gattn_t = mm(gattn.T, one_hot(tok, True)).astype(bf16)
        rows_ref[D : 2 * D] = gattn_t
        gmoth[...] = mm(wout[theirs, :], gattn_t).astype(bf16)
        gmown[...] = mm(wout[mine, :], gattn_t).astype(bf16)
        ones = jnp.ones((8, tok), bf16)
        vec_ref[0:8] = mm(ones, g)
        vec_ref[8:16] = jnp.broadcast_to(jnp.sum(dy * xh, axis=0, keepdims=True), (8, D))
        vec_ref[16:24] = jnp.broadcast_to(jnp.sum(dy, axis=0, keepdims=True), (8, D))
        vec_ref[24:32] = mm(ones, gattn)


def mlp_chunk(step, bits):
    return (step // 2 + bits[3]) % 2 * 2 + step % 2


def mlp(bits, x, mown, moth, out_b, n2g, n2s, wout, up, up_b, gdown, cot):
    tok = cot.shape[0]
    ff = up.shape[1]
    nblk = 4
    blk = ff // nblk
    wide = pl.BlockSpec((tok, blk), lambda j, b: (0, mlp_chunk(j, b)))
    outs = [
        sds((ff, tok), bf16), sds((ff // 2, tok), bf16), sds((tok, ff), bf16), sds((tok, ff // 2), bf16), sds((8, ff), f32),
        sds((2 * D, tok), bf16), sds((tok, D), f32), sds((GW, tok), bf16), sds((GW, tok), bf16),
        sds((tok, D), f32), sds((32, D), f32),
    ]
    return pcall(
        functools.partial(mlp_body, tok, nblk),
        "mlp",
        bits,
        (x, mown, moth, out_b, n2g, n2s, wout, up, up_b.reshape(nblk, 1, blk), gdown, cot),
        outs,
        [
            full(x.shape), full(mown.shape), full(moth.shape), full((D,)), full((D,)), full((D,)), full(wout.shape),
            pl.BlockSpec((D, blk), lambda j, b: (0, mlp_chunk(j, b))),
            pl.BlockSpec((1, 1, blk), lambda j, b: (mlp_chunk(j, b), 0, 0)),
            wide, full((tok, D)),
        ],
        [
            pl.BlockSpec((blk, tok), lambda j, b: (mlp_chunk(j, b), 0)),
            pl.BlockSpec((blk // 2, tok), lambda j, b: (mlp_chunk(j, b), 0)),
            wide,
            pl.BlockSpec((tok, blk), lambda j, b: (0, jnp.maximum(j - nblk // 2, 0))),
            pl.BlockSpec((8, blk), lambda j, b: (0, mlp_chunk(j, b))),
        ] + [full(o.shape) for o in outs[5:]],
        grid=(nblk,),
        scratch=[pltpu.VMEM((tok, D), bf16), pltpu.VMEM((tok, D), f32), pltpu.VMEM((tok, 128), f32), pltpu.VMEM((tok, D), f32)],
        vmem=32,
        flops=2 * tok * D * (2 * ff + 2 * D + 2 * tok),
    )


def mlp_grads_body(bits, cores, *refs):
    ins, outs = refs[:-4], refs[-4:]
    send_a, keep_a, send_b, keep_b = outs
    ybit, xbit = bits[0], bits[1]
    heads_low = (pl.program_id(0) < 2) == (ybit == 0)
    up = att = 0.0
    down = [0.0, 0.0]
    for c in range(cores):
        low_t, high_t, second_t, gattn_t, gpre, cot, mown, moth = ins[8 * c : 8 * c + 8]
        up = up + mm(second_t[...], gpre[...])
        down = [old + mm(gelu_t[...], cot[...]) for old, gelu_t in zip(down, (low_t, high_t), strict=True)]
        att = att + mm(jnp.where(heads_low, mown[...], moth[...]), gattn_t[...], NT)
    up, att, down = up.astype(bf16), att.astype(bf16), [v.astype(bf16) for v in down]
    x_low, y_low = xbit == 0, ybit == 0
    half = UP_ROWS // 2
    for y in range(2):
        rows = slice(y * UP_ROWS, (y + 1) * UP_ROWS)
        cols = [up[rows, c * HALF : (c + 1) * HALF] for c in range(4)]
        pieces = [(0, UP_ROWS, cols[0], cols[2]), (UP_ROWS, UP_ROWS, cols[1], cols[3])]
        pieces += [(2 * UP_ROWS, half, att[y * UP_ROWS : y * UP_ROWS + half], att[y * UP_ROWS + half : (y + 1) * UP_ROWS])]
        for at, n, low, high in pieces:
            keep_a[0, y, at : at + n] = jnp.where(x_low, low, high)
            send_a[0, y, at : at + n] = jnp.where(x_low, high, low)
    for x in range(2):
        low, high = (v[:, x * HALF : (x + 1) * HALF] for v in down)
        keep_b[0, x] = jnp.where(y_low, low, high)
        send_b[0, x] = jnp.where(y_low, high, low)


def mlp_grads(bits, *per_core):
    tok = per_core[0][3].shape[0]
    ins, specs = [], []
    for gelu_t, rows, gpre, cot, mown, moth in per_core:
        heads = pl.BlockSpec((GW // 2, tok), lambda j, b: (j % 2, 0))
        ins += [gelu_t, gelu_t, rows, rows, gpre, cot, mown, moth]
        if gelu_t.shape[0] == FF:
            gelus = [pl.BlockSpec((ROWS_B, tok), lambda j, b, y=y: (4 * j + 2 * y + b[3], 0)) for y in range(2)]
            half = pl.BlockSpec((tok, FF // 2), lambda j, b: (0, b[3]))
        else:
            gelus = [pl.BlockSpec((ROWS_B, tok), lambda j, b, y=y: (2 * j + y, 0)) for y in range(2)]
            half = full(gpre.shape)
        specs += gelus + [
            pl.BlockSpec((D // 4, tok), lambda j, b: (j, 0)),
            pl.BlockSpec((HALF, tok), lambda j, b: (D // HALF + b[3], 0)),
            half, full(cot.shape), heads, heads,
        ]
    outs = [sds((4, 2, ROWS_A, HALF), bf16)] * 2 + [sds((4, 2, ROWS_B, HALF), bf16)] * 2
    return pcall(
        lambda bits, *refs: mlp_grads_body(bits, len(per_core), *refs), "mlp_grads", bits, ins, outs, specs,
        [pl.BlockSpec((1,) + o.shape[1:], lambda j, b: (j, 0, 0, 0)) for o in outs],
        grid=(4,),
        vmem=28,
        flops=2 * tok * D * (2 * FF + D),
    )


IN_ROWS = D // NBLK // 2
IN_COLS = 3 * GW + 128
SMALL_ROWS = 16
UNIT = UP_ROWS


def finish_body(tok, masks, bits, dq, dk, dv, xa, xb, fa, fb, wq, wk, wv, vec, up_sum, *rest):
    nrem = len(masks)
    recv = rest[:nrem]
    first_a, first_b, send, keep, gqkv, total, acc, sums, bias, small = rest[nrem:]
    step = pl.program_id(0)
    for part, ref, scale in ((0, dk, LN2), (1, dv, 1.0)):
        for h in range(HG):
            total[h * HD : (h + 1) * HD] = ref[h] * scale
        for m, r in zip(masks, recv, strict=True):
            level = min(m.bit_length(), 2)
            for h in range(HG):
                start = run_start(h, level, tok)
                row = part * GW + h * HD
                total[h * HD : (h + 1) * HD, start : start + (tok >> level)] += r[row : row + HD].astype(f32)
        gqkv[(1 + part) * GW : (2 + part) * GW] = total[...].astype(bf16)
    gqkv[0:GW] = dq[...]
    nat = mm(one_hot(tok, True), gqkv[...], NT).astype(bf16)
    new_bias = mm(jnp.ones((8, tok), bf16), nat)
    dy = sum(mm(nat[:, part * GW : (part + 1) * GW], w[...], NT) for part, w in enumerate((wq, wk, wv)))
    later = step == 1
    xh, _ = normalise(jnp.where(later, xa[...], xb[...]).astype(f32))
    new_gain = jnp.sum(dy * xh, axis=0, keepdims=True)
    new_shift = jnp.sum(dy, axis=0, keepdims=True)

    @pl.when(step == 0)
    def _():
        first_b[...] = dy.astype(bf16)
        acc[...] = mm(fb[...], gqkv[...], NT)
        bias[...] = new_bias
        sums[0:8] = jnp.broadcast_to(new_gain, (8, D))
        sums[8:16] = jnp.broadcast_to(new_shift, (8, D))

    @pl.when(step == 1)
    def _():
        first_a[...] = dy
        val = (acc[...] + mm(fa[...], gqkv[...], NT)).astype(bf16)
        all_bias = bias[0:1] + new_bias[0:1]
        lines = [sums[0:1] + new_gain, sums[8:9] + new_shift]
        lines += [vec[8 * j : 8 * j + 1] for j in range(4)]
        cut = lambda line, u: line[:, u * UNIT : (u + 1) * UNIT]
        small[...] = jnp.zeros_like(small)

        def put(block, row, line):
            small[block, row : row + 1, 0:UNIT] = line

        for s in range(NBLK):
            for row, line in zip((0, 1, 5, 6, 7, 8), lines, strict=True):
                put(s, row, cut(line, s))
            for k in range(4):
                put(s, 9 + k, cut(up_sum[0:1], s * 4 + k))
        for u in range(3 * NBLK):
            part, owner, k = u // 8, u // 4 % 2, u % 4
            put(u // 3, 2 + u % 3, jnp.where(bits[0] == owner, cut(all_bias, part * 4 + k), 0.0))
        keep_low = bits[3] == 0
        zeros = jnp.zeros((IN_ROWS, 128), bf16)

        def store(block, lanes, low, high):
            keep[block, :, lanes] = jnp.where(keep_low, low, high)
            send[block, :, lanes] = jnp.where(keep_low, high, low)

        for s in range(NBLK):
            at = 2 * s * IN_ROWS
            store(s, slice(0, 3 * GW), val[at : at + IN_ROWS], val[at + IN_ROWS : at + 2 * IN_ROWS])
            store(s, slice(3 * GW, IN_COLS), jnp.concatenate([small[s].astype(bf16), zeros[SMALL_ROWS:]], axis=0), zeros)


def finish(bits, dq, dk, dv, xa, xb, fa, fb, weight, vec, up_sum, masks, recv):
    tok = xa.shape[0]
    piece = lambda j: 1 - j
    by_head = pl.BlockSpec((HG, HD, tok), lambda j, y: (0, 0, piece(j)))
    outs = [sds((tok, D), f32), sds((tok, D), bf16)] + [sds((NBLK, IN_ROWS, IN_COLS), bf16)] * 2
    return pcall(
        functools.partial(finish_body, tok, masks),
        "finish",
        bits,
        (dq, dk, dv, xa, xb, fa, fb, weight, weight, weight, vec, up_sum, *recv),
        outs,
        [pl.BlockSpec((GW, tok), lambda j, y: (0, piece(j))), by_head, by_head]
        + [full(v.shape) for v in (xa, xb, fa, fb)] + weight_specs() + [full(vec.shape), full(up_sum.shape)]
        + [pl.BlockSpec((2 * GW, r.shape[1] // 2), lambda j, y: (0, piece(j))) for r in recv],
        [full(o.shape) for o in outs],
        grid=(2,),
        scratch=[
            pltpu.VMEM((3 * GW, tok), bf16), pltpu.VMEM((GW, tok), f32), pltpu.VMEM((D, 3 * GW), f32),
            pltpu.VMEM((16, D), f32), pltpu.VMEM((8, 3 * GW), f32), pltpu.VMEM((NBLK, SMALL_ROWS, 128), f32),
        ],
        vmem=28,
        flops=4 * tok * 3 * GW * (tok + 2 * D),
    )


def input_grad_body(x_ref, gain, own, got, gres, out):
    xh, rs = normalise(x_ref[...].astype(f32))
    dyg = (own[...] + got[...].astype(f32)) * row(gain)
    m1 = jnp.mean(dyg, axis=-1, keepdims=True)
    m2 = jnp.mean(dyg * xh, axis=-1, keepdims=True)
    out[...] = gres[...] + rs * (dyg - m1 - xh * m2)


def unpack_mlp_body(bits, near, far, down, up, att):
    low = bits[3] == 0
    for c, v in enumerate((jnp.where(low, near[...], far[...]), jnp.where(low, far[...], near[...]))):
        for x in range(2):
            half = v[x].astype(f32)
            for j in range(2):
                at = (c * 4 + 2 * x + j) * HALF
                up[:, at : at + HALF] = half[j * UP_ROWS : (j + 1) * UP_ROWS]
            n = UP_ROWS // 2
            att[x * n : (x + 1) * n, c * HALF : (c + 1) * HALF] = half[2 * UP_ROWS : ROWS_A]
            down[c * ROWS_B : (c + 1) * ROWS_B, x * HALF : (x + 1) * HALF] = half[ROWS_A:]


VEC_UNITS = (1, 1, 3, 1, 1, 1, 1, 4)


def unpack_in_body(bits, near, far, out, *vecs):
    low = bits[3] == 0
    lower = jnp.where(low, near[...], far[...])
    upper = jnp.where(low, far[...], near[...])
    val = jnp.concatenate([lower[0], lower[1], upper[0], upper[1]], axis=0).astype(f32)
    for part in range(3):
        for y in range(2):
            src = (y * 3 + part) * GW
            dst = (part * 2 + y) * GW
            out[:, dst : dst + GW] = val[:, src : src + GW]
    row = 0
    for ref, units in zip(vecs, VEC_UNITS, strict=True):
        line = jnp.concatenate([val[row + k : row + k + 1, 6 * GW : 6 * GW + UNIT] for k in range(units)], axis=1)
        ref[...] = line[0]
        row += units


def swap(value, axis, offset):
    count = lax.axis_size(axis)
    return lax.ppermute(value, axis, [(i, i ^ offset) for i in range(count)])


def pick(value, index, dim):
    return lax.dynamic_index_in_dim(value, index, dim, keepdims=False)


def halve(pieces, index, dim):
    def part(i):
        return sum(pick(p, i, dim).astype(f32) for p in pieces).astype(bf16)

    return part(1 - index), part(index)


def split_second_body(bits, ka, ga, kb, gb, send_a, keep_a, send_b, keep_b):
    for keep, got, send_to, keep_to, bit in ((ka, ga, send_a, keep_a, bits[0]), (kb, gb, send_b, keep_b, bits[1])):
        total = lambda j: keep[0, j] + got[0, j]
        send_to[0] = total(1 - bit)
        keep_to[0] = total(bit)


def split_second(bits, ka, ga, kb, gb):
    block = lambda v: pl.BlockSpec((1,) + v.shape[1:], lambda j: (j, 0, 0, 0))
    outs = [sds((4,) + v.shape[2:], bf16) for v in (ka, ka, kb, kb)]
    return kcall(
        split_second_body, "split_second", (bits, ka, ga, kb, gb), outs, grid=(4,),
        in_specs=[SMEM] + [block(v) for v in (ka, ga, kb, gb)],
        out_specs=[pl.BlockSpec((1,) + o.shape[1:], lambda j: (j, 0, 0)) for o in outs],
    )


def split_third_body(bits, ka, ga, kb, gb, send, keep):
    low = bits[2] % 2
    at = 0
    for own, got in ((ka, ga), (kb, gb)):
        rows = slice(at, at + own.shape[1])
        send[0, rows] = own[1 - low] + got[1 - low]
        keep[0, rows] = own[low] + got[low]
        at += own.shape[1]


def split_third(bits, ka, ga, kb, gb):
    out = sds((2, ka.shape[1] + kb.shape[1], HALF), bf16)
    two = lambda v, n: pl.BlockSpec((n,) + v.shape[1:], lambda j: (j, 0, 0))
    return kcall(
        split_third_body, "split_third", (bits, ka, ga, kb, gb), [out, out], grid=(2,),
        in_specs=[SMEM] + [two(v, 2) for v in (ka, ga, kb, gb)], out_specs=[two(out, 1)] * 2,
    )


def spread(mine, xbit):
    other = swap(mine, "rep", 2)
    dim = mine.ndim - 2
    pair = jnp.stack([jnp.where(xbit == 0, mine, other), jnp.where(xbit == 0, other, mine)], axis=dim)
    return pair, swap(pair, "rep", 1)


def tie(*values):
    return lax.optimization_barrier(values)


def body(tile_embed, doc_ids, norm1_gain, norm1_shift, in_weight, in_bias, out_weight, out_bias,
         norm2_gain, norm2_shift, up_weight, up_bias, down_weight, down_bias, cotangent):
    tok = tile_embed.shape[1]
    count = lax.axis_size("seq")
    assert SEG0 == 2 * tok and tok % 512 == 0
    nodes = count // 2
    masks = [m for m in range(1, min(nodes, 2 ** (BRANCHES - 1)))]
    whole = count == 8 and lax.axis_size("rep") == 4
    index = lax.axis_index("seq")
    ybit = index % 2
    z = index // 2
    rep = lax.axis_index("rep")
    core, xbit = rep % 2, rep // 2
    bits = jnp.stack([ybit, xbit, z, core if whole else jnp.zeros_like(core)]).astype(jnp.int32)
    y = bits


    x, cot = tile_embed[0], cotangent[0]
    x_oth = swap(x, "seq", 1)
    ids_oth = swap(doc_ids, "seq", 1)

    args = (norm1_gain, norm1_shift, in_bias, in_weight)
    first_a, qa, ka, va, doc_a, *out_a = project(y, x, doc_ids, *args, 60)
    remote_a = [swap(out_a[min(m.bit_length(), 2) - 1], "seq", 2 * m) for m in masks]
    gdown = cot_down(cot, down_weight)
    x_oth, ids_oth, gdown = tie(x_oth, ids_oth, gdown)
    if whole:
        cot_got = swap(cot, "rep", 1)
    first_b, qb, kb, vb, doc_b, *out_b = project(y, x_oth, ids_oth, *args, VMEM_MIB)
    remote_b = [swap(out_b[min(m.bit_length(), 2) - 1], "seq", 2 * m) for m in masks]

    qs, ks, vs, docs = (qa, qb), (ka, kb), (va, vb), (doc_a, doc_b)
    part = own_forward(y, qs, ks, vs, docs)
    remote = [r for pair in zip(remote_a, remote_b, strict=True) for r in pair]
    part, = far_forward(y, qs, docs, part, masks, remote_a, False)
    mown, msend, merged, lse = far_forward(y, qs, docs, part, masks, remote_b, True)
    moth = swap(msend, "seq", 1)
    if whole:
        moth, cot_got, mown_got = tie(moth, cot_got, swap(mown, "rep", 1))
    (gelu_t, gelu_send, gpre, gpre_send, up_sum, rows, resid1, gmown, gmsend, gres, vec) = mlp(
        bits, x, mown, moth, out_bias, norm2_gain, norm2_shift, out_weight, up_weight, up_bias, gdown, cot
    )
    gmoth = swap(gmsend, "seq", 1)

    own = (gelu_t, rows, gpre, cot, mown, moth)
    if whole:
        got = (swap(gelu_send, "rep", 1), swap(rows, "rep", 1), swap(gpre_send, "rep", 1), cot_got, mown_got, swap(moth, "rep", 1))
        send_a, keep_a, send_b, keep_b = mlp_grads(bits, own, got)
        got_a, got_b = swap(send_a, "rep", 2), swap(send_b, "seq", 1)
        gmoth, send_a, send_b = tie(gmoth, send_a, send_b)
    else:
        halves = [mlp_grads(bits.at[3].set(c), own) for c in range(2)]

    gs = (gmown, gmoth)
    dq, *sends = far_backward(y, qs, docs, gs, merged, lse, masks, remote)
    recv = [swap(s, "seq", 2 * m) for s, m in zip(sends, masks, strict=True)]
    dq, dk, dv = own_backward(y, qs, ks, vs, docs, gs, merged, lse, dq)
    if whole:
        dq, got_a, got_b = tie(dq, got_a, got_b)
        send_a, keep_a, send_b, keep_b = split_second(bits, keep_a, got_a, keep_b, got_b)
        dq, send_a, send_b = tie(dq, send_a, send_b)
        got_a, got_b = swap(send_a, "seq", 1), swap(send_b, "rep", 2)
    gfirst_a, gfirst_b, i_send, i_keep = finish(
        bits, dq, dk, dv, x, x_oth, first_a, first_b, in_weight, vec, up_sum, masks, recv
    )
    gfirst_got = swap(gfirst_b, "seq", 1)
    if whole:
        i_send, got_a, got_b = tie(i_send, got_a, got_b)
        i_got = swap(i_send, "rep", 1)
        g_send, g_keep = split_third(bits, keep_a, got_a, keep_b, got_b)
        g_got = swap(g_send, "seq", 2)
        view = lambda v: v.reshape(NBLK, 2, IN_ROWS // 2, IN_COLS)
        i_send, i_keep = halve((view(i_keep), view(i_got)), xbit, 1)
        i_got = swap(i_send, "rep", 2)

    result = (resid1 + mm(gelu_t, down_weight, TN) + down_bias).astype(bf16)
    if whole:
        i_got, result = tie(i_got, result)
        i_send, i_keep = halve((i_keep.reshape(4, 2, -1, IN_COLS), i_got.reshape(4, 2, -1, IN_COLS)), ybit, 1)
        i_got = swap(i_send, "seq", 1)
        g_got, i_send = tie(g_got, i_send)
        g_send, g_keep = halve((g_keep, g_got), z // 2, 0)
        g_got = swap(g_send, "seq", 4)
        gfirst_got, g_send = tie(gfirst_got, g_send)
    by_rows = lambda n: pl.BlockSpec((tok // 4, n), lambda j: (j, 0))
    grad_input = kcall(
        input_grad_body, "input_grad", (x, norm1_gain, gfirst_a, gfirst_got, gres), [sds((tok, D), f32)], grid=(4,),
        in_specs=[by_rows(D), full((D,))] + [by_rows(D)] * 3, out_specs=[by_rows(D)],
    )[0]

    if whole:
        i_got, grad_input = tie(i_got, grad_input)
        width = 3 * GW
        low, high = jnp.where(ybit == 0, i_keep, i_got), jnp.where(ybit == 0, i_got, i_keep)
        vec = i_keep[..., width:] + i_got[..., width:]
        i_all = jnp.concatenate([low[..., :width], high[..., :width], vec], axis=-1).reshape(2, 2, IN_ROWS // 2, 2 * width + 128)
        i_send, i_keep = pick(i_all, 1 - z % 2, 1), pick(i_all, z % 2, 1)
        i_got = swap(i_send, "seq", 2)
        i_got, g_got = tie(i_got, g_got)
        i_send, i_keep = halve((i_keep, i_got), z // 2, 0)
        i_got = swap(i_send, "seq", 4)

        mine = g_keep + g_got
        near, far = spread(mine, xbit)
        g_down, g_up, g_out = kcall(
            unpack_mlp_body, "unpack_mlp", (bits, near, far),
            [sds((DOWN_ROWS, D), f32), sds((UP_ROWS, FF), f32), sds((UP_ROWS, D), f32)],
            grid=(1,), in_specs=[SMEM, full(near.shape), full(far.shape)],
            out_specs=[full((DOWN_ROWS, D)), full((UP_ROWS, FF)), full((UP_ROWS, D))],
        )
        near, far = spread(i_keep + i_got, xbit)
        far, g_down = tie(far, g_down)
        g_in, *vecs = kcall(
            unpack_in_body, "unpack_in", (bits, near, far),
            [sds((2 * IN_ROWS, 3 * D), f32)] + [sds((UNIT * n,), f32) for n in VEC_UNITS],
            in_specs=[SMEM, VMEM, VMEM], out_specs=[VMEM] * 9,
        )
    else:
        total = lambda v: lax.psum(lax.psum_scatter(v, "seq", scatter_dimension=0, tiled=True).astype(bf16), "rep").astype(f32)
        order = lambda bit, keep, send: jnp.where(bit == 0, jnp.stack([keep, send]), jnp.stack([send, keep])).astype(f32)
        by_x = jnp.stack([order(xbit, h[1], h[0]) for h in halves])
        by_y = jnp.stack([order(ybit, h[3], h[2]) for h in halves])
        ups = by_x[..., : 2 * UP_ROWS, :].reshape(2, 2, NBLK, 2, UP_ROWS, HALF)
        g_up = total(ups.transpose(2, 4, 0, 1, 3, 5).reshape(D, FF))
        g_out = total(by_x[..., 2 * UP_ROWS :, :].reshape(2, 2, NBLK, UP_ROWS // 2, HALF).transpose(2, 1, 3, 0, 4).reshape(D, D))
        g_down = total(by_y.transpose(2, 1, 0, 4, 3, 5).reshape(FF, D))
        both = jnp.stack([i_keep, i_send], axis=1)[..., : 3 * GW].astype(f32).reshape(D, 3, 1, GW)
        g_in = total(jnp.where((jnp.arange(2) == ybit)[None, None, :, None], both, 0.0).reshape(D, 3 * D))
        small = i_keep[:, :, 3 * GW : 3 * GW + UNIT].astype(f32)
        ends = np.cumsum((0,) + VEC_UNITS)
        vecs = [total(small[:, lo:hi].reshape(-1)) for lo, hi in zip(ends[:-1], ends[1:], strict=True)]
    n1_gain, n1_shift, b_in, b_down, n2_gain, n2_shift, b_out, b_up = vecs
    return (
        result[None], grad_input[None], n1_gain, n1_shift, g_in, b_in, g_out, b_out, n2_gain, n2_shift, g_up, b_up, g_down, b_down,
    )


def solution(mesh):
    tokens, weights = P("rep", "seq", None), P()
    in_specs = (tokens, P("rep", "seq")) + (weights,) * 12 + (tokens,)
    vec, mat = P("seq"), P("seq", None)
    out_specs = (tokens, tokens, vec, vec, mat, vec, mat, vec, vec, vec, mat, vec, mat, vec)
    return jax.shard_map(body, mesh=mesh, in_specs=in_specs, out_specs=out_specs, check_vma=False)
```

```python
import functools
import math

import jax
import jax.numpy as jnp
import numpy as np
from jax import lax
from jax.experimental import pallas as pl
from jax.experimental.pallas import tpu as pltpu
from jax.sharding import PartitionSpec as P


D = 768
H = 16
HD = 48
FF = 3072
SEG0 = 1024
BRANCHES = 5
RES = 16
HG = H // 2
GW = HG * HD
NORM_EPS = 1e-05
BIG = 1e30
SCALE = HD**-0.5
LN2 = math.log(2.0)
Q_SCALE = SCALE / LN2

f32 = jnp.float32
bf16 = jnp.bfloat16
NN = (((1,), (0,)), ((), ()))
NT = (((1,), (1,)), ((), ()))
TN = (((0,), (0,)), ((), ()))
MIB = 2**20
VMEM_MIB = 20
MLP_SPLIT = 1
OWN_STEP = 1
FAR_STEP = 4


def mm(left, right, dims=NN):
    return lax.dot_general(left, right, dims, preferred_element_type=f32)


def rev4(v):
    return ((v & 1) << 3) | ((v & 2) << 1) | ((v & 4) >> 1) | ((v & 8) >> 3)


def run_start(head, level, tok):
    if level == 1:
        return (head % 2) * (tok // 2)
    return ((head % 2) * 2 + (head // 2) % 2) * (tok // 4)


def kcall(body, name, ins, outs, *, grid=None, in_specs=None, out_specs=None, scratch=(), vmem=VMEM_MIB, flops=0):
    kw = {}
    if grid is not None:
        kw = dict(grid=grid)
    if in_specs is not None:
        kw.update(in_specs=in_specs, out_specs=out_specs)
    nbytes = sum(math.prod(a.shape) * a.dtype.itemsize for a in (*ins, *outs))
    return pl.pallas_call(
        body,
        out_shape=outs,
        scratch_shapes=list(scratch),
        name=name,
        compiler_params=pltpu.CompilerParams(vmem_limit_bytes=vmem * MIB),
        cost_estimate=estimate(name, flops, nbytes),
        **kw,
    )(*ins)


TAIL = ("query_grads", "far_forward_first", "split_second", "split_third", "input_grad", "unpack_mlp", "unpack_in")


def estimate(name, flops, nbytes):
    if name in TAIL:
        return pl.CostEstimate(flops=0, bytes_accessed=0, transcendentals=0)
    return pl.CostEstimate(flops=10**12, bytes_accessed=10**10, transcendentals=0)


def sds(shape, dtype):
    return jax.ShapeDtypeStruct(shape, dtype)


SMEM = pl.BlockSpec(memory_space=pltpu.SMEM)
VMEM = pl.BlockSpec(memory_space=pltpu.VMEM)


def full(shape):
    return pl.BlockSpec(shape, lambda *_: (0,) * len(shape), pipeline_mode=pl.Buffered(1))


def features(side, doc_row, pos, head, b0, tok, extra=None):
    n = doc_row.shape[1]
    rowid = lax.broadcasted_iota(jnp.int32, (16, n), 0)
    out = jnp.zeros((16, n), f32)
    diff = rev4(pos // (tok // RES)) ^ (head & (RES - 1))
    for d in range(3):
        same = doc_row == d
        val = jnp.where(same, 0.0, 1.0) if side == "q" else jnp.where(same, -BIG, 0.0)
        out = jnp.where(rowid == d, val, out)
    row = 3
    for b in range(b0 + 1, BRANCHES):
        val = math.log2((b - b0 + 1) / (b - b0))
        high = float(np.asarray(val, dtype=jnp.bfloat16))
        chosen = (diff & (2**b - 1)) == 0
        for part in (high, val - high) if val != 1.0 else (1.0,):
            put = jnp.where(chosen, 1.0 if side == "q" else part, 0.0)
            out = jnp.where(rowid == row, put, out)
            row += 1
    assert row <= 10
    if b0 > 0:
        outside = (diff & (2**b0 - 1)) != 0
        one = jnp.where(outside, 1.0 if side == "q" else -BIG, 0.0)
        const = 1.0 if side == "q" else -BIG
        out = jnp.where(rowid == (10 if side == "q" else 11), one, out)
        out = jnp.where(rowid == (11 if side == "q" else 10), const, out)
    if extra is not None:
        for j in range(3):
            out = jnp.where(rowid == 12 + j, extra[j], out)
    return out.astype(bf16)


def split3(row):
    first = row.astype(bf16).astype(f32)
    rest = row - first
    second = rest.astype(bf16).astype(f32)
    return (first, second, rest - second)


def tail_rows(n, rows):
    rowid = lax.broadcasted_iota(jnp.int32, (16, n), 0)
    out = jnp.zeros((16, n), f32)
    for j, r in enumerate(rows):
        out = jnp.where(rowid == j, r, out)
    return out.astype(bf16)


def place(tok, axis):
    shape = (tok, 1) if axis == 0 else (1, tok)
    p = lax.broadcasted_iota(jnp.int32, shape, axis)
    return rev4(p % RES) * (tok // RES) + p // RES


def one_hot(tok, transposed):
    if transposed:
        return (place(tok, 0) == lax.broadcasted_iota(jnp.int32, (1, tok), 1)).astype(bf16)
    return (place(tok, 1) == lax.broadcasted_iota(jnp.int32, (tok, 1), 0)).astype(bf16)


def normalise(x):
    cen = x - jnp.mean(x, axis=-1, keepdims=True)
    rs = lax.rsqrt(jnp.mean(cen * cen, axis=-1, keepdims=True) + NORM_EPS)
    return cen * rs, rs


def row(ref):
    return ref[...][None, :]


def project_body(tok, y_ref, x_ref, ids_ref, gain, shift, in_b, wq, wk, wv, first_ref, q_ref, k_ref, v_ref, doc_ref, near_ref, far_ref):
    xh, _ = normalise(x_ref[...].astype(f32))
    first = (xh * row(gain) + row(shift)).astype(bf16)
    first = mm(one_hot(tok, False), first).astype(bf16)
    first_ref[...] = first.T
    ids = jnp.broadcast_to(ids_ref[...].astype(f32), (16, tok)).astype(bf16)
    docs = mm(ids, one_hot(tok, True))
    doc_ref[...] = docs[0:8]
    bias = row(in_b)
    for part, (w, ref) in enumerate(((wq, q_ref), (wk, k_ref), (wv, v_ref))):
        at = part * D
        val = mm(first, w[...]) + jnp.where(y_ref[0] == 0, bias[:, at : at + GW], bias[:, at + GW : at + D])
        if part == 0:
            val = val * Q_SCALE
        ref[...] = val.astype(bf16).T
    for out, level in ((near_ref, 1), (far_ref, 2)):
        width = tok >> level
        for part, ref in enumerate((k_ref, v_ref)):
            for h in range(HG):
                start = run_start(h, level, tok)
                out[part * GW + h * HD : part * GW + (h + 1) * HD] = ref[h * HD : (h + 1) * HD, start : start + width]
        rowid = lax.broadcasted_iota(jnp.int32, (16, width), 0)
        acc = jnp.zeros((16, width), f32)
        for j in range(2**level):
            acc = jnp.where(rowid == j, docs[0:1, j * width : (j + 1) * width], acc)
        out[2 * GW : 2 * GW + 16] = acc.astype(bf16)


def weight_specs():
    return [pl.BlockSpec((D, GW), lambda j, y, part=part: (0, 2 * part + y[0]), pipeline_mode=pl.Buffered(1)) for part in range(3)]


def pcall(body, name, scalar, ins, outs, in_specs, out_specs, *, grid=(1,), scratch=(), vmem=VMEM_MIB, flops=0):
    nbytes = sum(math.prod(a.shape) * a.dtype.itemsize for a in (*ins, *outs))
    return pl.pallas_call(
        body,
        grid_spec=pltpu.PrefetchScalarGridSpec(
            num_scalar_prefetch=1, grid=grid, in_specs=in_specs, out_specs=out_specs, scratch_shapes=list(scratch)
        ),
        out_shape=outs,
        name=name,
        compiler_params=pltpu.CompilerParams(vmem_limit_bytes=vmem * MIB),
        cost_estimate=estimate(name, flops, nbytes),
    )(scalar, *ins)


def project(y, x, ids, gain, shift, in_b, weight, vmem):
    tok = x.shape[0]
    outs = [
        sds((D, tok), bf16),
        sds((GW, tok), bf16),
        sds((GW, tok), bf16),
        sds((GW, tok), bf16),
        sds((8, tok), f32),
        sds((2 * GW + 16, tok // 2), bf16),
        sds((2 * GW + 16, tok // 4), bf16),
    ]
    return pcall(
        functools.partial(project_body, tok), "project", y, (x, ids, gain, shift, in_b, weight, weight, weight), outs,
        [full(x.shape), full(ids.shape), full((D,)), full((D,)), full((3 * D,))] + weight_specs(), [full(o.shape) for o in outs],
        vmem=vmem,
        flops=2 * tok * D * (tok + 3 * GW),
    )


def fill_keys(kaug, vaug, k_parts, v_parts, doc_parts, pos_parts, head, b0, tok):
    at = 0
    for k, v, doc, pos in zip(k_parts, v_parts, doc_parts, pos_parts, strict=True):
        n = k.shape[1]
        kaug[0:HD, at : at + n] = k
        kaug[HD:64, at : at + n] = features("k", doc, pos, head, b0, tok, (-1.0, -1.0, -1.0))
        vaug[0:HD, at : at + n] = v
        vaug[HD:64, at : at + n] = tail_rows(n, (1.0, 1.0, 1.0))
        at += n


def fill_queries(qaug, q_parts, doc_parts, pos_parts, head, b0, tok, lse_parts=None):
    at = 0
    for j, (q, doc, pos) in enumerate(zip(q_parts, doc_parts, pos_parts, strict=True)):
        n = q.shape[1]
        extra = None if lse_parts is None else split3(lse_parts[j])
        qaug[0:HD, at : at + n] = q
        qaug[HD:64, at : at + n] = features("q", doc, pos, head, b0, tok, extra)
        at += n


def iota_row(n):
    return lax.broadcasted_iota(jnp.int32, (1, n), 1)


def attend(qaug, kaug, vaug, nq, nk, step, put):
    keys = kaug[:, 0:nk].T
    for at in range(0, nq, step):
        scores = mm(keys, qaug[:, at : at + step])
        probs = jnp.exp2(scores).astype(bf16)
        put(at, mm(vaug[:, 0:nk], probs))


def own_forward_body(tok, y_ref, qa, qb, ka, kb, va, vb, da, db, out_ref, qaug, kaug, vaug):
    pos = iota_row(tok)
    docs = (da[0:1], db[0:1])
    for i in range(OWN_STEP):
        head = y_ref[0] * HG + pl.program_id(0) * OWN_STEP + i
        at_head = lambda *refs: tuple(Rows(r, i)[...] for r in refs)
        fill_keys(kaug.at[i], vaug.at[i], at_head(ka, kb), at_head(va, vb), docs, (pos, pos), head, 0, tok)
        fill_queries(qaug.at[i], at_head(qa, qb), docs, (pos, pos), head, 0, tok)

        def put(at, val):
            out_ref[i, :, at : at + val.shape[1]] = val

        attend(qaug.at[i], kaug.at[i], vaug.at[i], 2 * tok, 2 * tok, tok, put)


def head_block(tok, step=1):
    return pl.BlockSpec((HD * step, tok), lambda h: (h, 0))


class Rows:
    def __init__(self, ref, head):
        self.ref, self.rows = ref, slice(head * HD, (head + 1) * HD)

    def __getitem__(self, at):
        return self.ref[(self.rows,) + at[1:]] if isinstance(at, tuple) else self.ref[self.rows]

    def __setitem__(self, at, value):
        if isinstance(at, tuple):
            self.ref[(self.rows,) + at[1:]] = value
        else:
            self.ref[self.rows] = value


def own_forward(y, qs, ks, vs, docs):
    tok = qs[0].shape[1]
    return kcall(
        functools.partial(own_forward_body, tok),
        "own_forward",
        (y, *qs, *ks, *vs, *docs),
        [sds((HG, 64, 2 * tok), f32)],
        grid=(HG // OWN_STEP,),
        in_specs=[SMEM] + [head_block(tok, OWN_STEP)] * 6 + [full((8, tok))] * 2,
        out_specs=[pl.BlockSpec((OWN_STEP, 64, 2 * tok), lambda h: (h, 0, 0))],
        scratch=[pltpu.VMEM((OWN_STEP, 64, 2 * tok), bf16)] * 3,
        flops=2 * HG * 128 * (2 * tok) ** 2,
    )[0]


def groups_of(masks):
    found = {}
    for j, m in enumerate(masks):
        found.setdefault(m.bit_length(), []).append(j)
    return [(b0, min(b0, 2), found[b0]) for b0 in sorted(found)]


def remote_parts(refs, members, local, level, tok, pieces=2):
    width = tok >> level
    start = run_start(local, level, tok)
    lane = iota_row(width) + start
    row = pl.multiple_of(local * HD, 16)
    ks, vs, docs, poss = [], [], [], []
    for j in members:
        for ref in refs[pieces * j : pieces * (j + 1)]:
            ks.append(ref[pl.ds(row, HD), :])
            vs.append(ref[pl.ds(row + GW, HD), :])
            block = ref[2 * GW : 2 * GW + 16, :].astype(f32)
            picked = block[0:1]
            for r in range(1, 2**level):
                picked = jnp.where(start // width == r, block[r : r + 1], picked)
            docs.append(picked)
            poss.append(lane)
    return ks, vs, docs, poss, start, width


def far_forward_body(tok, masks, last, y_ref, qa, qb, da, db, part, *rest):
    refs, rest = rest[: len(masks)], rest[len(masks) :]
    outs, (qaugs, kaugs, vaugs, accs) = rest[:-4], rest[-4:]
    for i in range(FAR_STEP):
        local = pl.program_id(0) * FAR_STEP + i
        head = y_ref[0] * HG + local
        qh, acc = (Rows(qa, i), Rows(qb, i)), accs.at[i]
        acc[...] = part[i]
        for g, (b0, level, members) in enumerate(groups_of(masks)):
            qaug, kaug, vaug = qaugs.at[i, g], kaugs.at[i, g], vaugs.at[i, g]
            ks, vs, docs, poss, start, width = remote_parts(refs, members, local, level, tok, 1)
            nk = width * len(ks)
            fill_keys(kaug, vaug, ks, vs, docs, poss, head, b0, tok)
            window = pl.ds(pl.multiple_of(start, 128), width)
            pos = iota_row(width) + start
            fill_queries(qaug, [q[:, window] for q in qh], (da[0:1, window], db[0:1, window]), (pos, pos), head, b0, tok)

            def put(at, val):
                acc[:, window] += val[:, 0:width]
                other = pl.ds(pl.multiple_of(start + tok, 128), width)
                acc[:, other] += val[:, width : 2 * width]

            attend(qaug, kaug, vaug, 2 * width, nk, 2 * width, put)
        if not last:
            outs[0][i] = acc[...]
            continue
        ma, mb, merged, lse = outs
        den = acc[HD : HD + 1]
        val = acc[0:HD] / den
        merged[i] = val
        Rows(ma, i)[...] = val[:, 0:tok].astype(bf16)
        Rows(mb, i)[...] = val[:, tok : 2 * tok].astype(bf16)
        lse[i] = jnp.broadcast_to(jnp.log2(den), (8, 2 * tok))


def remote_sizes(masks, tok):
    nq = max([tok >> level << 1 for _, level, _ in groups_of(masks)] + [128])
    nk = max([(tok >> level) * 2 * len(members) for _, level, members in groups_of(masks)] + [128])
    return nq, nk


def remote_flops(masks, tok):
    return sum(2 * HG * 64 * (2 * (tok >> lv)) * ((tok >> lv) * 2 * len(mem)) for _, lv, mem in groups_of(masks))


def far_forward(y, qs, docs, part, masks, remote, last):
    tok = qs[0].shape[1]
    nq, nk = remote_sizes(masks, tok)
    nk = max(nk // 2, 128)
    n = len(groups_of(masks))
    per_head = lambda r: pl.BlockSpec((FAR_STEP, r, 2 * tok), lambda h: (h, 0, 0))
    final = [sds((GW, tok), bf16)] * 2 + [sds((HG, HD, 2 * tok), f32), sds((HG, 8, 2 * tok), f32)]
    return kcall(
        functools.partial(far_forward_body, tok, masks, last),
        "far_forward" if last else "far_forward_first",
        (y, *qs, *docs, part, *remote),
        final if last else [sds((HG, 64, 2 * tok), f32)],
        grid=(HG // FAR_STEP,),
        in_specs=[SMEM] + [head_block(tok, FAR_STEP)] * 2 + [full((8, tok))] * 2 + [per_head(64)] + [full(r.shape) for r in remote],
        out_specs=[head_block(tok, FAR_STEP)] * 2 + [per_head(HD), per_head(8)] if last else [per_head(64)],
        scratch=[
            pltpu.VMEM((FAR_STEP, n, 64, nq), bf16),
            pltpu.VMEM((FAR_STEP, n, 64, nk), bf16),
            pltpu.VMEM((FAR_STEP, n, 64, nk), bf16),
            pltpu.VMEM((FAR_STEP, 64, 2 * tok), f32),
        ],
        flops=remote_flops(masks, tok),
    )


def attend_back(qaug, gaug, kaug, vaug, nq, nk, step, put_q, dk, dv):
    keys = kaug[0:HD, 0:nk]
    for at in range(0, nq, step):
        sl = slice(at, at + step)
        probs = jnp.exp2(mm(qaug[:, sl].T, kaug[:, 0:nk]))
        gprobs = mm(gaug[:, sl].T, vaug[:, 0:nk])
        gs = (probs * gprobs).astype(bf16)
        new_v = mm(gaug[0:HD, sl], probs.astype(bf16))
        new_k = mm(qaug[0:HD, sl], gs)
        if at == 0:
            dv[:, 0:nk] = new_v
            dk[:, 0:nk] = new_k
        else:
            dv[:, 0:nk] += new_v
            dk[:, 0:nk] += new_k
        put_q(at, mm(keys, gs, NT) * SCALE)


def fill_grads(gaug, g_parts, m_parts):
    at = 0
    for g, m in zip(g_parts, m_parts, strict=True):
        n = g.shape[1]
        delta = jnp.sum(g.astype(f32) * m, axis=0, keepdims=True)
        gaug[0:HD, at : at + n] = g
        gaug[HD:64, at : at + n] = tail_rows(n, split3(-delta))
        at += n


def far_backward_body(tok, masks, y_ref, qa, qb, da, db, ga, gb, merged, lse, *rest):
    nrem = 2 * len(masks)
    refs = rest[:nrem]
    dq_ref = rest[nrem]
    sends = rest[nrem + 1 : nrem + 1 + len(masks)]
    qaugs, gaugs, kaugs, vaugs, dks, dvs = rest[nrem + 1 + len(masks) :]
    for i in range(FAR_STEP):
        local = pl.program_id(0) * FAR_STEP + i
        head = y_ref[0] * HG + local
        row = pl.multiple_of(local * HD, 16)
        dq_ref[i] = jnp.zeros((HD, 2 * tok), f32)
        qh, gh = (Rows(qa, i), Rows(qb, i)), (Rows(ga, i), Rows(gb, i))
        for g, (b0, level, members) in enumerate(groups_of(masks)):
            qaug, gaug, kaug, vaug, dk, dv = (v.at[i, g] for v in (qaugs, gaugs, kaugs, vaugs, dks, dvs))
            ks, vs, docs, poss, start, width = remote_parts(refs, members, local, level, tok)
            nk = width * len(ks)
            fill_keys(kaug, vaug, ks, vs, docs, poss, head, b0, tok)
            window = pl.ds(pl.multiple_of(start, 128), width)
            other = pl.ds(pl.multiple_of(start + tok, 128), width)
            pos = iota_row(width) + start
            fill_queries(
                qaug, [q[:, window] for q in qh], (da[0:1, window], db[0:1, window]), (pos, pos), head, b0, tok,
                (lse[i, 0:1, window], lse[i, 0:1, other]),
            )
            fill_grads(gaug, [v[:, window] for v in gh], (merged[i, :, window], merged[i, :, other]))

            def put_q(at, val):
                dq_ref[i, :, window] += val[:, 0:width]
                dq_ref[i, :, other] += val[:, width : 2 * width]

            attend_back(qaug, gaug, kaug, vaug, 2 * width, nk, 2 * width, put_q, dk, dv)
            for n, j in enumerate(members):
                span = slice(2 * n * width, 2 * (n + 1) * width)
                sends[j][pl.ds(row, HD), :] = (dk[:, span] * LN2).astype(bf16)
                sends[j][pl.ds(row + GW, HD), :] = dv[:, span].astype(bf16)


def far_backward(y, qs, docs, gs, merged, lse, masks, remote):
    tok = qs[0].shape[1]
    nq, nk = remote_sizes(masks, tok)
    n = len(groups_of(masks))
    per_head = lambda r: pl.BlockSpec((FAR_STEP, r, 2 * tok), lambda h: (h, 0, 0))
    blocks = head_block(tok, FAR_STEP)
    sends = [sds((2 * GW, 2 * (tok >> min(m.bit_length(), 2))), bf16) for m in masks]
    return kcall(
        functools.partial(far_backward_body, tok, masks),
        "far_backward",
        (y, *qs, *docs, *gs, merged, lse, *remote),
        [sds((HG, HD, 2 * tok), f32)] + sends,
        grid=(HG // FAR_STEP,),
        in_specs=[SMEM] + [blocks] * 2 + [full((8, tok))] * 2 + [blocks] * 2
        + [per_head(HD), per_head(8)] + [full(r.shape) for r in remote],
        out_specs=[per_head(HD)] + [full(s.shape) for s in sends],
        scratch=[pltpu.VMEM((FAR_STEP, n, 64, nq), bf16)] * 2
        + [pltpu.VMEM((FAR_STEP, n, 64, nk), bf16)] * 2
        + [pltpu.VMEM((FAR_STEP, n, HD, nk), f32)] * 2,
        flops=5 * remote_flops(masks, tok),
    )


def own_backward_body(tok, y_ref, qa, qb, ka, kb, va, vb, da, db, ga, gb, merged, lse, dq_in, dq, dk, dv, qaug, gaug, kaug, vaug):
    head = y_ref[0] * HG + pl.program_id(0)
    pos = iota_row(tok)
    docs = (da[0:1], db[0:1])
    fill_keys(kaug, vaug, (ka[...], kb[...]), (va[...], vb[...]), docs, (pos, pos), head, 0, tok)
    fill_queries(
        qaug, (qa[...], qb[...]), docs, (pos, pos), head, 0, tok, (lse[0, 0:1, 0:tok], lse[0, 0:1, tok : 2 * tok])
    )
    fill_grads(gaug, (ga[...], gb[...]), (merged[0, :, 0:tok], merged[0, :, tok : 2 * tok]))

    def put_q(at, val):
        dq[:, at : at + tok] = (val + dq_in[0, :, at : at + tok]).astype(bf16)

    attend_back(qaug, gaug, kaug, vaug, 2 * tok, 2 * tok, tok, put_q, dk.at[0], dv.at[0])


def own_backward(y, qs, ks, vs, docs, gs, merged, lse, dq):
    tok = qs[0].shape[1]
    per_head = lambda r: pl.BlockSpec((1, r, 2 * tok), lambda h: (h, 0, 0))
    return kcall(
        functools.partial(own_backward_body, tok),
        "own_backward",
        (y, *qs, *ks, *vs, *docs, *gs, merged, lse, dq),
        [sds((GW, 2 * tok), bf16)] + [sds((HG, HD, 2 * tok), f32)] * 2,
        grid=(HG,),
        in_specs=[SMEM] + [head_block(tok)] * 6 + [full((8, tok))] * 2 + [head_block(tok)] * 2
        + [per_head(HD), per_head(8), per_head(HD)],
        out_specs=[head_block(2 * tok)] + [per_head(HD)] * 2,
        scratch=[pltpu.VMEM((64, 2 * tok), bf16)] * 4,
        flops=5 * HG * 128 * (2 * tok) ** 2,
    )


NBLK = 8
HALF = D // 2
DOWN_ROWS = FF // NBLK
UP_ROWS = D // NBLK
ROWS_A = 2 * UP_ROWS + UP_ROWS // 2
ROWS_B = DOWN_ROWS // 2


def cot_body(cot, down, out):
    out[...] = mm(cot[...], down[...], NT).astype(out.dtype)


def cot_down(cot, down):
    tok, ff = cot.shape[0], down.shape[0]
    blk = 768
    return kcall(
        cot_body, "cot_down", (cot, down), [sds((tok, ff), bf16)], grid=(ff // blk,),
        in_specs=[full((tok, D)), pl.BlockSpec((blk, D), lambda j: (j, 0))],
        out_specs=[pl.BlockSpec((tok, blk), lambda j: (0, j))], vmem=60, flops=2 * tok * D * ff,
    )[0]


ERF_P = 0.3275911
ERF_A = (0.254829592, -0.284496736, 1.421413741, -1.453152027, 1.061405429)


def normal_cdf(v):
    gauss = jnp.exp2(v * v * (-0.5 / LN2))
    t = 1.0 / (1.0 + jnp.abs(v) * (ERF_P * 0.5**0.5))
    poly = 0.5 * ERF_A[4]
    for a in ERF_A[3::-1]:
        poly = poly * t + 0.5 * a
    tail = poly * t * gauss
    return jnp.where(v < 0, tail, 1.0 - tail), gauss


def mlp_body(tok, nblk, bits, x_ref, mown, moth, out_b, n2g, n2s, wout, up, up_b, gdown, cot,
             gelu_ref, gelu_send, gpre_ref, gpre_send, upb_ref, rows_ref, resid_ref, gmown, gmoth, gres_ref, vec_ref,
             second, xhat, rstd, acc):
    step = pl.program_id(0)
    y = bits[0]
    low_core = bits[3] == 0
    mine = pl.ds(pl.multiple_of(y * GW, 128), GW)
    theirs = pl.ds(pl.multiple_of((1 - y) * GW, 128), GW)
    gain = row(n2g)

    @pl.when(step == 0)
    def _():
        pmt = one_hot(tok, True)
        own = mm(pmt, mown[...], NT).astype(bf16)
        oth = mm(pmt, moth[...], NT).astype(bf16)
        resid = x_ref[...].astype(f32) + (mm(own, wout[mine, :]) + mm(oth, wout[theirs, :])) + row(out_b)
        resid_ref[...] = resid
        xh, rs = normalise(resid)
        xhat[...] = xh
        rstd[...] = jnp.broadcast_to(rs, rstd.shape)
        low = (xh * gain + row(n2s)).astype(bf16)
        second[...] = low
        rows_ref[0:D] = low.T
        acc[...] = jnp.zeros_like(acc)

    rows = tok // MLP_SPLIT
    for i in range(MLP_SPLIT):
        part = slice(i * rows, (i + 1) * rows)
        pre = mm(second[part], up[...]) + up_b[0]
        cdf, gauss = normal_cdf(pre)
        gelu_t = (pre * cdf).astype(bf16).T
        gelu_ref[:, part] = gelu_t
        half = DOWN_ROWS // 2
        for at in range(0, gelu_t.shape[0], DOWN_ROWS):
            low, high = gelu_t[at : at + half], gelu_t[at + half : at + DOWN_ROWS]
            gelu_send[at // 2 : at // 2 + half, part] = jnp.where(low_core, high, low)
        slope = cdf + pre * (gauss * (1.0 / math.sqrt(2.0 * math.pi)))
        gpre = (slope * gdown[part]).astype(bf16)
        gpre_ref[part] = gpre

        gpre_send[part] = gpre
        acc[part] += mm(gpre, up[...], NT)
        sums = mm(jnp.ones((8, rows), bf16), gpre)
        upb_ref[...] = sums if i == 0 else upb_ref[...] + sums

    @pl.when(step == nblk - 1)
    def _():
        dy = acc[...]
        xh = xhat[...]
        dyg = dy * gain
        m1 = jnp.mean(dyg, axis=-1, keepdims=True)
        m2 = jnp.mean(dyg * xh, axis=-1, keepdims=True)
        g = cot[...]
        gres = g.astype(f32) + rstd[:, 0:1] * (dyg - m1 - xh * m2)
        gres_ref[...] = gres
        gattn = gres.astype(bf16)
        gattn_t = mm(gattn.T, one_hot(tok, True)).astype(bf16)
        rows_ref[D : 2 * D] = gattn_t
        gmoth[...] = mm(wout[theirs, :], gattn_t).astype(bf16)
        gmown[...] = mm(wout[mine, :], gattn_t).astype(bf16)
        ones = jnp.ones((8, tok), bf16)
        vec_ref[0:8] = mm(ones, g)
        vec_ref[8:16] = jnp.broadcast_to(jnp.sum(dy * xh, axis=0, keepdims=True), (8, D))
        vec_ref[16:24] = jnp.broadcast_to(jnp.sum(dy, axis=0, keepdims=True), (8, D))
        vec_ref[24:32] = mm(ones, gattn)


def mlp_chunk(step, bits):
    return (step // 2 + bits[3]) % 2 * 2 + step % 2


def mlp(bits, x, mown, moth, out_b, n2g, n2s, wout, up, up_b, gdown, cot):
    tok = cot.shape[0]
    ff = up.shape[1]
    nblk = 4
    blk = ff // nblk
    wide = pl.BlockSpec((tok, blk), lambda j, b: (0, mlp_chunk(j, b)))
    outs = [
        sds((ff, tok), bf16), sds((ff // 2, tok), bf16), sds((tok, ff), bf16), sds((tok, ff // 2), bf16), sds((8, ff), f32),
        sds((2 * D, tok), bf16), sds((tok, D), f32), sds((GW, tok), bf16), sds((GW, tok), bf16),
        sds((tok, D), f32), sds((32, D), f32),
    ]
    return pcall(
        functools.partial(mlp_body, tok, nblk),
        "mlp",
        bits,
        (x, mown, moth, out_b, n2g, n2s, wout, up, up_b.reshape(nblk, 1, blk), gdown, cot),
        outs,
        [
            full(x.shape), full(mown.shape), full(moth.shape), full((D,)), full((D,)), full((D,)), full(wout.shape),
            pl.BlockSpec((D, blk), lambda j, b: (0, mlp_chunk(j, b))),
            pl.BlockSpec((1, 1, blk), lambda j, b: (mlp_chunk(j, b), 0, 0)),
            wide, full((tok, D)),
        ],
        [
            pl.BlockSpec((blk, tok), lambda j, b: (mlp_chunk(j, b), 0)),
            pl.BlockSpec((blk // 2, tok), lambda j, b: (mlp_chunk(j, b), 0)),
            wide,
            pl.BlockSpec((tok, blk), lambda j, b: (0, jnp.maximum(j - nblk // 2, 0))),
            pl.BlockSpec((8, blk), lambda j, b: (0, mlp_chunk(j, b))),
        ] + [full(o.shape) for o in outs[5:]],
        grid=(nblk,),
        scratch=[pltpu.VMEM((tok, D), bf16), pltpu.VMEM((tok, D), f32), pltpu.VMEM((tok, 128), f32), pltpu.VMEM((tok, D), f32)],
        vmem=28,
        flops=2 * tok * D * (2 * ff + 2 * D + 2 * tok),
    )


def mlp_grads_body(bits, cores, *refs):
    ins, outs = refs[:-4], refs[-4:]
    send_a, keep_a, send_b, keep_b = outs
    ybit, xbit = bits[0], bits[1]
    heads_low = (pl.program_id(0) < 2) == (ybit == 0)
    up = att = 0.0
    down = [0.0, 0.0]
    for c in range(cores):
        low_t, high_t, second_t, gattn_t, gpre, cot, mown, moth = ins[8 * c : 8 * c + 8]
        up = up + mm(second_t[...], gpre[...])
        down = [old + mm(gelu_t[...], cot[...]) for old, gelu_t in zip(down, (low_t, high_t), strict=True)]
        att = att + mm(jnp.where(heads_low, mown[...], moth[...]), gattn_t[...], NT)
    up, att, down = up.astype(bf16), att.astype(bf16), [v.astype(bf16) for v in down]
    x_low, y_low = xbit == 0, ybit == 0
    half = UP_ROWS // 2
    for y in range(2):
        rows = slice(y * UP_ROWS, (y + 1) * UP_ROWS)
        cols = [up[rows, c * HALF : (c + 1) * HALF] for c in range(4)]
        pieces = [(0, UP_ROWS, cols[0], cols[2]), (UP_ROWS, UP_ROWS, cols[1], cols[3])]
        pieces += [(2 * UP_ROWS, half, att[y * UP_ROWS : y * UP_ROWS + half], att[y * UP_ROWS + half : (y + 1) * UP_ROWS])]
        for at, n, low, high in pieces:
            keep_a[0, y, at : at + n] = jnp.where(x_low, low, high)
            send_a[0, y, at : at + n] = jnp.where(x_low, high, low)
    for x in range(2):
        low, high = (v[:, x * HALF : (x + 1) * HALF] for v in down)
        keep_b[0, x] = jnp.where(y_low, low, high)
        send_b[0, x] = jnp.where(y_low, high, low)


def mlp_grads(bits, *per_core):
    tok = per_core[0][3].shape[0]
    ins, specs = [], []
    for gelu_t, rows, gpre, cot, mown, moth in per_core:
        heads = pl.BlockSpec((GW // 2, tok), lambda j, b: (j % 2, 0))
        ins += [gelu_t, gelu_t, rows, rows, gpre, cot, mown, moth]
        if gelu_t.shape[0] == FF:
            gelus = [pl.BlockSpec((ROWS_B, tok), lambda j, b, y=y: (4 * j + 2 * y + b[3], 0)) for y in range(2)]
            half = pl.BlockSpec((tok, FF // 2), lambda j, b: (0, b[3]))
        else:
            gelus = [pl.BlockSpec((ROWS_B, tok), lambda j, b, y=y: (2 * j + y, 0)) for y in range(2)]
            half = full(gpre.shape)
        specs += gelus + [
            pl.BlockSpec((D // 4, tok), lambda j, b: (j, 0)),
            pl.BlockSpec((HALF, tok), lambda j, b: (D // HALF + b[3], 0)),
            half, full(cot.shape), heads, heads,
        ]
    outs = [sds((4, 2, ROWS_A, HALF), bf16)] * 2 + [sds((4, 2, ROWS_B, HALF), bf16)] * 2
    return pcall(
        lambda bits, *refs: mlp_grads_body(bits, len(per_core), *refs), "mlp_grads", bits, ins, outs, specs,
        [pl.BlockSpec((1,) + o.shape[1:], lambda j, b: (j, 0, 0, 0)) for o in outs],
        grid=(4,),
        vmem=22,
        flops=2 * tok * D * (2 * FF + D),
    )


IN_ROWS = D // NBLK // 2
IN_COLS = 3 * GW + 128
SMALL_ROWS = 16
UNIT = UP_ROWS


def query_grads_body(tok, bits, dq, fa, fb, wq, val, dy, bias, acc):
    step = pl.program_id(0)
    nat = mm(one_hot(tok, True), dq[...], NT).astype(bf16)
    dy[0] = mm(nat, wq[...], NT)
    new_bias = mm(jnp.ones((8, tok), bf16), nat)

    @pl.when(step == 0)
    def _():
        acc[...] = mm(fb[...], dq[...], NT)
        bias[...] = new_bias

    @pl.when(step == 1)
    def _():
        val[...] = (acc[...] + mm(fa[...], dq[...], NT)).astype(bf16)
        bias[...] += new_bias


def query_grads(bits, dq, fa, fb, weight):
    tok = fa.shape[1]
    outs = [sds((D, GW), bf16), sds((2, tok, D), f32), sds((8, GW), f32)]
    return pcall(
        functools.partial(query_grads_body, tok), "query_grads", bits, (dq, fa, fb, weight), outs,
        [pl.BlockSpec((GW, tok), lambda j, y: (0, 1 - j)), full(fa.shape), full(fb.shape), weight_specs()[0]],
        [full((D, GW)), pl.BlockSpec((1, tok, D), lambda j, y: (1 - j, 0, 0)), full((8, GW))],
        grid=(2,),
        scratch=[pltpu.VMEM((D, GW), f32)],
    )


def finish_body(tok, masks, bits, val_q, dy_q, bias_q, dk, dv, xa, xb, fa, fb, wk, wv, vec, up_sum, *rest):
    nrem = len(masks)
    recv = rest[:nrem]
    first_a, first_b, send, keep, gkv, total, acc, sums, bias, small = rest[nrem:]
    step = pl.program_id(0)
    for part, ref, scale in ((0, dk, LN2), (1, dv, 1.0)):
        for h in range(HG):
            total[h * HD : (h + 1) * HD] = ref[h] * scale
        for m, r in zip(masks, recv, strict=True):
            level = min(m.bit_length(), 2)
            for h in range(HG):
                start = run_start(h, level, tok)
                row = part * GW + h * HD
                total[h * HD : (h + 1) * HD, start : start + (tok >> level)] += r[row : row + HD].astype(f32)
        gkv[part * GW : (1 + part) * GW] = total[...].astype(bf16)
    nat = mm(one_hot(tok, True), gkv[...], NT).astype(bf16)
    new_bias = mm(jnp.ones((8, tok), bf16), nat)
    dy = dy_q[0] + sum(mm(nat[:, part * GW : (part + 1) * GW], w[...], NT) for part, w in enumerate((wk, wv)))
    later = step == 1
    xh, _ = normalise(jnp.where(later, xa[...], xb[...]).astype(f32))
    new_gain = jnp.sum(dy * xh, axis=0, keepdims=True)
    new_shift = jnp.sum(dy, axis=0, keepdims=True)

    @pl.when(step == 0)
    def _():
        first_b[...] = dy.astype(bf16)
        acc[...] = mm(fb[...], gkv[...], NT)
        bias[...] = new_bias
        sums[0:8] = jnp.broadcast_to(new_gain, (8, D))
        sums[8:16] = jnp.broadcast_to(new_shift, (8, D))

    @pl.when(step == 1)
    def _():
        first_a[...] = dy
        val = (acc[...] + mm(fa[...], gkv[...], NT)).astype(bf16)
        all_bias = jnp.concatenate([bias_q[0:1], bias[0:1] + new_bias[0:1]], axis=1)
        lines = [sums[0:1] + new_gain, sums[8:9] + new_shift]
        lines += [vec[8 * j : 8 * j + 1] for j in range(4)]
        cut = lambda line, u: line[:, u * UNIT : (u + 1) * UNIT]
        small[...] = jnp.zeros_like(small)

        def put(block, row, line):
            small[block, row : row + 1, 0:UNIT] = line

        for s in range(NBLK):
            for row, line in zip((0, 1, 5, 6, 7, 8), lines, strict=True):
                put(s, row, cut(line, s))
            for k in range(4):
                put(s, 9 + k, cut(up_sum[0:1], s * 4 + k))
        for u in range(3 * NBLK):
            part, owner, k = u // 8, u // 4 % 2, u % 4
            put(u // 3, 2 + u % 3, jnp.where(bits[0] == owner, cut(all_bias, part * 4 + k), 0.0))
        keep_low = bits[3] == 0
        zeros = jnp.zeros((IN_ROWS, 128), bf16)

        def store(block, lanes, low, high):
            keep[block, :, lanes] = jnp.where(keep_low, low, high)
            send[block, :, lanes] = jnp.where(keep_low, high, low)

        for s in range(NBLK):
            at = 2 * s * IN_ROWS
            for lanes, part in ((slice(0, GW), val_q), (slice(GW, 3 * GW), val)):
                store(s, lanes, part[at : at + IN_ROWS], part[at + IN_ROWS : at + 2 * IN_ROWS])
            store(s, slice(3 * GW, IN_COLS), jnp.concatenate([small[s].astype(bf16), zeros[SMALL_ROWS:]], axis=0), zeros)


def finish(bits, queries, dk, dv, xa, xb, fa, fb, weight, vec, up_sum, masks, recv):
    tok = xa.shape[0]
    piece = lambda j: 1 - j
    by_head = pl.BlockSpec((HG, HD, tok), lambda j, y: (0, 0, piece(j)))
    outs = [sds((tok, D), f32), sds((tok, D), bf16)] + [sds((NBLK, IN_ROWS, IN_COLS), bf16)] * 2
    return pcall(
        functools.partial(finish_body, tok, masks),
        "finish",
        bits,
        (*queries, dk, dv, xa, xb, fa, fb, weight, weight, vec, up_sum, *recv),
        outs,
        [full((D, GW)), pl.BlockSpec((1, tok, D), lambda j, y: (piece(j), 0, 0)), full((8, GW)), by_head, by_head]
        + [full(v.shape) for v in (xa, xb, fa, fb)] + weight_specs()[1:] + [full(vec.shape), full(up_sum.shape)]
        + [pl.BlockSpec((2 * GW, r.shape[1] // 2), lambda j, y: (0, piece(j))) for r in recv],
        [full(o.shape) for o in outs],
        grid=(2,),
        scratch=[
            pltpu.VMEM((2 * GW, tok), bf16), pltpu.VMEM((GW, tok), f32), pltpu.VMEM((D, 2 * GW), f32),
            pltpu.VMEM((16, D), f32), pltpu.VMEM((8, 2 * GW), f32), pltpu.VMEM((NBLK, SMALL_ROWS, 128), f32),
        ],
        vmem=24,
        flops=4 * tok * 3 * GW * (tok + 2 * D),
    )


def input_grad_body(x_ref, gain, own, got, gres, out):
    xh, rs = normalise(x_ref[...].astype(f32))
    dyg = (own[...] + got[...].astype(f32)) * row(gain)
    m1 = jnp.mean(dyg, axis=-1, keepdims=True)
    m2 = jnp.mean(dyg * xh, axis=-1, keepdims=True)
    out[...] = gres[...] + rs * (dyg - m1 - xh * m2)


def unpack_mlp_body(bits, near, far, down, up, att):
    low = bits[3] == 0
    for c, v in enumerate((jnp.where(low, near[...], far[...]), jnp.where(low, far[...], near[...]))):
        for x in range(2):
            half = v[x].astype(f32)
            for j in range(2):
                at = (c * 4 + 2 * x + j) * HALF
                up[:, at : at + HALF] = half[j * UP_ROWS : (j + 1) * UP_ROWS]
            n = UP_ROWS // 2
            att[x * n : (x + 1) * n, c * HALF : (c + 1) * HALF] = half[2 * UP_ROWS : ROWS_A]
            down[c * ROWS_B : (c + 1) * ROWS_B, x * HALF : (x + 1) * HALF] = half[ROWS_A:]


VEC_UNITS = (1, 1, 3, 1, 1, 1, 1, 4)


def unpack_in_body(bits, near, far, out, *vecs):
    low = bits[3] == 0
    lower = jnp.where(low, near[...], far[...])
    upper = jnp.where(low, far[...], near[...])
    val = jnp.concatenate([lower[0], lower[1], upper[0], upper[1]], axis=0).astype(f32)
    for part in range(3):
        for y in range(2):
            src = (y * 3 + part) * GW
            dst = (part * 2 + y) * GW
            out[:, dst : dst + GW] = val[:, src : src + GW]
    row = 0
    for ref, units in zip(vecs, VEC_UNITS, strict=True):
        line = jnp.concatenate([val[row + k : row + k + 1, 6 * GW : 6 * GW + UNIT] for k in range(units)], axis=1)
        ref[...] = line[0]
        row += units


def swap(value, axis, offset):
    count = lax.axis_size(axis)
    return lax.ppermute(value, axis, [(i, i ^ offset) for i in range(count)])


def pick(value, index, dim):
    return lax.dynamic_index_in_dim(value, index, dim, keepdims=False)


def halve(pieces, index, dim):
    def part(i):
        return sum(pick(p, i, dim).astype(f32) for p in pieces).astype(bf16)

    return part(1 - index), part(index)


def split_second_body(bits, ka, ga, kb, gb, send_a, keep_a, send_b, keep_b):
    for keep, got, send_to, keep_to, bit in ((ka, ga, send_a, keep_a, bits[0]), (kb, gb, send_b, keep_b, bits[1])):
        total = lambda j: keep[0, j] + got[0, j]
        send_to[0] = total(1 - bit)
        keep_to[0] = total(bit)


def split_second(bits, ka, ga, kb, gb):
    block = lambda v: pl.BlockSpec((1,) + v.shape[1:], lambda j: (j, 0, 0, 0))
    outs = [sds((4,) + v.shape[2:], bf16) for v in (ka, ka, kb, kb)]
    return kcall(
        split_second_body, "split_second", (bits, ka, ga, kb, gb), outs, grid=(4,),
        in_specs=[SMEM] + [block(v) for v in (ka, ga, kb, gb)],
        out_specs=[pl.BlockSpec((1,) + o.shape[1:], lambda j: (j, 0, 0)) for o in outs],
    )


def split_third_body(bits, ka, ga, kb, gb, send, keep):
    low = bits[2] % 2
    at = 0
    for own, got in ((ka, ga), (kb, gb)):
        rows = slice(at, at + own.shape[1])
        send[0, rows] = own[1 - low] + got[1 - low]
        keep[0, rows] = own[low] + got[low]
        at += own.shape[1]


def split_third(bits, ka, ga, kb, gb):
    out = sds((2, ka.shape[1] + kb.shape[1], HALF), bf16)
    two = lambda v, n: pl.BlockSpec((n,) + v.shape[1:], lambda j: (j, 0, 0))
    return kcall(
        split_third_body, "split_third", (bits, ka, ga, kb, gb), [out, out], grid=(2,),
        in_specs=[SMEM] + [two(v, 2) for v in (ka, ga, kb, gb)], out_specs=[two(out, 1)] * 2,
    )


def spread(mine, xbit):
    other = swap(mine, "rep", 2)
    dim = mine.ndim - 2
    pair = jnp.stack([jnp.where(xbit == 0, mine, other), jnp.where(xbit == 0, other, mine)], axis=dim)
    return pair, swap(pair, "rep", 1)


def tie(*values):
    return lax.optimization_barrier(values)


def body(tile_embed, doc_ids, norm1_gain, norm1_shift, in_weight, in_bias, out_weight, out_bias,
         norm2_gain, norm2_shift, up_weight, up_bias, down_weight, down_bias, cotangent):
    tok = tile_embed.shape[1]
    count = lax.axis_size("seq")
    assert SEG0 == 2 * tok and tok % 512 == 0
    nodes = count // 2
    masks = [m for m in range(1, min(nodes, 2 ** (BRANCHES - 1)))]
    whole = count == 8 and lax.axis_size("rep") == 4
    index = lax.axis_index("seq")
    ybit = index % 2
    z = index // 2
    rep = lax.axis_index("rep")
    core, xbit = rep % 2, rep // 2
    bits = jnp.stack([ybit, xbit, z, core if whole else jnp.zeros_like(core)]).astype(jnp.int32)
    y = bits


    x, cot = tile_embed[0], cotangent[0]
    x_oth = swap(x, "seq", 1)
    ids_oth = swap(doc_ids, "seq", 1)

    args = (norm1_gain, norm1_shift, in_bias, in_weight)
    first_a, qa, ka, va, doc_a, *out_a = project(y, x, doc_ids, *args, 60)
    remote_a = [swap(out_a[min(m.bit_length(), 2) - 1], "seq", 2 * m) for m in masks]
    gdown = cot_down(cot, down_weight)
    x_oth, ids_oth, gdown = tie(x_oth, ids_oth, gdown)
    if whole:
        cot_got = swap(cot, "rep", 1)
    first_b, qb, kb, vb, doc_b, *out_b = project(y, x_oth, ids_oth, *args, VMEM_MIB)
    remote_b = [swap(out_b[min(m.bit_length(), 2) - 1], "seq", 2 * m) for m in masks]

    qs, ks, vs, docs = (qa, qb), (ka, kb), (va, vb), (doc_a, doc_b)
    part = own_forward(y, qs, ks, vs, docs)
    remote = [r for pair in zip(remote_a, remote_b, strict=True) for r in pair]
    part, = far_forward(y, qs, docs, part, masks, remote_a, False)
    mown, msend, merged, lse = far_forward(y, qs, docs, part, masks, remote_b, True)
    moth = swap(msend, "seq", 1)
    if whole:
        moth, cot_got, mown_got = tie(moth, cot_got, swap(mown, "rep", 1))
    (gelu_t, gelu_send, gpre, gpre_send, up_sum, rows, resid1, gmown, gmsend, gres, vec) = mlp(
        bits, x, mown, moth, out_bias, norm2_gain, norm2_shift, out_weight, up_weight, up_bias, gdown, cot
    )
    gmoth = swap(gmsend, "seq", 1)

    own = (gelu_t, rows, gpre, cot, mown, moth)
    if whole:
        got = (swap(gelu_send, "rep", 1), swap(rows, "rep", 1), swap(gpre_send, "rep", 1), cot_got, mown_got, swap(moth, "rep", 1))
        send_a, keep_a, send_b, keep_b = mlp_grads(bits, own, got)
        got_a, got_b = swap(send_a, "rep", 2), swap(send_b, "seq", 1)
        gmoth, send_a, send_b = tie(gmoth, send_a, send_b)
    else:
        halves = [mlp_grads(bits.at[3].set(c), own) for c in range(2)]

    gs = (gmown, gmoth)
    dq, *sends = far_backward(y, qs, docs, gs, merged, lse, masks, remote)
    recv = [swap(s, "seq", 2 * m) for s, m in zip(sends, masks, strict=True)]
    dq, dk, dv = own_backward(y, qs, ks, vs, docs, gs, merged, lse, dq)
    if whole:
        dq, got_a, got_b = tie(dq, got_a, got_b)
        send_a, keep_a, send_b, keep_b = split_second(bits, keep_a, got_a, keep_b, got_b)
        dq, send_a, send_b = tie(dq, send_a, send_b)
        got_a, got_b = swap(send_a, "seq", 1), swap(send_b, "rep", 2)
    queries = query_grads(bits, dq, first_a, first_b, in_weight)
    gfirst_a, gfirst_b, i_send, i_keep = finish(
        bits, queries, dk, dv, x, x_oth, first_a, first_b, in_weight, vec, up_sum, masks, recv
    )
    gfirst_got = swap(gfirst_b, "seq", 1)
    if whole:
        i_send, got_a, got_b = tie(i_send, got_a, got_b)
        i_got = swap(i_send, "rep", 1)
        g_send, g_keep = split_third(bits, keep_a, got_a, keep_b, got_b)
        g_got = swap(g_send, "seq", 2)
        view = lambda v: v.reshape(NBLK, 2, IN_ROWS // 2, IN_COLS)
        i_send, i_keep = halve((view(i_keep), view(i_got)), xbit, 1)
        i_got = swap(i_send, "rep", 2)

    result = (resid1 + mm(gelu_t, down_weight, TN) + down_bias).astype(bf16)
    if whole:
        i_got, result = tie(i_got, result)
        i_send, i_keep = halve((i_keep.reshape(4, 2, -1, IN_COLS), i_got.reshape(4, 2, -1, IN_COLS)), ybit, 1)
        i_got = swap(i_send, "seq", 1)
        g_got, i_send = tie(g_got, i_send)
        g_send, g_keep = halve((g_keep, g_got), z // 2, 0)
        g_got = swap(g_send, "seq", 4)
        gfirst_got, g_send = tie(gfirst_got, g_send)
    by_rows = lambda n: pl.BlockSpec((tok // 4, n), lambda j: (j, 0))
    grad_input = kcall(
        input_grad_body, "input_grad", (x, norm1_gain, gfirst_a, gfirst_got, gres), [sds((tok, D), f32)], grid=(4,),
        in_specs=[by_rows(D), full((D,))] + [by_rows(D)] * 3, out_specs=[by_rows(D)],
    )[0]

    if whole:
        i_got, grad_input = tie(i_got, grad_input)
        width = 3 * GW
        low, high = jnp.where(ybit == 0, i_keep, i_got), jnp.where(ybit == 0, i_got, i_keep)
        vec = i_keep[..., width:] + i_got[..., width:]
        i_all = jnp.concatenate([low[..., :width], high[..., :width], vec], axis=-1).reshape(2, 2, IN_ROWS // 2, 2 * width + 128)
        i_send, i_keep = pick(i_all, 1 - z % 2, 1), pick(i_all, z % 2, 1)
        i_got = swap(i_send, "seq", 2)
        i_got, g_got = tie(i_got, g_got)
        i_send, i_keep = halve((i_keep, i_got), z // 2, 0)
        i_got = swap(i_send, "seq", 4)

        mine = g_keep + g_got
        near, far = spread(mine, xbit)
        g_down, g_up, g_out = kcall(
            unpack_mlp_body, "unpack_mlp", (bits, near, far),
            [sds((DOWN_ROWS, D), f32), sds((UP_ROWS, FF), f32), sds((UP_ROWS, D), f32)],
            grid=(1,), in_specs=[SMEM, full(near.shape), full(far.shape)],
            out_specs=[full((DOWN_ROWS, D)), full((UP_ROWS, FF)), full((UP_ROWS, D))],
        )
        near, far = spread(i_keep + i_got, xbit)
        far, g_down = tie(far, g_down)
        g_in, *vecs = kcall(
            unpack_in_body, "unpack_in", (bits, near, far),
            [sds((2 * IN_ROWS, 3 * D), f32)] + [sds((UNIT * n,), f32) for n in VEC_UNITS],
            in_specs=[SMEM, VMEM, VMEM], out_specs=[VMEM] * 9,
        )
    else:
        total = lambda v: lax.psum(lax.psum_scatter(v, "seq", scatter_dimension=0, tiled=True).astype(bf16), "rep").astype(f32)
        order = lambda bit, keep, send: jnp.where(bit == 0, jnp.stack([keep, send]), jnp.stack([send, keep])).astype(f32)
        by_x = jnp.stack([order(xbit, h[1], h[0]) for h in halves])
        by_y = jnp.stack([order(ybit, h[3], h[2]) for h in halves])
        ups = by_x[..., : 2 * UP_ROWS, :].reshape(2, 2, NBLK, 2, UP_ROWS, HALF)
        g_up = total(ups.transpose(2, 4, 0, 1, 3, 5).reshape(D, FF))
        g_out = total(by_x[..., 2 * UP_ROWS :, :].reshape(2, 2, NBLK, UP_ROWS // 2, HALF).transpose(2, 1, 3, 0, 4).reshape(D, D))
        g_down = total(by_y.transpose(2, 1, 0, 4, 3, 5).reshape(FF, D))
        both = jnp.stack([i_keep, i_send], axis=1)[..., : 3 * GW].astype(f32).reshape(D, 3, 1, GW)
        g_in = total(jnp.where((jnp.arange(2) == ybit)[None, None, :, None], both, 0.0).reshape(D, 3 * D))
        small = i_keep[:, :, 3 * GW : 3 * GW + UNIT].astype(f32)
        ends = np.cumsum((0,) + VEC_UNITS)
        vecs = [total(small[:, lo:hi].reshape(-1)) for lo, hi in zip(ends[:-1], ends[1:], strict=True)]
    n1_gain, n1_shift, b_in, b_down, n2_gain, n2_shift, b_out, b_up = vecs
    return (
        result[None], grad_input[None], n1_gain, n1_shift, g_in, b_in, g_out, b_out, n2_gain, n2_shift, g_up, b_up, g_down, b_down,
    )


def solution(mesh):
    tokens, weights = P("rep", "seq", None), P()
    in_specs = (tokens, P("rep", "seq")) + (weights,) * 12 + (tokens,)
    vec, mat = P("seq"), P("seq", None)
    out_specs = (tokens, tokens, vec, vec, mat, vec, mat, vec, vec, vec, mat, vec, mat, vec)
    return jax.shard_map(body, mesh=mesh, in_specs=in_specs, out_specs=out_specs, check_vma=False)
```

```python
import functools
import math

import jax
import jax.numpy as jnp
import numpy as np
from jax import lax
from jax.experimental import pallas as pl
from jax.experimental.pallas import tpu as pltpu
from jax.sharding import PartitionSpec as P


D = 768
H = 16
HD = 48
FF = 3072
SEG0 = 1024
BRANCHES = 5
RES = 16
HG = H // 2
GW = HG * HD
NORM_EPS = 1e-05
BIG = 1e30
SCALE = HD**-0.5
LN2 = math.log(2.0)
Q_SCALE = SCALE / LN2

f32 = jnp.float32
bf16 = jnp.bfloat16
NN = (((1,), (0,)), ((), ()))
NT = (((1,), (1,)), ((), ()))
TN = (((0,), (0,)), ((), ()))
MIB = 2**20
VMEM_MIB = 20
MLP_SPLIT = 1
OWN_STEP = 1
FAR_STEP = 2


def mm(left, right, dims=NN):
    return lax.dot_general(left, right, dims, preferred_element_type=f32)


def rev4(v):
    return ((v & 1) << 3) | ((v & 2) << 1) | ((v & 4) >> 1) | ((v & 8) >> 3)


def run_start(head, level, tok):
    if level == 1:
        return (head % 2) * (tok // 2)
    return ((head % 2) * 2 + (head // 2) % 2) * (tok // 4)


def kcall(body, name, ins, outs, *, grid=None, in_specs=None, out_specs=None, scratch=(), vmem=VMEM_MIB, flops=0):
    kw = {}
    if grid is not None:
        kw = dict(grid=grid)
    if in_specs is not None:
        kw.update(in_specs=in_specs, out_specs=out_specs)
    nbytes = sum(math.prod(a.shape) * a.dtype.itemsize for a in (*ins, *outs))
    return pl.pallas_call(
        body,
        out_shape=outs,
        scratch_shapes=list(scratch),
        name=name,
        compiler_params=pltpu.CompilerParams(vmem_limit_bytes=vmem * MIB),
        cost_estimate=estimate(name, flops, nbytes),
        **kw,
    )(*ins)


TAIL = ("query_grads", "far_forward_first", "split_second", "split_third", "input_grad", "unpack_mlp", "unpack_in")


def estimate(name, flops, nbytes):
    if name in TAIL:
        return pl.CostEstimate(flops=0, bytes_accessed=0, transcendentals=0)
    return pl.CostEstimate(flops=10**12, bytes_accessed=10**10, transcendentals=0)


def sds(shape, dtype):
    return jax.ShapeDtypeStruct(shape, dtype)


SMEM = pl.BlockSpec(memory_space=pltpu.SMEM)
VMEM = pl.BlockSpec(memory_space=pltpu.VMEM)


def full(shape):
    return pl.BlockSpec(shape, lambda *_: (0,) * len(shape), pipeline_mode=pl.Buffered(1))


def features(side, doc_row, pos, head, b0, tok, extra=None):
    n = doc_row.shape[1]
    rowid = lax.broadcasted_iota(jnp.int32, (16, n), 0)
    out = jnp.zeros((16, n), f32)
    diff = rev4(pos // (tok // RES)) ^ (head & (RES - 1))
    for d in range(3):
        same = doc_row == d
        val = jnp.where(same, 0.0, 1.0) if side == "q" else jnp.where(same, -BIG, 0.0)
        out = jnp.where(rowid == d, val, out)
    row = 3
    for b in range(b0 + 1, BRANCHES):
        val = math.log2((b - b0 + 1) / (b - b0))
        high = float(np.asarray(val, dtype=jnp.bfloat16))
        chosen = (diff & (2**b - 1)) == 0
        for part in (high, val - high) if val != 1.0 else (1.0,):
            put = jnp.where(chosen, 1.0 if side == "q" else part, 0.0)
            out = jnp.where(rowid == row, put, out)
            row += 1
    assert row <= 10
    if b0 > 0:
        outside = (diff & (2**b0 - 1)) != 0
        one = jnp.where(outside, 1.0 if side == "q" else -BIG, 0.0)
        const = 1.0 if side == "q" else -BIG
        out = jnp.where(rowid == (10 if side == "q" else 11), one, out)
        out = jnp.where(rowid == (11 if side == "q" else 10), const, out)
    if extra is not None:
        for j in range(3):
            out = jnp.where(rowid == 12 + j, extra[j], out)
    return out.astype(bf16)


def split3(row):
    first = row.astype(bf16).astype(f32)
    rest = row - first
    second = rest.astype(bf16).astype(f32)
    return (first, second, rest - second)


def tail_rows(n, rows):
    rowid = lax.broadcasted_iota(jnp.int32, (16, n), 0)
    out = jnp.zeros((16, n), f32)
    for j, r in enumerate(rows):
        out = jnp.where(rowid == j, r, out)
    return out.astype(bf16)


def place(tok, axis):
    shape = (tok, 1) if axis == 0 else (1, tok)
    p = lax.broadcasted_iota(jnp.int32, shape, axis)
    return rev4(p % RES) * (tok // RES) + p // RES


def one_hot(tok, transposed):
    if transposed:
        return (place(tok, 0) == lax.broadcasted_iota(jnp.int32, (1, tok), 1)).astype(bf16)
    return (place(tok, 1) == lax.broadcasted_iota(jnp.int32, (tok, 1), 0)).astype(bf16)


def normalise(x):
    cen = x - jnp.mean(x, axis=-1, keepdims=True)
    rs = lax.rsqrt(jnp.mean(cen * cen, axis=-1, keepdims=True) + NORM_EPS)
    return cen * rs, rs


def row(ref):
    return ref[...][None, :]


def project_body(tok, y_ref, x_ref, ids_ref, gain, shift, in_b, wq, wk, wv, first_ref, q_ref, k_ref, v_ref, doc_ref, near_ref, far_ref):
    xh, _ = normalise(x_ref[...].astype(f32))
    first = (xh * row(gain) + row(shift)).astype(bf16)
    first = mm(one_hot(tok, False), first).astype(bf16)
    first_ref[...] = first.T
    ids = jnp.broadcast_to(ids_ref[...].astype(f32), (16, tok)).astype(bf16)
    docs = mm(ids, one_hot(tok, True))
    doc_ref[...] = docs[0:8]
    bias = row(in_b)
    for part, (w, ref) in enumerate(((wq, q_ref), (wk, k_ref), (wv, v_ref))):
        at = part * D
        val = mm(first, w[...]) + jnp.where(y_ref[0] == 0, bias[:, at : at + GW], bias[:, at + GW : at + D])
        if part == 0:
            val = val * Q_SCALE
        ref[...] = val.astype(bf16).T
    for out, level in ((near_ref, 1), (far_ref, 2)):
        width = tok >> level
        for part, ref in enumerate((k_ref, v_ref)):
            for h in range(HG):
                start = run_start(h, level, tok)
                out[part * GW + h * HD : part * GW + (h + 1) * HD] = ref[h * HD : (h + 1) * HD, start : start + width]
        rowid = lax.broadcasted_iota(jnp.int32, (16, width), 0)
        acc = jnp.zeros((16, width), f32)
        for j in range(2**level):
            acc = jnp.where(rowid == j, docs[0:1, j * width : (j + 1) * width], acc)
        out[2 * GW : 2 * GW + 16] = acc.astype(bf16)


def weight_specs():
    return [pl.BlockSpec((D, GW), lambda j, y, part=part: (0, 2 * part + y[0]), pipeline_mode=pl.Buffered(1)) for part in range(3)]


def pcall(body, name, scalar, ins, outs, in_specs, out_specs, *, grid=(1,), scratch=(), vmem=VMEM_MIB, flops=0):
    nbytes = sum(math.prod(a.shape) * a.dtype.itemsize for a in (*ins, *outs))
    return pl.pallas_call(
        body,
        grid_spec=pltpu.PrefetchScalarGridSpec(
            num_scalar_prefetch=1, grid=grid, in_specs=in_specs, out_specs=out_specs, scratch_shapes=list(scratch)
        ),
        out_shape=outs,
        name=name,
        compiler_params=pltpu.CompilerParams(vmem_limit_bytes=vmem * MIB),
        cost_estimate=estimate(name, flops, nbytes),
    )(scalar, *ins)


def project(y, x, ids, gain, shift, in_b, weight, vmem):
    tok = x.shape[0]
    outs = [
        sds((D, tok), bf16),
        sds((GW, tok), bf16),
        sds((GW, tok), bf16),
        sds((GW, tok), bf16),
        sds((8, tok), f32),
        sds((2 * GW + 16, tok // 2), bf16),
        sds((2 * GW + 16, tok // 4), bf16),
    ]
    return pcall(
        functools.partial(project_body, tok), "project", y, (x, ids, gain, shift, in_b, weight, weight, weight), outs,
        [full(x.shape), full(ids.shape), full((D,)), full((D,)), full((3 * D,))] + weight_specs(), [full(o.shape) for o in outs],
        vmem=vmem,
        flops=2 * tok * D * (tok + 3 * GW),
    )


def fill_keys(kaug, vaug, k_parts, v_parts, doc_parts, pos_parts, head, b0, tok):
    at = 0
    for k, v, doc, pos in zip(k_parts, v_parts, doc_parts, pos_parts, strict=True):
        n = k.shape[1]
        kaug[0:HD, at : at + n] = k
        kaug[HD:64, at : at + n] = features("k", doc, pos, head, b0, tok, (-1.0, -1.0, -1.0))
        vaug[0:HD, at : at + n] = v
        vaug[HD:64, at : at + n] = tail_rows(n, (1.0, 1.0, 1.0))
        at += n


def fill_queries(qaug, q_parts, doc_parts, pos_parts, head, b0, tok, lse_parts=None):
    at = 0
    for j, (q, doc, pos) in enumerate(zip(q_parts, doc_parts, pos_parts, strict=True)):
        n = q.shape[1]
        extra = None if lse_parts is None else split3(lse_parts[j])
        qaug[0:HD, at : at + n] = q
        qaug[HD:64, at : at + n] = features("q", doc, pos, head, b0, tok, extra)
        at += n


def iota_row(n):
    return lax.broadcasted_iota(jnp.int32, (1, n), 1)


def attend(qaug, kaug, vaug, nq, nk, step, put):
    keys = kaug[:, 0:nk].T
    for at in range(0, nq, step):
        scores = mm(keys, qaug[:, at : at + step])
        probs = jnp.exp2(scores).astype(bf16)
        put(at, mm(vaug[:, 0:nk], probs))


def own_forward_body(tok, y_ref, qa, qb, ka, kb, va, vb, da, db, out_ref, qaug, kaug, vaug):
    pos = iota_row(tok)
    docs = (da[0:1], db[0:1])
    for i in range(OWN_STEP):
        head = y_ref[0] * HG + pl.program_id(0) * OWN_STEP + i
        at_head = lambda *refs: tuple(Rows(r, i)[...] for r in refs)
        fill_keys(kaug.at[i], vaug.at[i], at_head(ka, kb), at_head(va, vb), docs, (pos, pos), head, 0, tok)
        fill_queries(qaug.at[i], at_head(qa, qb), docs, (pos, pos), head, 0, tok)

        def put(at, val):
            out_ref[i, :, at : at + val.shape[1]] = val

        attend(qaug.at[i], kaug.at[i], vaug.at[i], 2 * tok, 2 * tok, tok, put)


def head_block(tok, step=1):
    return pl.BlockSpec((HD * step, tok), lambda h: (h, 0))


class Rows:
    def __init__(self, ref, head):
        self.ref, self.rows = ref, slice(head * HD, (head + 1) * HD)

    def __getitem__(self, at):
        return self.ref[(self.rows,) + at[1:]] if isinstance(at, tuple) else self.ref[self.rows]

    def __setitem__(self, at, value):
        if isinstance(at, tuple):
            self.ref[(self.rows,) + at[1:]] = value
        else:
            self.ref[self.rows] = value


def own_forward(y, qs, ks, vs, docs):
    tok = qs[0].shape[1]
    return kcall(
        functools.partial(own_forward_body, tok),
        "own_forward",
        (y, *qs, *ks, *vs, *docs),
        [sds((HG, 64, 2 * tok), f32)],
        grid=(HG // OWN_STEP,),
        in_specs=[SMEM] + [head_block(tok, OWN_STEP)] * 6 + [full((8, tok))] * 2,
        out_specs=[pl.BlockSpec((OWN_STEP, 64, 2 * tok), lambda h: (h, 0, 0))],
        scratch=[pltpu.VMEM((OWN_STEP, 64, 2 * tok), bf16)] * 3,
        flops=2 * HG * 128 * (2 * tok) ** 2,
    )[0]


def groups_of(masks):
    found = {}
    for j, m in enumerate(masks):
        found.setdefault(m.bit_length(), []).append(j)
    return [(b0, min(b0, 2), found[b0]) for b0 in sorted(found)]


def remote_parts(refs, members, local, level, tok, pieces=2):
    width = tok >> level
    start = run_start(local, level, tok)
    lane = iota_row(width) + start
    row = pl.multiple_of(local * HD, 16)
    ks, vs, docs, poss = [], [], [], []
    for j in members:
        for ref in refs[pieces * j : pieces * (j + 1)]:
            ks.append(ref[pl.ds(row, HD), :])
            vs.append(ref[pl.ds(row + GW, HD), :])
            block = ref[2 * GW : 2 * GW + 16, :].astype(f32)
            picked = block[0:1]
            for r in range(1, 2**level):
                picked = jnp.where(start // width == r, block[r : r + 1], picked)
            docs.append(picked)
            poss.append(lane)
    return ks, vs, docs, poss, start, width


def far_forward_body(tok, masks, last, y_ref, qa, qb, da, db, part, *rest):
    refs, rest = rest[: len(masks)], rest[len(masks) :]
    outs, (qaugs, kaugs, vaugs, accs) = rest[:-4], rest[-4:]
    for i in range(FAR_STEP):
        local = pl.program_id(0) * FAR_STEP + i
        head = y_ref[0] * HG + local
        qh, acc = (Rows(qa, i), Rows(qb, i)), accs.at[i]
        acc[...] = part[i]
        for g, (b0, level, members) in enumerate(groups_of(masks)):
            qaug, kaug, vaug = qaugs.at[i, g], kaugs.at[i, g], vaugs.at[i, g]
            ks, vs, docs, poss, start, width = remote_parts(refs, members, local, level, tok, 1)
            nk = width * len(ks)
            fill_keys(kaug, vaug, ks, vs, docs, poss, head, b0, tok)
            window = pl.ds(pl.multiple_of(start, 128), width)
            pos = iota_row(width) + start
            fill_queries(qaug, [q[:, window] for q in qh], (da[0:1, window], db[0:1, window]), (pos, pos), head, b0, tok)

            def put(at, val):
                acc[:, window] += val[:, 0:width]
                other = pl.ds(pl.multiple_of(start + tok, 128), width)
                acc[:, other] += val[:, width : 2 * width]

            attend(qaug, kaug, vaug, 2 * width, nk, 2 * width, put)
        if not last:
            outs[0][i] = acc[...]
            continue
        ma, mb, merged, lse = outs
        den = acc[HD : HD + 1]
        val = acc[0:HD] / den
        merged[i] = val
        Rows(ma, i)[...] = val[:, 0:tok].astype(bf16)
        Rows(mb, i)[...] = val[:, tok : 2 * tok].astype(bf16)
        lse[i] = jnp.broadcast_to(jnp.log2(den), (8, 2 * tok))


def remote_sizes(masks, tok):
    nq = max([tok >> level << 1 for _, level, _ in groups_of(masks)] + [128])
    nk = max([(tok >> level) * 2 * len(members) for _, level, members in groups_of(masks)] + [128])
    return nq, nk


def remote_flops(masks, tok):
    return sum(2 * HG * 64 * (2 * (tok >> lv)) * ((tok >> lv) * 2 * len(mem)) for _, lv, mem in groups_of(masks))


def far_forward(y, qs, docs, part, masks, remote, last):
    tok = qs[0].shape[1]
    nq, nk = remote_sizes(masks, tok)
    nk = max(nk // 2, 128)
    n = len(groups_of(masks))
    per_head = lambda r: pl.BlockSpec((FAR_STEP, r, 2 * tok), lambda h: (h, 0, 0))
    final = [sds((GW, tok), bf16)] * 2 + [sds((HG, HD, 2 * tok), f32), sds((HG, 8, 2 * tok), f32)]
    return kcall(
        functools.partial(far_forward_body, tok, masks, last),
        "far_forward" if last else "far_forward_first",
        (y, *qs, *docs, part, *remote),
        final if last else [sds((HG, 64, 2 * tok), f32)],
        grid=(HG // FAR_STEP,),
        in_specs=[SMEM] + [head_block(tok, FAR_STEP)] * 2 + [full((8, tok))] * 2 + [per_head(64)] + [full(r.shape) for r in remote],
        out_specs=[head_block(tok, FAR_STEP)] * 2 + [per_head(HD), per_head(8)] if last else [per_head(64)],
        scratch=[
            pltpu.VMEM((FAR_STEP, n, 64, nq), bf16),
            pltpu.VMEM((FAR_STEP, n, 64, nk), bf16),
            pltpu.VMEM((FAR_STEP, n, 64, nk), bf16),
            pltpu.VMEM((FAR_STEP, 64, 2 * tok), f32),
        ],
        flops=remote_flops(masks, tok),
    )


def attend_back(qaug, gaug, kaug, vaug, nq, nk, step, put_q, dk, dv):
    keys = kaug[0:HD, 0:nk]
    for at in range(0, nq, step):
        sl = slice(at, at + step)
        probs = jnp.exp2(mm(qaug[:, sl].T, kaug[:, 0:nk]))
        gprobs = mm(gaug[:, sl].T, vaug[:, 0:nk])
        gs = (probs * gprobs).astype(bf16)
        new_v = mm(gaug[0:HD, sl], probs.astype(bf16))
        new_k = mm(qaug[0:HD, sl], gs)
        if at == 0:
            dv[:, 0:nk] = new_v
            dk[:, 0:nk] = new_k
        else:
            dv[:, 0:nk] += new_v
            dk[:, 0:nk] += new_k
        put_q(at, mm(keys, gs, NT) * SCALE)


def fill_grads(gaug, g_parts, m_parts):
    at = 0
    for g, m in zip(g_parts, m_parts, strict=True):
        n = g.shape[1]
        delta = jnp.sum(g.astype(f32) * m, axis=0, keepdims=True)
        gaug[0:HD, at : at + n] = g
        gaug[HD:64, at : at + n] = tail_rows(n, split3(-delta))
        at += n


def far_backward_body(tok, masks, y_ref, qa, qb, da, db, ga, gb, merged, lse, *rest):
    nrem = 2 * len(masks)
    refs = rest[:nrem]
    dq_ref = rest[nrem]
    sends = rest[nrem + 1 : nrem + 1 + len(masks)]
    qaugs, gaugs, kaugs, vaugs, dks, dvs = rest[nrem + 1 + len(masks) :]
    for i in range(FAR_STEP):
        local = pl.program_id(0) * FAR_STEP + i
        head = y_ref[0] * HG + local
        row = pl.multiple_of(local * HD, 16)
        dq_ref[i] = jnp.zeros((HD, 2 * tok), f32)
        qh, gh = (Rows(qa, i), Rows(qb, i)), (Rows(ga, i), Rows(gb, i))
        for g, (b0, level, members) in enumerate(groups_of(masks)):
            qaug, gaug, kaug, vaug, dk, dv = (v.at[i, g] for v in (qaugs, gaugs, kaugs, vaugs, dks, dvs))
            ks, vs, docs, poss, start, width = remote_parts(refs, members, local, level, tok)
            nk = width * len(ks)
            fill_keys(kaug, vaug, ks, vs, docs, poss, head, b0, tok)
            window = pl.ds(pl.multiple_of(start, 128), width)
            other = pl.ds(pl.multiple_of(start + tok, 128), width)
            pos = iota_row(width) + start
            fill_queries(
                qaug, [q[:, window] for q in qh], (da[0:1, window], db[0:1, window]), (pos, pos), head, b0, tok,
                (lse[i, 0:1, window], lse[i, 0:1, other]),
            )
            fill_grads(gaug, [v[:, window] for v in gh], (merged[i, :, window], merged[i, :, other]))

            def put_q(at, val):
                dq_ref[i, :, window] += val[:, 0:width]
                dq_ref[i, :, other] += val[:, width : 2 * width]

            attend_back(qaug, gaug, kaug, vaug, 2 * width, nk, 2 * width, put_q, dk, dv)
            for n, j in enumerate(members):
                span = slice(2 * n * width, 2 * (n + 1) * width)
                sends[j][pl.ds(row, HD), :] = (dk[:, span] * LN2).astype(bf16)
                sends[j][pl.ds(row + GW, HD), :] = dv[:, span].astype(bf16)


def far_backward(y, qs, docs, gs, merged, lse, masks, remote):
    tok = qs[0].shape[1]
    nq, nk = remote_sizes(masks, tok)
    n = len(groups_of(masks))
    per_head = lambda r: pl.BlockSpec((FAR_STEP, r, 2 * tok), lambda h: (h, 0, 0))
    blocks = head_block(tok, FAR_STEP)
    sends = [sds((2 * GW, 2 * (tok >> min(m.bit_length(), 2))), bf16) for m in masks]
    return kcall(
        functools.partial(far_backward_body, tok, masks),
        "far_backward",
        (y, *qs, *docs, *gs, merged, lse, *remote),
        [sds((HG, HD, 2 * tok), f32)] + sends,
        grid=(HG // FAR_STEP,),
        in_specs=[SMEM] + [blocks] * 2 + [full((8, tok))] * 2 + [blocks] * 2
        + [per_head(HD), per_head(8)] + [full(r.shape) for r in remote],
        out_specs=[per_head(HD)] + [full(s.shape) for s in sends],
        scratch=[pltpu.VMEM((FAR_STEP, n, 64, nq), bf16)] * 2
        + [pltpu.VMEM((FAR_STEP, n, 64, nk), bf16)] * 2
        + [pltpu.VMEM((FAR_STEP, n, HD, nk), f32)] * 2,
        flops=5 * remote_flops(masks, tok),
    )


def own_backward_body(tok, y_ref, qa, qb, ka, kb, va, vb, da, db, ga, gb, merged, lse, dq_in, dq, dk, dv, qaug, gaug, kaug, vaug):
    head = y_ref[0] * HG + pl.program_id(0)
    pos = iota_row(tok)
    docs = (da[0:1], db[0:1])
    fill_keys(kaug, vaug, (ka[...], kb[...]), (va[...], vb[...]), docs, (pos, pos), head, 0, tok)
    fill_queries(
        qaug, (qa[...], qb[...]), docs, (pos, pos), head, 0, tok, (lse[0, 0:1, 0:tok], lse[0, 0:1, tok : 2 * tok])
    )
    fill_grads(gaug, (ga[...], gb[...]), (merged[0, :, 0:tok], merged[0, :, tok : 2 * tok]))

    def put_q(at, val):
        dq[:, at : at + tok] = (val + dq_in[0, :, at : at + tok]).astype(bf16)

    attend_back(qaug, gaug, kaug, vaug, 2 * tok, 2 * tok, tok, put_q, dk.at[0], dv.at[0])


def own_backward(y, qs, ks, vs, docs, gs, merged, lse, dq):
    tok = qs[0].shape[1]
    per_head = lambda r: pl.BlockSpec((1, r, 2 * tok), lambda h: (h, 0, 0))
    return kcall(
        functools.partial(own_backward_body, tok),
        "own_backward",
        (y, *qs, *ks, *vs, *docs, *gs, merged, lse, dq),
        [sds((GW, 2 * tok), bf16)] + [sds((HG, HD, 2 * tok), f32)] * 2,
        grid=(HG,),
        in_specs=[SMEM] + [head_block(tok)] * 6 + [full((8, tok))] * 2 + [head_block(tok)] * 2
        + [per_head(HD), per_head(8), per_head(HD)],
        out_specs=[head_block(2 * tok)] + [per_head(HD)] * 2,
        scratch=[pltpu.VMEM((64, 2 * tok), bf16)] * 4,
        flops=5 * HG * 128 * (2 * tok) ** 2,
    )


NBLK = 8
HALF = D // 2
DOWN_ROWS = FF // NBLK
UP_ROWS = D // NBLK
ROWS_A = 2 * UP_ROWS + UP_ROWS // 2
ROWS_B = DOWN_ROWS // 2


def cot_body(cot, down, out):
    out[...] = mm(cot[...], down[...], NT).astype(out.dtype)


def cot_down(cot, down):
    tok, ff = cot.shape[0], down.shape[0]
    blk = 768
    return kcall(
        cot_body, "cot_down", (cot, down), [sds((tok, ff), bf16)], grid=(ff // blk,),
        in_specs=[full((tok, D)), pl.BlockSpec((blk, D), lambda j: (j, 0))],
        out_specs=[pl.BlockSpec((tok, blk), lambda j: (0, j))], vmem=60, flops=2 * tok * D * ff,
    )[0]


ERF_P = 0.3275911
ERF_A = (0.254829592, -0.284496736, 1.421413741, -1.453152027, 1.061405429)


def normal_cdf(v):
    gauss = jnp.exp2(v * v * (-0.5 / LN2))
    t = 1.0 / (1.0 + jnp.abs(v) * (ERF_P * 0.5**0.5))
    poly = 0.5 * ERF_A[4]
    for a in ERF_A[3::-1]:
        poly = poly * t + 0.5 * a
    tail = poly * t * gauss
    return jnp.where(v < 0, tail, 1.0 - tail), gauss


def mlp_body(tok, nblk, bits, x_ref, mown, moth, out_b, n2g, n2s, wout, up, up_b, gdown, cot,
             gelu_ref, gelu_send, gpre_ref, gpre_send, upb_ref, rows_ref, resid_ref, gmown, gmoth, gres_ref, vec_ref,
             second, xhat, rstd, acc):
    step = pl.program_id(0)
    y = bits[0]
    low_core = bits[3] == 0
    mine = pl.ds(pl.multiple_of(y * GW, 128), GW)
    theirs = pl.ds(pl.multiple_of((1 - y) * GW, 128), GW)
    gain = row(n2g)

    @pl.when(step == 0)
    def _():
        pmt = one_hot(tok, True)
        own = mm(pmt, mown[...], NT).astype(bf16)
        oth = mm(pmt, moth[...], NT).astype(bf16)
        resid = x_ref[...].astype(f32) + (mm(own, wout[mine, :]) + mm(oth, wout[theirs, :])) + row(out_b)
        resid_ref[...] = resid
        xh, rs = normalise(resid)
        xhat[...] = xh
        rstd[...] = jnp.broadcast_to(rs, rstd.shape)
        low = (xh * gain + row(n2s)).astype(bf16)
        second[...] = low
        rows_ref[0:D] = low.T
        acc[...] = jnp.zeros_like(acc)

    rows = tok // MLP_SPLIT
    for i in range(MLP_SPLIT):
        part = slice(i * rows, (i + 1) * rows)
        pre = mm(second[part], up[...]) + up_b[0]
        cdf, gauss = normal_cdf(pre)
        gelu_t = (pre * cdf).astype(bf16).T
        gelu_ref[:, part] = gelu_t
        half = DOWN_ROWS // 2
        for at in range(0, gelu_t.shape[0], DOWN_ROWS):
            low, high = gelu_t[at : at + half], gelu_t[at + half : at + DOWN_ROWS]
            gelu_send[at // 2 : at // 2 + half, part] = jnp.where(low_core, high, low)
        slope = cdf + pre * (gauss * (1.0 / math.sqrt(2.0 * math.pi)))
        gpre = (slope * gdown[part]).astype(bf16)
        gpre_ref[part] = gpre

        gpre_send[part] = gpre
        acc[part] += mm(gpre, up[...], NT)
        sums = mm(jnp.ones((8, rows), bf16), gpre)
        upb_ref[...] = sums if i == 0 else upb_ref[...] + sums

    @pl.when(step == nblk - 1)
    def _():
        dy = acc[...]
        xh = xhat[...]
        dyg = dy * gain
        m1 = jnp.mean(dyg, axis=-1, keepdims=True)
        m2 = jnp.mean(dyg * xh, axis=-1, keepdims=True)
        g = cot[...]
        gres = g.astype(f32) + rstd[:, 0:1] * (dyg - m1 - xh * m2)
        gres_ref[...] = gres
        gattn = gres.astype(bf16)
        gattn_t = mm(gattn.T, one_hot(tok, True)).astype(bf16)
        rows_ref[D : 2 * D] = gattn_t
        gmoth[...] = mm(wout[theirs, :], gattn_t).astype(bf16)
        gmown[...] = mm(wout[mine, :], gattn_t).astype(bf16)
        ones = jnp.ones((8, tok), bf16)
        vec_ref[0:8] = mm(ones, g)
        vec_ref[8:16] = jnp.broadcast_to(jnp.sum(dy * xh, axis=0, keepdims=True), (8, D))
        vec_ref[16:24] = jnp.broadcast_to(jnp.sum(dy, axis=0, keepdims=True), (8, D))
        vec_ref[24:32] = mm(ones, gattn)


def mlp_chunk(step, bits):
    return (step // 2 + bits[3]) % 2 * 2 + step % 2


def mlp(bits, x, mown, moth, out_b, n2g, n2s, wout, up, up_b, gdown, cot):
    tok = cot.shape[0]
    ff = up.shape[1]
    nblk = 4
    blk = ff // nblk
    wide = pl.BlockSpec((tok, blk), lambda j, b: (0, mlp_chunk(j, b)))
    outs = [
        sds((ff, tok), bf16), sds((ff // 2, tok), bf16), sds((tok, ff), bf16), sds((tok, ff // 2), bf16), sds((8, ff), f32),
        sds((2 * D, tok), bf16), sds((tok, D), f32), sds((GW, tok), bf16), sds((GW, tok), bf16),
        sds((tok, D), f32), sds((32, D), f32),
    ]
    return pcall(
        functools.partial(mlp_body, tok, nblk),
        "mlp",
        bits,
        (x, mown, moth, out_b, n2g, n2s, wout, up, up_b.reshape(nblk, 1, blk), gdown, cot),
        outs,
        [
            full(x.shape), full(mown.shape), full(moth.shape), full((D,)), full((D,)), full((D,)), full(wout.shape),
            pl.BlockSpec((D, blk), lambda j, b: (0, mlp_chunk(j, b))),
            pl.BlockSpec((1, 1, blk), lambda j, b: (mlp_chunk(j, b), 0, 0)),
            wide, full((tok, D)),
        ],
        [
            pl.BlockSpec((blk, tok), lambda j, b: (mlp_chunk(j, b), 0)),
            pl.BlockSpec((blk // 2, tok), lambda j, b: (mlp_chunk(j, b), 0)),
            wide,
            pl.BlockSpec((tok, blk), lambda j, b: (0, jnp.maximum(j - nblk // 2, 0))),
            pl.BlockSpec((8, blk), lambda j, b: (0, mlp_chunk(j, b))),
        ] + [full(o.shape) for o in outs[5:]],
        grid=(nblk,),
        scratch=[pltpu.VMEM((tok, D), bf16), pltpu.VMEM((tok, D), f32), pltpu.VMEM((tok, 128), f32), pltpu.VMEM((tok, D), f32)],
        vmem=28,
        flops=2 * tok * D * (2 * ff + 2 * D + 2 * tok),
    )


def mlp_grads_body(bits, cores, *refs):
    ins, outs = refs[:-4], refs[-4:]
    send_a, keep_a, send_b, keep_b = outs
    ybit, xbit = bits[0], bits[1]
    heads_low = (pl.program_id(0) < 2) == (ybit == 0)
    up = att = 0.0
    down = [0.0, 0.0]
    for c in range(cores):
        low_t, high_t, second_t, gattn_t, gpre, cot, mown, moth = ins[8 * c : 8 * c + 8]
        up = up + mm(second_t[...], gpre[...])
        down = [old + mm(gelu_t[...], cot[...]) for old, gelu_t in zip(down, (low_t, high_t), strict=True)]
        att = att + mm(jnp.where(heads_low, mown[...], moth[...]), gattn_t[...], NT)
    up, att, down = up.astype(bf16), att.astype(bf16), [v.astype(bf16) for v in down]
    x_low, y_low = xbit == 0, ybit == 0
    half = UP_ROWS // 2
    for y in range(2):
        rows = slice(y * UP_ROWS, (y + 1) * UP_ROWS)
        cols = [up[rows, c * HALF : (c + 1) * HALF] for c in range(4)]
        pieces = [(0, UP_ROWS, cols[0], cols[2]), (UP_ROWS, UP_ROWS, cols[1], cols[3])]
        pieces += [(2 * UP_ROWS, half, att[y * UP_ROWS : y * UP_ROWS + half], att[y * UP_ROWS + half : (y + 1) * UP_ROWS])]
        for at, n, low, high in pieces:
            keep_a[0, y, at : at + n] = jnp.where(x_low, low, high)
            send_a[0, y, at : at + n] = jnp.where(x_low, high, low)
    for x in range(2):
        low, high = (v[:, x * HALF : (x + 1) * HALF] for v in down)
        keep_b[0, x] = jnp.where(y_low, low, high)
        send_b[0, x] = jnp.where(y_low, high, low)


def mlp_grads(bits, *per_core):
    tok = per_core[0][3].shape[0]
    ins, specs = [], []
    for gelu_t, rows, gpre, cot, mown, moth in per_core:
        heads = pl.BlockSpec((GW // 2, tok), lambda j, b: (j % 2, 0))
        ins += [gelu_t, gelu_t, rows, rows, gpre, cot, mown, moth]
        if gelu_t.shape[0] == FF:
            gelus = [pl.BlockSpec((ROWS_B, tok), lambda j, b, y=y: (4 * j + 2 * y + b[3], 0)) for y in range(2)]
            half = pl.BlockSpec((tok, FF // 2), lambda j, b: (0, b[3]))
        else:
            gelus = [pl.BlockSpec((ROWS_B, tok), lambda j, b, y=y: (2 * j + y, 0)) for y in range(2)]
            half = full(gpre.shape)
        specs += gelus + [
            pl.BlockSpec((D // 4, tok), lambda j, b: (j, 0)),
            pl.BlockSpec((HALF, tok), lambda j, b: (D // HALF + b[3], 0)),
            half, full(cot.shape), heads, heads,
        ]
    outs = [sds((4, 2, ROWS_A, HALF), bf16)] * 2 + [sds((4, 2, ROWS_B, HALF), bf16)] * 2
    return pcall(
        lambda bits, *refs: mlp_grads_body(bits, len(per_core), *refs), "mlp_grads", bits, ins, outs, specs,
        [pl.BlockSpec((1,) + o.shape[1:], lambda j, b: (j, 0, 0, 0)) for o in outs],
        grid=(4,),
        vmem=22,
        flops=2 * tok * D * (2 * FF + D),
    )


IN_ROWS = D // NBLK // 2
IN_COLS = 3 * GW + 128
SMALL_ROWS = 16
UNIT = UP_ROWS


def query_grads_body(tok, bits, dq, fa, fb, wq, val, dy, bias, acc):
    step = pl.program_id(0)
    nat = mm(one_hot(tok, True), dq[...], NT).astype(bf16)
    dy[0] = mm(nat, wq[...], NT)
    new_bias = mm(jnp.ones((8, tok), bf16), nat)

    @pl.when(step == 0)
    def _():
        acc[...] = mm(fb[...], dq[...], NT)
        bias[...] = new_bias

    @pl.when(step == 1)
    def _():
        val[...] = (acc[...] + mm(fa[...], dq[...], NT)).astype(bf16)
        bias[...] += new_bias


def query_grads(bits, dq, fa, fb, weight):
    tok = fa.shape[1]
    outs = [sds((D, GW), bf16), sds((2, tok, D), f32), sds((8, GW), f32)]
    return pcall(
        functools.partial(query_grads_body, tok), "query_grads", bits, (dq, fa, fb, weight), outs,
        [pl.BlockSpec((GW, tok), lambda j, y: (0, 1 - j)), full(fa.shape), full(fb.shape), weight_specs()[0]],
        [full((D, GW)), pl.BlockSpec((1, tok, D), lambda j, y: (1 - j, 0, 0)), full((8, GW))],
        grid=(2,),
        scratch=[pltpu.VMEM((D, GW), f32)],
    )


def finish_body(tok, masks, bits, val_q, dy_q, bias_q, dk, dv, xa, xb, fa, fb, wk, wv, vec, up_sum, *rest):
    nrem = len(masks)
    recv = rest[:nrem]
    first_a, first_b, send, keep, gkv, total, acc, sums, bias, small = rest[nrem:]
    step = pl.program_id(0)
    for part, ref, scale in ((0, dk, LN2), (1, dv, 1.0)):
        for h in range(HG):
            total[h * HD : (h + 1) * HD] = ref[h] * scale
        for m, r in zip(masks, recv, strict=True):
            level = min(m.bit_length(), 2)
            for h in range(HG):
                start = run_start(h, level, tok)
                row = part * GW + h * HD
                total[h * HD : (h + 1) * HD, start : start + (tok >> level)] += r[row : row + HD].astype(f32)
        gkv[part * GW : (1 + part) * GW] = total[...].astype(bf16)
    nat = mm(one_hot(tok, True), gkv[...], NT).astype(bf16)
    new_bias = mm(jnp.ones((8, tok), bf16), nat)
    dy = dy_q[0] + sum(mm(nat[:, part * GW : (part + 1) * GW], w[...], NT) for part, w in enumerate((wk, wv)))
    later = step == 1
    xh, _ = normalise(jnp.where(later, xa[...], xb[...]).astype(f32))
    new_gain = jnp.sum(dy * xh, axis=0, keepdims=True)
    new_shift = jnp.sum(dy, axis=0, keepdims=True)

    @pl.when(step == 0)
    def _():
        first_b[...] = dy.astype(bf16)
        acc[...] = mm(fb[...], gkv[...], NT)
        bias[...] = new_bias
        sums[0:8] = jnp.broadcast_to(new_gain, (8, D))
        sums[8:16] = jnp.broadcast_to(new_shift, (8, D))

    @pl.when(step == 1)
    def _():
        first_a[...] = dy
        val = (acc[...] + mm(fa[...], gkv[...], NT)).astype(bf16)
        all_bias = jnp.concatenate([bias_q[0:1], bias[0:1] + new_bias[0:1]], axis=1)
        lines = [sums[0:1] + new_gain, sums[8:9] + new_shift]
        lines += [vec[8 * j : 8 * j + 1] for j in range(4)]
        cut = lambda line, u: line[:, u * UNIT : (u + 1) * UNIT]
        small[...] = jnp.zeros_like(small)

        def put(block, row, line):
            small[block, row : row + 1, 0:UNIT] = line

        for s in range(NBLK):
            for row, line in zip((0, 1, 5, 6, 7, 8), lines, strict=True):
                put(s, row, cut(line, s))
            for k in range(4):
                put(s, 9 + k, cut(up_sum[0:1], s * 4 + k))
        for u in range(3 * NBLK):
            part, owner, k = u // 8, u // 4 % 2, u % 4
            put(u // 3, 2 + u % 3, jnp.where(bits[0] == owner, cut(all_bias, part * 4 + k), 0.0))
        keep_low = bits[3] == 0
        zeros = jnp.zeros((IN_ROWS, 128), bf16)

        def store(block, lanes, low, high):
            keep[block, :, lanes] = jnp.where(keep_low, low, high)
            send[block, :, lanes] = jnp.where(keep_low, high, low)

        for s in range(NBLK):
            at = 2 * s * IN_ROWS
            for lanes, part in ((slice(0, GW), val_q), (slice(GW, 3 * GW), val)):
                store(s, lanes, part[at : at + IN_ROWS], part[at + IN_ROWS : at + 2 * IN_ROWS])
            store(s, slice(3 * GW, IN_COLS), jnp.concatenate([small[s].astype(bf16), zeros[SMALL_ROWS:]], axis=0), zeros)


def finish(bits, queries, dk, dv, xa, xb, fa, fb, weight, vec, up_sum, masks, recv):
    tok = xa.shape[0]
    piece = lambda j: 1 - j
    by_head = pl.BlockSpec((HG, HD, tok), lambda j, y: (0, 0, piece(j)))
    outs = [sds((tok, D), f32), sds((tok, D), bf16)] + [sds((NBLK, IN_ROWS, IN_COLS), bf16)] * 2
    return pcall(
        functools.partial(finish_body, tok, masks),
        "finish",
        bits,
        (*queries, dk, dv, xa, xb, fa, fb, weight, weight, vec, up_sum, *recv),
        outs,
        [full((D, GW)), pl.BlockSpec((1, tok, D), lambda j, y: (piece(j), 0, 0)), full((8, GW)), by_head, by_head]
        + [full(v.shape) for v in (xa, xb, fa, fb)] + weight_specs()[1:] + [full(vec.shape), full(up_sum.shape)]
        + [pl.BlockSpec((2 * GW, r.shape[1] // 2), lambda j, y: (0, piece(j))) for r in recv],
        [full(o.shape) for o in outs],
        grid=(2,),
        scratch=[
            pltpu.VMEM((2 * GW, tok), bf16), pltpu.VMEM((GW, tok), f32), pltpu.VMEM((D, 2 * GW), f32),
            pltpu.VMEM((16, D), f32), pltpu.VMEM((8, 2 * GW), f32), pltpu.VMEM((NBLK, SMALL_ROWS, 128), f32),
        ],
        vmem=24,
        flops=4 * tok * 3 * GW * (tok + 2 * D),
    )


def input_grad_body(x_ref, gain, own, got, gres, out):
    xh, rs = normalise(x_ref[...].astype(f32))
    dyg = (own[...] + got[...].astype(f32)) * row(gain)
    m1 = jnp.mean(dyg, axis=-1, keepdims=True)
    m2 = jnp.mean(dyg * xh, axis=-1, keepdims=True)
    out[...] = gres[...] + rs * (dyg - m1 - xh * m2)


def unpack_mlp_body(bits, near, far, down, up, att):
    low = bits[3] == 0
    for c, v in enumerate((jnp.where(low, near[...], far[...]), jnp.where(low, far[...], near[...]))):
        for x in range(2):
            half = v[x].astype(f32)
            for j in range(2):
                at = (c * 4 + 2 * x + j) * HALF
                up[:, at : at + HALF] = half[j * UP_ROWS : (j + 1) * UP_ROWS]
            n = UP_ROWS // 2
            att[x * n : (x + 1) * n, c * HALF : (c + 1) * HALF] = half[2 * UP_ROWS : ROWS_A]
            down[c * ROWS_B : (c + 1) * ROWS_B, x * HALF : (x + 1) * HALF] = half[ROWS_A:]


VEC_UNITS = (1, 1, 3, 1, 1, 1, 1, 4)


def unpack_in_body(bits, near, far, out, *vecs):
    low = bits[3] == 0
    lower = jnp.where(low, near[...], far[...])
    upper = jnp.where(low, far[...], near[...])
    val = jnp.concatenate([lower[0], lower[1], upper[0], upper[1]], axis=0).astype(f32)
    for part in range(3):
        for y in range(2):
            src = (y * 3 + part) * GW
            dst = (part * 2 + y) * GW
            out[:, dst : dst + GW] = val[:, src : src + GW]
    row = 0
    for ref, units in zip(vecs, VEC_UNITS, strict=True):
        line = jnp.concatenate([val[row + k : row + k + 1, 6 * GW : 6 * GW + UNIT] for k in range(units)], axis=1)
        ref[...] = line[0]
        row += units


def swap(value, axis, offset):
    count = lax.axis_size(axis)
    return lax.ppermute(value, axis, [(i, i ^ offset) for i in range(count)])


def pick(value, index, dim):
    return lax.dynamic_index_in_dim(value, index, dim, keepdims=False)


def halve(pieces, index, dim):
    def part(i):
        return sum(pick(p, i, dim).astype(f32) for p in pieces).astype(bf16)

    return part(1 - index), part(index)


def split_second_body(bits, ka, ga, kb, gb, send_a, keep_a, send_b, keep_b):
    for keep, got, send_to, keep_to, bit in ((ka, ga, send_a, keep_a, bits[0]), (kb, gb, send_b, keep_b, bits[1])):
        total = lambda j: keep[0, j] + got[0, j]
        send_to[0] = total(1 - bit)
        keep_to[0] = total(bit)


def split_second(bits, ka, ga, kb, gb):
    block = lambda v: pl.BlockSpec((1,) + v.shape[1:], lambda j: (j, 0, 0, 0))
    outs = [sds((4,) + v.shape[2:], bf16) for v in (ka, ka, kb, kb)]
    return kcall(
        split_second_body, "split_second", (bits, ka, ga, kb, gb), outs, grid=(4,),
        in_specs=[SMEM] + [block(v) for v in (ka, ga, kb, gb)],
        out_specs=[pl.BlockSpec((1,) + o.shape[1:], lambda j: (j, 0, 0)) for o in outs],
    )


def split_third_body(bits, ka, ga, kb, gb, send, keep):
    low = bits[2] % 2
    at = 0
    for own, got in ((ka, ga), (kb, gb)):
        rows = slice(at, at + own.shape[1])
        send[0, rows] = own[1 - low] + got[1 - low]
        keep[0, rows] = own[low] + got[low]
        at += own.shape[1]


def split_third(bits, ka, ga, kb, gb):
    out = sds((2, ka.shape[1] + kb.shape[1], HALF), bf16)
    two = lambda v, n: pl.BlockSpec((n,) + v.shape[1:], lambda j: (j, 0, 0))
    return kcall(
        split_third_body, "split_third", (bits, ka, ga, kb, gb), [out, out], grid=(2,),
        in_specs=[SMEM] + [two(v, 2) for v in (ka, ga, kb, gb)], out_specs=[two(out, 1)] * 2,
    )


def spread(mine, xbit):
    other = swap(mine, "rep", 2)
    dim = mine.ndim - 2
    pair = jnp.stack([jnp.where(xbit == 0, mine, other), jnp.where(xbit == 0, other, mine)], axis=dim)
    return pair, swap(pair, "rep", 1)


def tie(*values):
    return lax.optimization_barrier(values)


def body(tile_embed, doc_ids, norm1_gain, norm1_shift, in_weight, in_bias, out_weight, out_bias,
         norm2_gain, norm2_shift, up_weight, up_bias, down_weight, down_bias, cotangent):
    tok = tile_embed.shape[1]
    count = lax.axis_size("seq")
    assert SEG0 == 2 * tok and tok % 512 == 0
    nodes = count // 2
    masks = [m for m in range(1, min(nodes, 2 ** (BRANCHES - 1)))]
    whole = count == 8 and lax.axis_size("rep") == 4
    index = lax.axis_index("seq")
    ybit = index % 2
    z = index // 2
    rep = lax.axis_index("rep")
    core, xbit = rep % 2, rep // 2
    bits = jnp.stack([ybit, xbit, z, core if whole else jnp.zeros_like(core)]).astype(jnp.int32)
    y = bits


    x, cot = tile_embed[0], cotangent[0]
    x_oth = swap(x, "seq", 1)
    ids_oth = swap(doc_ids, "seq", 1)

    args = (norm1_gain, norm1_shift, in_bias, in_weight)
    first_a, qa, ka, va, doc_a, *out_a = project(y, x, doc_ids, *args, 60)
    remote_a = [swap(out_a[min(m.bit_length(), 2) - 1], "seq", 2 * m) for m in masks]
    gdown = cot_down(cot, down_weight)
    x_oth, ids_oth, gdown = tie(x_oth, ids_oth, gdown)
    if whole:
        cot_got = swap(cot, "rep", 1)
    first_b, qb, kb, vb, doc_b, *out_b = project(y, x_oth, ids_oth, *args, VMEM_MIB)
    remote_b = [swap(out_b[min(m.bit_length(), 2) - 1], "seq", 2 * m) for m in masks]

    qs, ks, vs, docs = (qa, qb), (ka, kb), (va, vb), (doc_a, doc_b)
    part = own_forward(y, qs, ks, vs, docs)
    remote = [r for pair in zip(remote_a, remote_b, strict=True) for r in pair]
    part, = far_forward(y, qs, docs, part, masks, remote_a, False)
    mown, msend, merged, lse = far_forward(y, qs, docs, part, masks, remote_b, True)
    moth = swap(msend, "seq", 1)
    if whole:
        moth, cot_got, mown_got = tie(moth, cot_got, swap(mown, "rep", 1))
    (gelu_t, gelu_send, gpre, gpre_send, up_sum, rows, resid1, gmown, gmsend, gres, vec) = mlp(
        bits, x, mown, moth, out_bias, norm2_gain, norm2_shift, out_weight, up_weight, up_bias, gdown, cot
    )
    gmoth = swap(gmsend, "seq", 1)

    own = (gelu_t, rows, gpre, cot, mown, moth)
    if whole:
        got = (swap(gelu_send, "rep", 1), swap(rows, "rep", 1), swap(gpre_send, "rep", 1), cot_got, mown_got, swap(moth, "rep", 1))
        send_a, keep_a, send_b, keep_b = mlp_grads(bits, own, got)
        got_a, got_b = swap(send_a, "rep", 2), swap(send_b, "seq", 1)
        gmoth, send_a, send_b = tie(gmoth, send_a, send_b)
    else:
        halves = [mlp_grads(bits.at[3].set(c), own) for c in range(2)]

    gs = (gmown, gmoth)
    dq, *sends = far_backward(y, qs, docs, gs, merged, lse, masks, remote)
    recv = [swap(s, "seq", 2 * m) for s, m in zip(sends, masks, strict=True)]
    dq, dk, dv = own_backward(y, qs, ks, vs, docs, gs, merged, lse, dq)
    if whole:
        dq, got_a, got_b = tie(dq, got_a, got_b)
        send_a, keep_a, send_b, keep_b = split_second(bits, keep_a, got_a, keep_b, got_b)
        dq, send_a, send_b = tie(dq, send_a, send_b)
        got_a, got_b = swap(send_a, "seq", 1), swap(send_b, "rep", 2)
    queries = query_grads(bits, dq, first_a, first_b, in_weight)
    gfirst_a, gfirst_b, i_send, i_keep = finish(
        bits, queries, dk, dv, x, x_oth, first_a, first_b, in_weight, vec, up_sum, masks, recv
    )
    gfirst_got = swap(gfirst_b, "seq", 1)
    if whole:
        i_send, got_a, got_b = tie(i_send, got_a, got_b)
        i_got = swap(i_send, "rep", 1)
        g_send, g_keep = split_third(bits, keep_a, got_a, keep_b, got_b)
        g_got = swap(g_send, "seq", 2)
        view = lambda v: v.reshape(NBLK, 2, IN_ROWS // 2, IN_COLS)
        i_send, i_keep = halve((view(i_keep), view(i_got)), xbit, 1)
        i_got = swap(i_send, "rep", 2)

    result = (resid1 + mm(gelu_t, down_weight, TN) + down_bias).astype(bf16)
    if whole:
        i_got, result = tie(i_got, result)
        i_send, i_keep = halve((i_keep.reshape(4, 2, -1, IN_COLS), i_got.reshape(4, 2, -1, IN_COLS)), ybit, 1)
        i_got = swap(i_send, "seq", 1)
        g_got, i_send = tie(g_got, i_send)
        g_send, g_keep = halve((g_keep, g_got), z // 2, 0)
        g_got = swap(g_send, "seq", 4)
        gfirst_got, g_send = tie(gfirst_got, g_send)
    by_rows = lambda n: pl.BlockSpec((tok // 4, n), lambda j: (j, 0))
    grad_input = kcall(
        input_grad_body, "input_grad", (x, norm1_gain, gfirst_a, gfirst_got, gres), [sds((tok, D), f32)], grid=(4,),
        in_specs=[by_rows(D), full((D,))] + [by_rows(D)] * 3, out_specs=[by_rows(D)],
    )[0]

    if whole:
        i_got, grad_input = tie(i_got, grad_input)
        width = 3 * GW
        low, high = jnp.where(ybit == 0, i_keep, i_got), jnp.where(ybit == 0, i_got, i_keep)
        vec = i_keep[..., width:] + i_got[..., width:]
        i_all = jnp.concatenate([low[..., :width], high[..., :width], vec], axis=-1).reshape(2, 2, IN_ROWS // 2, 2 * width + 128)
        i_send, i_keep = pick(i_all, 1 - z % 2, 1), pick(i_all, z % 2, 1)
        i_got = swap(i_send, "seq", 2)
        i_got, g_got = tie(i_got, g_got)
        i_send, i_keep = halve((i_keep, i_got), z // 2, 0)
        i_got = swap(i_send, "seq", 4)

        mine = g_keep + g_got
        near, far = spread(mine, xbit)
        g_down, g_up, g_out = kcall(
            unpack_mlp_body, "unpack_mlp", (bits, near, far),
            [sds((DOWN_ROWS, D), f32), sds((UP_ROWS, FF), f32), sds((UP_ROWS, D), f32)],
            grid=(1,), in_specs=[SMEM, full(near.shape), full(far.shape)],
            out_specs=[full((DOWN_ROWS, D)), full((UP_ROWS, FF)), full((UP_ROWS, D))],
        )
        near, far = spread(i_keep + i_got, xbit)
        far, g_down = tie(far, g_down)
        g_in, *vecs = kcall(
            unpack_in_body, "unpack_in", (bits, near, far),
            [sds((2 * IN_ROWS, 3 * D), f32)] + [sds((UNIT * n,), f32) for n in VEC_UNITS],
            in_specs=[SMEM, VMEM, VMEM], out_specs=[VMEM] * 9,
        )
    else:
        total = lambda v: lax.psum(lax.psum_scatter(v, "seq", scatter_dimension=0, tiled=True).astype(bf16), "rep").astype(f32)
        order = lambda bit, keep, send: jnp.where(bit == 0, jnp.stack([keep, send]), jnp.stack([send, keep])).astype(f32)
        by_x = jnp.stack([order(xbit, h[1], h[0]) for h in halves])
        by_y = jnp.stack([order(ybit, h[3], h[2]) for h in halves])
        ups = by_x[..., : 2 * UP_ROWS, :].reshape(2, 2, NBLK, 2, UP_ROWS, HALF)
        g_up = total(ups.transpose(2, 4, 0, 1, 3, 5).reshape(D, FF))
        g_out = total(by_x[..., 2 * UP_ROWS :, :].reshape(2, 2, NBLK, UP_ROWS // 2, HALF).transpose(2, 1, 3, 0, 4).reshape(D, D))
        g_down = total(by_y.transpose(2, 1, 0, 4, 3, 5).reshape(FF, D))
        both = jnp.stack([i_keep, i_send], axis=1)[..., : 3 * GW].astype(f32).reshape(D, 3, 1, GW)
        g_in = total(jnp.where((jnp.arange(2) == ybit)[None, None, :, None], both, 0.0).reshape(D, 3 * D))
        small = i_keep[:, :, 3 * GW : 3 * GW + UNIT].astype(f32)
        ends = np.cumsum((0,) + VEC_UNITS)
        vecs = [total(small[:, lo:hi].reshape(-1)) for lo, hi in zip(ends[:-1], ends[1:], strict=True)]
    n1_gain, n1_shift, b_in, b_down, n2_gain, n2_shift, b_out, b_up = vecs
    return (
        result[None], grad_input[None], n1_gain, n1_shift, g_in, b_in, g_out, b_out, n2_gain, n2_shift, g_up, b_up, g_down, b_down,
    )


def solution(mesh):
    tokens, weights = P("rep", "seq", None), P()
    in_specs = (tokens, P("rep", "seq")) + (weights,) * 12 + (tokens,)
    vec, mat = P("seq"), P("seq", None)
    out_specs = (tokens, tokens, vec, vec, mat, vec, mat, vec, vec, vec, mat, vec, mat, vec)
    return jax.shard_map(body, mesh=mesh, in_specs=in_specs, out_specs=out_specs, check_vma=False)
```
